128 devices in a mesh: gx: 32 (over y, z, core), gy: 4 (over x).
Axes of the slice: x: 4, y: 4, z: 4, core: 2. Of those that a mesh axis runs over, the one named last changes fastest.
Arguments:
- features: bfloat16 [32, 256, 32, 128], P(None, 'gx', 'gy'), may hold values from -6 to 6
- w_enc1: bfloat16 [27, 32, 32], replicated, may hold values from -0.21875 to 0.21875
- w_enc2: bfloat16 [27, 64, 32], replicated, may hold values from -0.21875 to 0.21875
- w_enc3: bfloat16 [27, 128, 64], replicated, may hold values from -0.15625 to 0.15625
- w_enc4: bfloat16 [27, 256, 128], replicated, may hold values from -0.21875 to 0.21875
- w_dec3: bfloat16 [27, 128, 256], replicated, may hold values from -0.15625 to 0.15625
- w_dec2: bfloat16 [27, 64, 128], replicated, may hold values from -0.21875 to 0.21875
- w_dec1: bfloat16 [27, 32, 64], replicated, may hold values from -0.3125 to 0.3125
Outputs:
- decoded: bfloat16 [32, 256, 32, 128], P(None, 'gx', 'gy')
The draws below stay inside these ranges and needn't reach their ends.
All inputs are finite; a program needn't handle non-finite values.
Results may differ from the reference program's by a relative error of at most 0.013.
Values may be sent and summed in bfloat16 or wider, within the bound.
A program may use at most 64 MiB of HBM per device.

```python
import jax
import jax.numpy as jnp
from jax import lax

C1 = 32
C2 = 64
C3 = 128
C4 = 256
W = 128
NX = 256
NY = 32


def block_scale(rng, shape, cuts, least, largest):
    level = 1.0
    for dim, shards_of in cuts:
        steps = jax.random.uniform(jax.random.fold_in(jax.random.fold_in(rng, 6), dim), (shards_of,), jnp.float32, least / len(cuts), largest / len(cuts))
        level = level * jnp.repeat(jnp.exp(steps), shape[dim] // shards_of).reshape((-1,) + (1,) * (len(shape) - 1 - dim))
    return level


def normal_values(stream_key, extent, scale, reach, split=(), kind=jnp.bfloat16):
    drawn = jax.random.normal(stream_key, extent, jnp.float32) * scale
    if len(split) > 0:
        drawn = block_scale(stream_key, extent, split, -0.22, 0.18) * drawn
    return jnp.clip(drawn, min=-reach, max=reach).astype(kind)


def setup_inputs(seed: int = 0) -> dict:
    seeds = jax.random.split(jax.random.key(seed), 9)
    features = normal_values(seeds[0], (C1, NX, NY, W), 1.0, 6.0, ((1, 32), (2, 4)))
    w_enc1 = normal_values(seeds[1], (27, C1, C1), (27 * C1) ** -0.5, 0.21875)
    w_enc2 = normal_values(seeds[2], (27, C2, C1), (27 * C1) ** -0.5, 0.21875)
    w_enc3 = normal_values(seeds[3], (27, C3, C2), (27 * C2) ** -0.5, 0.15625)
    w_enc4 = normal_values(seeds[4], (27, C4, C3), (27 * C3 // 4) ** -0.5, 0.21875)
    w_dec3 = normal_values(seeds[5], (27, C3, C4), (27 * C4 // 4) ** -0.5, 0.15625)
    w_dec2 = normal_values(seeds[6], (27, C2, C3), (27 * C3 // 4) ** -0.5, 0.21875)
    w_dec1 = normal_values(seeds[7], (27, C1, C2), (27 * C2 // 4) ** -0.5, 0.3125)
    return {"features": features, "w_enc1": w_enc1, "w_enc2": w_enc2, "w_enc3": w_enc3, "w_enc4": w_enc4, "w_dec3": w_dec3, "w_dec2": w_dec2, "w_dec1": w_dec1}


def conv(field, kernel):
    cout = kernel.shape[1]
    cin = kernel.shape[2]
    rhs = kernel.astype(jnp.float32).reshape(3, 3, 3, cout, cin).transpose(3, 4, 0, 1, 2)
    lhs = field.astype(jnp.float32)[None]
    out = lax.conv_general_dilated(lhs, rhs, (1, 1, 1), "SAME", dimension_numbers=("NCDHW", "OIDHW", "NCDHW"), precision=lax.Precision.HIGHEST)
    return out[0]


def pool(field):
    c, x, y, z = field.shape
    blocks = field.astype(jnp.float32).reshape(c, x // 2, 2, y // 2, 2, z // 2, 2)
    return jnp.mean(blocks, axis=(2, 4, 6)).astype(jnp.bfloat16)


def upsample(field):
    return jnp.repeat(jnp.repeat(jnp.repeat(field, 2, axis=1), 2, axis=2), 2, axis=3)


def reference(features, w_enc1, w_enc2, w_enc3, w_enc4, w_dec3, w_dec2, w_dec1):
    e1 = jax.nn.gelu(conv(features, w_enc1)).astype(jnp.bfloat16)
    e2 = jax.nn.gelu(conv(pool(e1), w_enc2)).astype(jnp.bfloat16)
    e3 = jax.nn.gelu(conv(pool(e2), w_enc3)).astype(jnp.bfloat16)
    e4 = jax.nn.gelu(conv(pool(e3), w_enc4)).astype(jnp.bfloat16)
    d3 = (jax.nn.gelu(conv(upsample(e4), w_dec3)) + e3.astype(jnp.float32)).astype(jnp.bfloat16)
    d2 = (jax.nn.gelu(conv(upsample(d3), w_dec2)) + e2.astype(jnp.float32)).astype(jnp.bfloat16)
    return (jax.nn.gelu(conv(upsample(d2), w_dec1)) + e1.astype(jnp.float32)).astype(jnp.bfloat16)
```

```python
import functools

import jax
import jax.numpy as jnp
from jax import lax
from jax.experimental import pallas as pl
from jax.experimental.pallas import tpu as pltpu
from jax.sharding import PartitionSpec as P

BF = jnp.bfloat16
F32 = jnp.float32
MESH = pl.DeviceIdType.MESH
DIRS = [(dx, dy) for dx in (-1, 0, 1) for dy in (-1, 0, 1) if (dx, dy) != (0, 0)]
TAPS = (((0,), (1, 2)), ((0, 1), (2,)))


def nn(a, b):
    return lax.dot_general(a, b, (((1,), (0,)), ((), ())), preferred_element_type=F32)


def nt(a, b):
    return lax.dot_general(a, b, (((1,), (1,)), ((), ())), preferred_element_type=F32)


def iota(shape, dim):
    return lax.broadcasted_iota(jnp.int32, shape, dim)


def ones_where(mask):
    return jnp.where(mask, 1.0, 0.0).astype(BF)


def gelu(x):
    return 0.5 * x * (1.0 + jnp.tanh(0.7978845608028654 * (x + 0.044715 * (x * x * x))))


def shifted(v, step, axis, period):
    n = v.shape[axis]
    place = iota(v.shape, axis) % period
    edge = 0 if step == 1 else period - 1
    return jnp.where(place == edge, 0.0, pltpu.roll(v, step % n, axis))


def cat(parts, axis):
    return parts[0] if len(parts) == 1 else jnp.concatenate(parts, axis=axis)


def side(d, n, width=1, pad=1):
    if d == 1:
        return (pad + (n - 1)) * width, 0, width
    if d == -1:
        return pad * width, (n + pad) * width, width
    return pad * width, pad * width, n * width


def kernel(
    feat, w1h, w2h, w3h, w4h, v3h, v2h, v1h, out,
    fv, w1, w2, w3, w4, v3, v2, v1, ov,
    fext, e1, pbs, p1, y1s, y1r, p2, y2s, y2r, p3, e2e, e3e,
    k1, k2, k3, g2, g1, pd3, d3e, d2e, q, dd,
    lsem, osem, s1, r1, s2, r2, s3, r3, s4, r4, se2, re2, se3, re3,
):
    gx, gy = lax.axis_index("gx"), lax.axis_index("gy")
    nx, ny = lax.axis_size("gx"), lax.axis_size("gy")

    loads = [
        pltpu.make_async_copy(src, dst, lsem.at[n])
        for n, (src, dst) in enumerate(
            [(feat, fv), (w1h, w1), (w2h, w2), (w3h, w3), (w4h, w4), (v3h, v3), (v2h, v2), (v1h, v1)]
        )
    ]
    for c in loads:
        c.start()

    def target(dx, dy):
        return (lax.rem(gx + dx + nx, nx), lax.rem(gy + dy + ny, ny))

    window = [(dx, dy) for dx in range(-2, 3) for dy in range(ny) if (dx, dy) != (0, 0)]
    barrier = pltpu.get_barrier_semaphore()
    for dx, dy in window:
        pl.semaphore_signal(barrier, inc=1, device_id=target(dx, dy), device_id_type=MESH)

    def send(n, dx, dy, src, dst, ss, rs):
        return pltpu.make_async_remote_copy(
            src_ref=src, dst_ref=dst, send_sem=ss.at[n], recv_sem=rs.at[n],
            device_id=target(dx, dy), device_id_type=MESH,
        )

    def start(copies):
        for c in copies:
            c.start()

    def arrive(copies):
        for c in copies:
            c.wait_recv()

    loads[0].wait()
    r, c = iota((256, 256), 0), iota((256, 256), 1)
    perm = ones_where((r // 32 == c % 8) & (r % 32 == c // 8))
    perm_t = ones_where((c // 32 == r % 8) & (c % 32 == r // 8))

    def place(x, carry):
        a = fv[:, pl.ds(2 * x, 1)].astype(F32).reshape(256, 128).astype(BF)
        b = fv[:, pl.ds(2 * x + 1, 1)].astype(F32).reshape(256, 128).astype(BF)
        t = nn(perm, cat([a, b], 1)).astype(BF)
        fext[2 * x + 1, pl.ds(32, 256), :] = t[:, :128]
        fext[2 * x + 2, pl.ds(32, 256), :] = t[:, 128:]
        return carry

    lax.fori_loop(0, 4, place, 0)
    for n in range(4):
        p3[:, n if n < 2 else n + 4] = jnp.zeros((5, 16, 128), BF)
    pl.semaphore_wait(barrier, len(window))

    x1 = []
    for n, (dx, dy) in enumerate(DIRS):
        sx, tx, cx = side(dx, 8)
        sy, ty, cy = side(dy, 8, 32)
        x1.append(
            send(n, dx, dy, fext.at[pl.ds(sx, cx), pl.ds(sy, cy)], fext.at[pl.ds(tx, cx), pl.ds(ty, cy)], s1, r1)
        )
    start(x1)

    loads[1].wait()
    z32 = jnp.zeros((32, 32), BF)
    for l in range(3):
        for yo in range(2):
            row = []
            for i in range(3):
                for yi in range(4):
                    j = yi - yo
                    row.append(w1[9 * i + 3 * j + l] if 0 <= j < 3 else z32)
            k1[pl.ds(64 * l + 32 * yo, 32), :] = cat(row, 1)
    loads[2].wait()
    z64 = jnp.zeros((64, 32), BF)
    for l in range(3):
        for yo in range(4):
            row = []
            for i in range(3):
                for yi in (0, 1, 2, 3, -1, 4, 9, 9):
                    j = yi - yo + 1
                    row.append(w2[9 * i + 3 * j + l] if 0 <= j < 3 else z64)
            k2[pl.ds(256 * l + 64 * yo, 64), :] = cat(row, 1)
    loads[3].wait()
    z128 = jnp.zeros((128, 64), BF)
    for l in range(3):
        for yo in range(2):
            row = []
            for i in range(3):
                for yi in (0, 1, -1, 2):
                    j = yi - yo + 1
                    row.append(w3[9 * i + 3 * j + l] if 0 <= j < 3 else z128)
            k3[pl.ds(256 * l + 128 * yo, 128), :] = cat(row, 1)

    arrive(x1)

    @pl.when(gx == 0)
    def _():
        fext[0] = jnp.zeros((320, 128), BF)

    @pl.when(gx == nx - 1)
    def _():
        fext[9] = jnp.zeros((320, 128), BF)

    @pl.when(gy == 0)
    def _():
        fext[:, pl.ds(0, 32)] = jnp.zeros((10, 32, 128), BF)

    @pl.when(gy == ny - 1)
    def _():
        fext[:, pl.ds(288, 32)] = jnp.zeros((10, 32, 128), BF)

    def enc1(x, carry):
        for b in range(4):
            rhs = cat(
                [
                    cat([fext[2 * x + i, pl.ds(64 * b, 128), :], fext[2 * x + 1 + i, pl.ds(64 * b, 128), :]], 1)
                    for i in range(3)
                ],
                0,
            )
            t = nn(k1[...], rhs)
            total = None
            for h in range(2):
                u = t[:, 128 * h : 128 * (h + 1)]
                v = u[64:128] + shifted(u[:64], 1, 1, 128) + shifted(u[128:], -1, 1, 128)
                v = gelu(v).astype(BF)
                e1[2 * x + h, pl.ds(64 * b, 64), :] = v
                f = v.astype(F32)
                f = f[:32] + f[32:]
                total = f if total is None else total + f
            total = total + pltpu.roll(total, 127, 1)
            pbs[x, pl.ds(32 * b, 32), :] = (total * 0.125).astype(BF)
        return carry

    lax.fori_loop(0, 4, enc1, 0)

    pick64 = ones_where(iota((64, 128), 1) == 2 * iota((64, 128), 0))
    for s, y in ((0, 0), (1, 96)):
        y1s[s] = nt(pick64, cat([pbs[x, pl.ds(y, 32), :] for x in range(4)], 0)).astype(BF)
    for x in range(4):
        p1[x + 1] = nt(pick64, pbs[x]).astype(BF)

    def halo(main, ys, yr, n_local, ss, rs):
        copies = []
        for n, (dx, dy) in enumerate(DIRS):
            if dy == 0:
                sx, tx, _ = side(dx, n_local)
                copies.append(send(n, dx, dy, main.at[sx], main.at[tx], ss, rs))
            else:
                s = 1 if dy == 1 else 0
                copies.append(send(n, dx, dy, ys.at[s], yr.at[1 - s, 1 - dx], ss, rs))
        return copies

    x2 = halo(p1, y1s, y1r, 4, s2, r2)
    start(x2)
    arrive(x2)

    def sides(yr, n_local, c):
        found = []
        for x in range(n_local + 2):
            slot, at = (0, n_local - 1) if x == 0 else (2, 0) if x == n_local + 1 else (1, x - 1)
            inside = (gx > 0) if x == 0 else (gx < nx - 1) if x == n_local + 1 else True
            lo = yr[0, slot][:, at * c : (at + 1) * c]
            hi = yr[1, slot][:, at * c : (at + 1) * c]
            zero = jnp.zeros_like(lo)
            lo = jnp.where(inside & (gy > 0), lo, zero)
            hi = jnp.where(inside & (gy < ny - 1), hi, zero)
            parts = [lo, hi]
            if c < 64:
                parts.append(jnp.zeros((lo.shape[0], 128 - 2 * c), BF))
            found.append(cat(parts, 1))
        return found

    def mains(main, n_local):
        found = []
        for x in range(n_local + 2):
            v = main[x]
            if x == 0:
                v = jnp.where(gx > 0, v, jnp.zeros_like(v))
            if x == n_local + 1:
                v = jnp.where(gx < nx - 1, v, jnp.zeros_like(v))
            found.append(v)
        return found

    m1, h1 = mains(p1, 4), sides(y1r, 4, 32)
    lhs = cat([cat([cat([m1[x + i], h1[x + i]], 1) for i in range(3)], 1) for x in range(4)], 0)
    t = nt(lhs, k2[...])
    e2 = gelu(t[:, 256:512] + shifted(t[:, :256], 1, 0, 64) + shifted(t[:, 512:], -1, 0, 64)).astype(BF)
    f = e2.astype(F32)
    low = iota((64, 128), 1) < 64
    pick32 = ones_where(iota((32, 64), 1) == 2 * iota((32, 64), 0))
    p2v = []
    for x in range(2):
        a = f[128 * x : 128 * x + 64] + f[128 * x + 64 : 128 * x + 128]
        a0, a1 = a[:, :128], a[:, 128:]
        a = jnp.where(low, a0 + pltpu.roll(a0, 64, 1), a1 + pltpu.roll(a1, 64, 1))
        a = (a + pltpu.roll(a, 63, 0)) * 0.125
        a = nn(pick32, a.astype(BF))
        p2v.append(a)
        p2[x + 1] = a.astype(BF)
    low32 = iota((32, 128), 1) < 64
    y2s[0] = jnp.where(low32, p2v[0], pltpu.roll(p2v[1], 64, 1)).astype(BF)
    y2s[1] = jnp.where(low32, pltpu.roll(p2v[0], 64, 1), p2v[1]).astype(BF)
    x3 = halo(p2, y2s, y2r, 2, s3, r3)
    start(x3)

    rr, cc = iota((64, 64), 0), iota((64, 64), 1)
    split = ones_where(cc == 2 * (rr % 32) + rr // 32)
    for x in range(4):
        a = nn(split, e2[64 * x : 64 * x + 64])
        for y in range(4):
            ev = a[:32, 128 * (y // 2) : 128 * (y // 2) + 128]
            od = a[32:, 128 * (y // 2) : 128 * (y // 2) + 128]
            if y % 2 == 0:
                cell = jnp.where(low32, ev, pltpu.roll(od, 64, 1))
            else:
                cell = jnp.where(low32, pltpu.roll(ev, 64, 1), od)
            e2e[x + 1, y + 1] = cell.astype(BF)

    def cells(ref, n_local, ss, rs):
        copies = []
        for n, (dx, dy) in enumerate(DIRS):
            sx, tx, cx = side(dx, n_local)
            sy, ty, cy = side(dy, n_local)
            copies.append(
                send(n, dx, dy, ref.at[pl.ds(sx, cx), pl.ds(sy, cy)], ref.at[pl.ds(tx, cx), pl.ds(ty, cy)], ss, rs)
            )
        return copies

    xe2 = cells(e2e, 4, se2, re2)
    start(xe2)
    arrive(x3)

    m2, h2 = mains(p2, 2), sides(y2r, 2, 64)
    lhs = cat([cat([cat([m2[x + i], h2[x + i]], 1) for i in range(3)], 1) for x in range(2)], 0)
    t = nt(lhs, k3[...])
    e3 = gelu(t[:, 256:512] + shifted(t[:, :256], 1, 0, 32) + shifted(t[:, 512:], -1, 0, 32)).astype(BF)
    f = e3.astype(F32)
    a = f[:32] + f[32:]
    a = a[:, :128] + a[:, 128:]
    a = (a + pltpu.roll(a, 31, 0)) * 0.125
    pick16 = ones_where(iota((16, 32), 1) == 2 * iota((16, 32), 0))
    p3[2, gy + 2] = nn(pick16, a.astype(BF)).astype(BF)
    x4 = []
    for n, (dx, dy) in enumerate(window):
        x4.append(send(n, dx, dy, p3.at[2, gy + 2], p3.at[2 - dx, gy + 2], s4, r4))
    start(x4)
    for x in range(2):
        for y in range(2):
            e3e[x + 1, y + 1] = e3[32 * x : 32 * x + 32, 128 * y : 128 * y + 128]
    xe3 = cells(e3e, 2, se3, re3)
    start(xe3)

    loads[6].wait()
    for px in range(2):
        for py in range(2):
            for tx in range(2):
                for ty in range(2):
                    s = []
                    for l in range(3):
                        terms = [
                            v2[9 * i + 3 * j + l].astype(F32) for i in TAPS[px][tx] for j in TAPS[py][ty]
                        ]
                        s.append(functools.reduce(jnp.add, terms))
                    block = cat([s[0], s[2], s[1] + s[2], s[0] + s[1]], 0).astype(BF)
                    g2[pl.ds(256 * (2 * px + py), 256), pl.ds(128 * (2 * tx + ty), 128)] = block
    loads[7].wait()
    for px in range(2):
        for py in range(2):
            for l in range(3):
                row = []
                for tx in range(2):
                    for ty in range(2):
                        terms = [
                            v1[9 * i + 3 * j + l].astype(F32) for i in TAPS[px][tx] for j in TAPS[py][ty]
                        ]
                        row.append(functools.reduce(jnp.add, terms).astype(BF))
                g1[pl.ds(96 * (2 * px + py) + 32 * l, 32), :] = cat(row, 1)

    loads[4].wait()
    for n, (dx, dy) in enumerate(window):
        pltpu.make_async_remote_copy(
            src_ref=p3.at[2, gy + 2], dst_ref=p3.at[2 - dx, lax.rem(gy - dy + ny, ny) + 2],
            send_sem=s4.at[n], recv_sem=r4.at[n], device_id=target(dx, dy), device_id_type=MESH,
        ).wait_recv()

    cell = []
    for x in range(5):
        inside = (gx + (x - 2) >= 0) & (gx + (x - 2) < nx)
        line = []
        for y in range(5):
            v = p3[x, gy + y]
            line.append(jnp.where(inside, v, jnp.zeros_like(v)))
        cell.append(line)
    lhs = cat(
        [
            cat([cell[x + i][y + j] for i in range(3) for j in range(3)], 1)
            for x in range(3)
            for y in range(3)
        ],
        0,
    )
    t = cat(
        [nt(lhs, cat([w4[9 * i + 3 * j + l] for i in range(3) for j in range(3)], 1)) for l in range(3)], 1
    )
    e4 = gelu(t[:, 256:512] + shifted(t[:, :256], 1, 0, 16) + shifted(t[:, 512:], -1, 0, 16))

    def inside(x, y, width, n_local):
        ok = True
        if x == 0:
            ok = gx > 0
        if x == n_local + 1:
            ok = gx < nx - 1
        if y == 0:
            ok = ok & (gy > 0)
        if y == n_local + 1:
            ok = ok & (gy < ny - 1)
        return ok

    def kept(v, ok):
        return v if ok is True else jnp.where(ok, v, jnp.zeros_like(v))

    e4 = [kept(e4[16 * n : 16 * n + 16], inside(n // 3, n % 3, 16, 1)).astype(BF) for n in range(9)]

    loads[5].wait()
    twice = ones_where(iota((32, 16), 1) == iota((32, 16), 0) // 2)
    up = nn(twice, cat(e4, 1)).astype(BF)
    at = ((0, 0, 1), (0, 1, 1), (1, 1, 2), (1, 2, 2))
    for x in range(4):
        for y in range(4):
            for i in range(3):
                for j in range(3):
                    n = 3 * at[x][i] + at[y][j]
                    pd3[pl.ds(128 * x + 32 * y, 32), pl.ds(256 * (3 * i + j), 256)] = up[:, 256 * n : 256 * n + 256]
    arrive(xe3)
    for x in range(4):
        t = None
        for i in range(3):
            for j in range(3):
                u = nt(
                    pd3[pl.ds(128 * x, 128), pl.ds(256 * (3 * i + j), 256)],
                    cat([v3[9 * i + 3 * j + l] for l in range(3)], 0),
                )
                t = u if t is None else t + u
        v = gelu(t[:, 128:256] + shifted(t[:, :128], 1, 0, 32) + shifted(t[:, 256:], -1, 0, 32))
        for y in range(4):
            w = v[32 * y : 32 * y + 32] + e3e[x, y].astype(F32)
            d3e[x, y] = kept(w, inside(x, y, 32, 2)).astype(BF)

    arrive(xe2)
    lane96 = iota((96, 128), 1) < 64
    for k in range(3):
        lhs = cat(
            [cat([d3e[k, m], d3e[k, m + 1], d3e[k + 1, m], d3e[k + 1, m + 1]], 1) for m in range(3)], 0
        )
        t = nt(lhs, g2[...])
        for px in range(2):
            for py in range(2):
                n = 256 * (2 * px + py)
                a, b = t[:, n : n + 128], t[:, n + 128 : n + 256]
                v = gelu(b + jnp.where(lane96, shifted(a, 1, 0, 32), shifted(a, -1, 0, 32)))
                for m in range(3):
                    x, y = 2 * k + 1 - px, 2 * m + 1 - py
                    w = v[32 * m : 32 * m + 32] + e2e[x, y].astype(F32)
                    d2e[x, y] = kept(w, inside(x, y, 32, 4))

    rr, cc = iota((128, 64), 0), iota((128, 64), 1)
    spread = ones_where((rr // 4 == cc % 32) & (rr // 2 % 2 == cc // 32))
    for x in range(6):
        line = []
        for m in range(5):
            a, b = d2e[x, m], d2e[x, m + 1]
            top = jnp.where(low32, a, pltpu.roll(b, 64, 1))
            bottom = jnp.where(low32, pltpu.roll(a, 64, 1), b)
            line.append(cat([top, bottom], 0).astype(BF))
        a = nn(spread, cat(line, 1)).astype(BF)
        for m in range(5):
            q[x, m] = a[:, 128 * m : 128 * m + 128]

    for k in range(5):
        for m in range(5):
            t = nt(g1[...], cat([q[k, m], q[k + 1, m]], 1))
            for px in range(2):
                for py in range(2):
                    a, b = k - px, m - py
                    if not (0 <= a < 4 and 0 <= b < 4):
                        continue
                    x, y = 2 * a + px, 2 * b + py
                    u = t[96 * (2 * px + py) : 96 * (2 * px + py) + 96]
                    v = gelu(u[32:64] + shifted(u[:32], 1, 1, 128) + shifted(u[64:], -1, 1, 128))
                    v = v + e1[x, pl.ds(32 * y, 32), :].astype(F32)
                    dd[x, pl.ds(32 * y, 32), :] = v.astype(BF)

    def back(x, carry):
        t = nn(perm_t, cat([dd[2 * x], dd[2 * x + 1]], 1))
        for h in range(2):
            u = t[:, 128 * h : 128 * h + 128].reshape(32, 1, 8, 128).astype(BF)
            ov[:, pl.ds(2 * x + h, 1)] = u
        return carry

    lax.fori_loop(0, 4, back, 0)
    done = pltpu.make_async_copy(ov, out, osem)
    done.start()
    for copies in (x1, x2, x3, x4, xe2, xe3):
        for c in copies:
            c.wait_send()
    done.wait()


def local(features, w_enc1, w_enc2, w_enc3, w_enc4, w_dec3, w_dec2, w_dec1):
    args = (features, w_enc1, w_enc2, w_enc3, w_enc4, w_dec3, w_dec2, w_dec1)
    ny = lax.axis_size("gy")
    far = 5 * ny - 1
    dma = pltpu.SemaphoreType.DMA
    scratch = [pltpu.VMEM(a.shape, BF) for a in args]
    scratch.append(pltpu.VMEM((32, 8, 8, 128), BF))
    for shape in (
        (10, 320, 128), (8, 256, 128), (4, 128, 128),
        (6, 64, 128), (2, 64, 128), (2, 3, 64, 128),
        (4, 32, 128), (2, 32, 128), (2, 3, 32, 128),
        (5, ny + 4, 16, 128), (6, 6, 32, 128), (4, 4, 32, 128),
        (192, 384), (768, 768), (768, 768), (1024, 512), (384, 256),
        (512, 2304), (4, 4, 32, 128),
    ):
        scratch.append(pltpu.VMEM(shape, BF))
    scratch.append(pltpu.VMEM((6, 6, 32, 128), F32))
    scratch.append(pltpu.VMEM((6, 5, 128, 128), BF))
    scratch.append(pltpu.VMEM((8, 256, 128), BF))
    scratch += [dma((8,)), dma]
    for n in (8, 8, 8, far, 8, 8):
        scratch += [dma((n,)), dma((n,))]
    return pl.pallas_call(
        kernel,
        out_shape=jax.ShapeDtypeStruct(features.shape, BF),
        in_specs=[pl.BlockSpec(memory_space=pl.ANY)] * 8,
        out_specs=pl.BlockSpec(memory_space=pl.ANY),
        scratch_shapes=scratch,
        compiler_params=pltpu.CompilerParams(
            collective_id=0, has_side_effects=True, vmem_limit_bytes=56 * 1024 * 1024
        ),
        cost_estimate=pl.CostEstimate(flops=2 * 1115000000, bytes_accessed=7000000, transcendentals=1000000),
    )(*args)


def solution(mesh):
    return jax.shard_map(
        local,
        mesh=mesh,
        in_specs=(P(None, "gx", "gy", None), P(), P(), P(), P(), P(), P(), P()),
        out_specs=P(None, "gx", "gy", None),
        check_vma=False,
    )
```

```python
import functools

import jax
import jax.numpy as jnp
from jax import lax
from jax.experimental import pallas as pl
from jax.experimental.pallas import tpu as pltpu
from jax.sharding import PartitionSpec as P

BF = jnp.bfloat16
F32 = jnp.float32
MESH = pl.DeviceIdType.MESH
DIRS = [(dx, dy) for dx in (-1, 0, 1) for dy in (-1, 0, 1) if (dx, dy) != (0, 0)]
TAPS = (((0,), (1, 2)), ((0, 1), (2,)))


def nn(a, b):
    return lax.dot_general(a, b, (((1,), (0,)), ((), ())), preferred_element_type=F32)


def nt(a, b):
    return lax.dot_general(a, b, (((1,), (1,)), ((), ())), preferred_element_type=F32)


def iota(shape, dim):
    return lax.broadcasted_iota(jnp.int32, shape, dim)


def ones_where(mask):
    return jnp.where(mask, 1.0, 0.0).astype(BF)


def gelu(x):
    return 0.5 * x * (1.0 + jnp.tanh(0.7978845608028654 * (x + 0.044715 * (x * x * x))))


def shifted(v, step, axis, period):
    n = v.shape[axis]
    place = iota(v.shape, axis) % period
    edge = 0 if step == 1 else period - 1
    return jnp.where(place == edge, 0.0, pltpu.roll(v, step % n, axis))


def cat(parts, axis):
    return parts[0] if len(parts) == 1 else jnp.concatenate(parts, axis=axis)


def side(d, n, width=1, pad=1):
    if d == 1:
        return (pad + (n - 1)) * width, 0, width
    if d == -1:
        return pad * width, (n + pad) * width, width
    return pad * width, pad * width, n * width


def kernel(
    feat, w1h, w2h, w3h, w4h, v3h, v2h, v1h, out,
    fv, w1, w2, w3, w4, v3, v2, v1, ov,
    fext, e1, pbs, p1, y1s, y1r, p2, y2s, y2r, p3, e2e, e3e,
    k1, k2, k3, g2, g1, pd3, d3e, d2e, q, dd,
    lsem, osem, s1, r1, s2, r2, s3, r3, s4, r4, se2, re2, se3, re3,
):
    gx, gy = lax.axis_index("gx"), lax.axis_index("gy")
    nx, ny = lax.axis_size("gx"), lax.axis_size("gy")

    loads = [
        pltpu.make_async_copy(src, dst, lsem.at[n])
        for n, (src, dst) in enumerate(
            [(feat, fv), (w1h, w1), (w2h, w2), (w3h, w3), (w4h, w4), (v3h, v3), (v2h, v2), (v1h, v1)]
        )
    ]
    for c in loads:
        c.start()

    def target(dx, dy):
        return (lax.rem(gx + dx + nx, nx), lax.rem(gy + dy + ny, ny))

    window = [(dx, dy) for dx in range(-2, 3) for dy in range(ny) if (dx, dy) != (0, 0)]
    barrier = pltpu.get_barrier_semaphore()
    for dx, dy in window:
        pl.semaphore_signal(barrier, inc=1, device_id=target(dx, dy), device_id_type=MESH)

    def send(n, dx, dy, src, dst, ss, rs):
        return pltpu.make_async_remote_copy(
            src_ref=src, dst_ref=dst, send_sem=ss.at[n], recv_sem=rs.at[n],
            device_id=target(dx, dy), device_id_type=MESH,
        )

    def start(copies):
        for c in copies:
            c.start()

    def arrive(copies):
        for c in copies:
            c.wait_recv()

    loads[0].wait()
    r, c = iota((256, 256), 0), iota((256, 256), 1)
    perm = ones_where((r // 32 == c % 8) & (r % 32 == c // 8))
    perm_t = ones_where((c // 32 == r % 8) & (c % 32 == r // 8))

    def place(x, carry):
        a = fv[:, pl.ds(2 * x, 1)].astype(F32).reshape(256, 128).astype(BF)
        b = fv[:, pl.ds(2 * x + 1, 1)].astype(F32).reshape(256, 128).astype(BF)
        t = nn(perm, cat([a, b], 1)).astype(BF)
        fext[2 * x + 1, pl.ds(32, 256), :] = t[:, :128]
        fext[2 * x + 2, pl.ds(32, 256), :] = t[:, 128:]
        return carry

    lax.fori_loop(0, 4, place, 0)
    for n in range(4):
        p3[:, n if n < 2 else n + 4] = jnp.zeros((5, 16, 128), BF)
    pl.semaphore_wait(barrier, len(window))

    x1 = []
    for n, (dx, dy) in enumerate(DIRS):
        sx, tx, cx = side(dx, 8)
        sy, ty, cy = side(dy, 8, 32)
        x1.append(
            send(n, dx, dy, fext.at[pl.ds(sx, cx), pl.ds(sy, cy)], fext.at[pl.ds(tx, cx), pl.ds(ty, cy)], s1, r1)
        )
    start(x1)

    loads[1].wait()
    z32 = jnp.zeros((32, 32), BF)
    for l in range(3):
        for yo in range(2):
            row = []
            for i in range(3):
                for yi in range(4):
                    j = yi - yo
                    row.append(w1[9 * i + 3 * j + l] if 0 <= j < 3 else z32)
            k1[pl.ds(64 * l + 32 * yo, 32), :] = cat(row, 1)
    loads[2].wait()
    z64 = jnp.zeros((32, 64), BF)
    for i in range(3):
        for n, yi in enumerate((0, 1, 2, 3, -1, 4, 9, 9)):
            row = []
            for l in range(3):
                for yo in range(4):
                    j = yi - yo + 1
                    row.append(w2[9 * i + 3 * j + l] if 0 <= j < 3 else z64)
            k2[pl.ds(256 * i + 32 * n, 32), :] = cat(row, 1)
    loads[3].wait()
    z128 = jnp.zeros((64, 128), BF)
    for i in range(3):
        for n, yi in enumerate((0, 1, -1, 2)):
            for l in range(3):
                for yo in range(2):
                    j = yi - yo + 1
                    k3[pl.ds(256 * i + 64 * n, 64), pl.ds(256 * l + 128 * yo, 128)] = (
                        w3[9 * i + 3 * j + l] if 0 <= j < 3 else z128
                    )

    arrive(x1)

    @pl.when(gx == 0)
    def _():
        fext[0] = jnp.zeros((320, 128), BF)

    @pl.when(gx == nx - 1)
    def _():
        fext[9] = jnp.zeros((320, 128), BF)

    @pl.when(gy == 0)
    def _():
        fext[:, pl.ds(0, 32)] = jnp.zeros((10, 32, 128), BF)

    @pl.when(gy == ny - 1)
    def _():
        fext[:, pl.ds(288, 32)] = jnp.zeros((10, 32, 128), BF)

    def enc1(x, carry):
        for b in range(4):
            rhs = cat(
                [
                    cat([fext[2 * x + i, pl.ds(64 * b, 128), :], fext[2 * x + 1 + i, pl.ds(64 * b, 128), :]], 1)
                    for i in range(3)
                ],
                0,
            )
            t = nn(k1[...], rhs)
            total = None
            for h in range(2):
                u = t[:, 128 * h : 128 * (h + 1)]
                v = u[64:128] + shifted(u[:64], 1, 1, 128) + shifted(u[128:], -1, 1, 128)
                v = gelu(v).astype(BF)
                e1[2 * x + h, pl.ds(64 * b, 64), :] = v
                f = v.astype(F32)
                f = f[:32] + f[32:]
                total = f if total is None else total + f
            total = total + pltpu.roll(total, 127, 1)
            pbs[x, pl.ds(32 * b, 32), :] = (total * 0.125).astype(BF)
        return carry

    lax.fori_loop(0, 4, enc1, 0)

    pick64 = ones_where(iota((64, 128), 1) == 2 * iota((64, 128), 0))
    for s, y in ((0, 0), (1, 96)):
        y1s[s] = nt(pick64, cat([pbs[x, pl.ds(y, 32), :] for x in range(4)], 0)).astype(BF)
    for x in range(4):
        p1[x + 1] = nt(pick64, pbs[x]).astype(BF)

    def halo(main, ys, yr, n_local, ss, rs):
        copies = []
        for n, (dx, dy) in enumerate(DIRS):
            if dy == 0:
                sx, tx, _ = side(dx, n_local)
                copies.append(send(n, dx, dy, main.at[sx], main.at[tx], ss, rs))
            else:
                s = 1 if dy == 1 else 0
                copies.append(send(n, dx, dy, ys.at[s], yr.at[1 - s, 1 - dx], ss, rs))
        return copies

    x2 = halo(p1, y1s, y1r, 4, s2, r2)
    start(x2)
    arrive(x2)

    def sides(yr, n_local, c):
        found = []
        for x in range(n_local + 2):
            slot, at = (0, n_local - 1) if x == 0 else (2, 0) if x == n_local + 1 else (1, x - 1)
            inside = (gx > 0) if x == 0 else (gx < nx - 1) if x == n_local + 1 else True
            lo = yr[0, slot][:, at * c : (at + 1) * c]
            hi = yr[1, slot][:, at * c : (at + 1) * c]
            zero = jnp.zeros_like(lo)
            lo = jnp.where(inside & (gy > 0), lo, zero)
            hi = jnp.where(inside & (gy < ny - 1), hi, zero)
            parts = [lo, hi]
            if c < 64:
                parts.append(jnp.zeros((lo.shape[0], 128 - 2 * c), BF))
            found.append(cat(parts, 1))
        return found

    def mains(main, n_local):
        found = []
        for x in range(n_local + 2):
            v = main[x]
            if x == 0:
                v = jnp.where(gx > 0, v, jnp.zeros_like(v))
            if x == n_local + 1:
                v = jnp.where(gx < nx - 1, v, jnp.zeros_like(v))
            found.append(v)
        return found

    m1, h1 = mains(p1, 4), sides(y1r, 4, 32)
    lhs = cat([cat([cat([m1[x + i], h1[x + i]], 1) for i in range(3)], 1) for x in range(4)], 0)
    t = nn(lhs, k2[...])
    e2 = gelu(t[:, 256:512] + shifted(t[:, :256], 1, 0, 64) + shifted(t[:, 512:], -1, 0, 64)).astype(BF)
    f = e2.astype(F32)
    low = iota((64, 128), 1) < 64
    pick32 = ones_where(iota((32, 64), 1) == 2 * iota((32, 64), 0))
    p2v = []
    for x in range(2):
        a = f[128 * x : 128 * x + 64] + f[128 * x + 64 : 128 * x + 128]
        a0, a1 = a[:, :128], a[:, 128:]
        a = jnp.where(low, a0 + pltpu.roll(a0, 64, 1), a1 + pltpu.roll(a1, 64, 1))
        a = (a + pltpu.roll(a, 63, 0)) * 0.125
        a = nn(pick32, a.astype(BF))
        p2v.append(a)
        p2[x + 1] = a.astype(BF)
    low32 = iota((32, 128), 1) < 64
    y2s[0] = jnp.where(low32, p2v[0], pltpu.roll(p2v[1], 64, 1)).astype(BF)
    y2s[1] = jnp.where(low32, pltpu.roll(p2v[0], 64, 1), p2v[1]).astype(BF)
    x3 = halo(p2, y2s, y2r, 2, s3, r3)
    start(x3)

    rr, cc = iota((64, 64), 0), iota((64, 64), 1)
    split = ones_where(cc == 2 * (rr % 32) + rr // 32)
    for x in range(4):
        a = nn(split, e2[64 * x : 64 * x + 64])
        for y in range(4):
            ev = a[:32, 128 * (y // 2) : 128 * (y // 2) + 128]
            od = a[32:, 128 * (y // 2) : 128 * (y // 2) + 128]
            if y % 2 == 0:
                cell = jnp.where(low32, ev, pltpu.roll(od, 64, 1))
            else:
                cell = jnp.where(low32, pltpu.roll(ev, 64, 1), od)
            e2e[x + 1, y + 1] = cell.astype(BF)

    def cells(ref, n_local, ss, rs):
        copies = []
        for n, (dx, dy) in enumerate(DIRS):
            sx, tx, cx = side(dx, n_local)
            sy, ty, cy = side(dy, n_local)
            copies.append(
                send(n, dx, dy, ref.at[pl.ds(sx, cx), pl.ds(sy, cy)], ref.at[pl.ds(tx, cx), pl.ds(ty, cy)], ss, rs)
            )
        return copies

    xe2 = cells(e2e, 4, se2, re2)
    start(xe2)
    arrive(x3)

    m2, h2 = mains(p2, 2), sides(y2r, 2, 64)
    lhs = cat([cat([cat([m2[x + i], h2[x + i]], 1) for i in range(3)], 1) for x in range(2)], 0)
    t = nn(lhs, k3[...])
    e3 = gelu(t[:, 256:512] + shifted(t[:, :256], 1, 0, 32) + shifted(t[:, 512:], -1, 0, 32)).astype(BF)
    f = e3.astype(F32)
    a = f[:32] + f[32:]
    a = a[:, :128] + a[:, 128:]
    a = (a + pltpu.roll(a, 31, 0)) * 0.125
    pick16 = ones_where(iota((16, 32), 1) == 2 * iota((16, 32), 0))
    p3[2, gy + 2] = nn(pick16, a.astype(BF)).astype(BF)
    x4 = []
    for n, (dx, dy) in enumerate(window):
        x4.append(send(n, dx, dy, p3.at[2, gy + 2], p3.at[2 - dx, gy + 2], s4, r4))
    start(x4)
    for x in range(2):
        for y in range(2):
            e3e[x + 1, y + 1] = e3[32 * x : 32 * x + 32, 128 * y : 128 * y + 128]
    xe3 = cells(e3e, 2, se3, re3)
    start(xe3)

    loads[6].wait()
    for px in range(2):
        for py in range(2):
            for tx in range(2):
                for ty in range(2):
                    s = []
                    for l in range(3):
                        terms = [
                            v2[9 * i + 3 * j + l].astype(F32) for i in TAPS[px][tx] for j in TAPS[py][ty]
                        ]
                        s.append(functools.reduce(jnp.add, terms))
                    block = cat([s[0], s[2], s[1] + s[2], s[0] + s[1]], 0).astype(BF)
                    g2[pl.ds(256 * (2 * px + py), 256), pl.ds(128 * (2 * tx + ty), 128)] = block
    loads[7].wait()
    for px in range(2):
        for py in range(2):
            for l in range(3):
                row = []
                for tx in range(2):
                    for ty in range(2):
                        terms = [
                            v1[9 * i + 3 * j + l].astype(F32) for i in TAPS[px][tx] for j in TAPS[py][ty]
                        ]
                        row.append(functools.reduce(jnp.add, terms).astype(BF))
                g1[pl.ds(96 * (2 * px + py) + 32 * l, 32), :] = cat(row, 1)

    loads[4].wait()
    for n, (dx, dy) in enumerate(window):
        pltpu.make_async_remote_copy(
            src_ref=p3.at[2, gy + 2], dst_ref=p3.at[2 - dx, lax.rem(gy - dy + ny, ny) + 2],
            send_sem=s4.at[n], recv_sem=r4.at[n], device_id=target(dx, dy), device_id_type=MESH,
        ).wait_recv()

    cell = []
    for x in range(5):
        inside = (gx + (x - 2) >= 0) & (gx + (x - 2) < nx)
        line = []
        for y in range(5):
            v = p3[x, gy + y]
            line.append(jnp.where(inside, v, jnp.zeros_like(v)))
        cell.append(line)
    lhs = cat(
        [
            cat([cell[x + i][y + j] for i in range(3) for j in range(3)], 1)
            for x in range(3)
            for y in range(3)
        ],
        0,
    )
    t = cat(
        [nt(lhs, cat([w4[9 * i + 3 * j + l] for i in range(3) for j in range(3)], 1)) for l in range(3)], 1
    )
    e4 = gelu(t[:, 256:512] + shifted(t[:, :256], 1, 0, 16) + shifted(t[:, 512:], -1, 0, 16))

    def inside(x, y, width, n_local):
        ok = True
        if x == 0:
            ok = gx > 0
        if x == n_local + 1:
            ok = gx < nx - 1
        if y == 0:
            ok = ok & (gy > 0)
        if y == n_local + 1:
            ok = ok & (gy < ny - 1)
        return ok

    def kept(v, ok):
        return v if ok is True else jnp.where(ok, v, jnp.zeros_like(v))

    e4 = [kept(e4[16 * n : 16 * n + 16], inside(n // 3, n % 3, 16, 1)).astype(BF) for n in range(9)]

    loads[5].wait()
    twice = ones_where(iota((32, 16), 1) == iota((32, 16), 0) // 2)
    up = nn(twice, cat(e4, 1)).astype(BF)
    at = ((0, 0, 1), (0, 1, 1), (1, 1, 2), (1, 2, 2))
    for x in range(4):
        for y in range(4):
            for i in range(3):
                for j in range(3):
                    n = 3 * at[x][i] + at[y][j]
                    pd3[pl.ds(128 * x + 32 * y, 32), pl.ds(256 * (3 * i + j), 256)] = up[:, 256 * n : 256 * n + 256]
    arrive(xe3)
    for x in range(4):
        t = None
        for i in range(3):
            for j in range(3):
                u = nt(
                    pd3[pl.ds(128 * x, 128), pl.ds(256 * (3 * i + j), 256)],
                    cat([v3[9 * i + 3 * j + l] for l in range(3)], 0),
                )
                t = u if t is None else t + u
        v = gelu(t[:, 128:256] + shifted(t[:, :128], 1, 0, 32) + shifted(t[:, 256:], -1, 0, 32))
        for y in range(4):
            w = v[32 * y : 32 * y + 32] + e3e[x, y].astype(F32)
            d3e[x, y] = kept(w, inside(x, y, 32, 2)).astype(BF)

    arrive(xe2)
    lane96 = iota((96, 128), 1) < 64
    for k in range(3):
        lhs = cat(
            [cat([d3e[k, m], d3e[k, m + 1], d3e[k + 1, m], d3e[k + 1, m + 1]], 1) for m in range(3)], 0
        )
        t = nt(lhs, g2[...])
        for px in range(2):
            for py in range(2):
                n = 256 * (2 * px + py)
                a, b = t[:, n : n + 128], t[:, n + 128 : n + 256]
                v = gelu(b + jnp.where(lane96, shifted(a, 1, 0, 32), shifted(a, -1, 0, 32)))
                for m in range(3):
                    x, y = 2 * k + 1 - px, 2 * m + 1 - py
                    w = v[32 * m : 32 * m + 32] + e2e[x, y].astype(F32)
                    d2e[x, y] = kept(w, inside(x, y, 32, 4))

    rr, cc = iota((128, 64), 0), iota((128, 64), 1)
    spread = ones_where((rr // 4 == cc % 32) & (rr // 2 % 2 == cc // 32))
    for x in range(6):
        line = []
        for m in range(5):
            a, b = d2e[x, m], d2e[x, m + 1]
            top = jnp.where(low32, a, pltpu.roll(b, 64, 1))
            bottom = jnp.where(low32, pltpu.roll(a, 64, 1), b)
            line.append(cat([top, bottom], 0).astype(BF))
        a = nn(spread, cat(line, 1)).astype(BF)
        for m in range(5):
            q[x, m] = a[:, 128 * m : 128 * m + 128]

    for k in range(5):
        for m in range(5):
            t = nt(g1[...], cat([q[k, m], q[k + 1, m]], 1))
            for px in range(2):
                for py in range(2):
                    a, b = k - px, m - py
                    if not (0 <= a < 4 and 0 <= b < 4):
                        continue
                    x, y = 2 * a + px, 2 * b + py
                    u = t[96 * (2 * px + py) : 96 * (2 * px + py) + 96]
                    v = gelu(u[32:64] + shifted(u[:32], 1, 1, 128) + shifted(u[64:], -1, 1, 128))
                    v = v + e1[x, pl.ds(32 * y, 32), :].astype(F32)
                    dd[x, pl.ds(32 * y, 32), :] = v.astype(BF)

    def back(x, carry):
        t = nn(perm_t, cat([dd[2 * x], dd[2 * x + 1]], 1))
        for h in range(2):
            u = t[:, 128 * h : 128 * h + 128].reshape(32, 1, 8, 128).astype(BF)
            ov[:, pl.ds(2 * x + h, 1)] = u
        return carry

    lax.fori_loop(0, 4, back, 0)
    done = pltpu.make_async_copy(ov, out, osem)
    done.start()
    for copies in (x1, x2, x3, x4, xe2, xe3):
        for c in copies:
            c.wait_send()
    done.wait()


def local(features, w_enc1, w_enc2, w_enc3, w_enc4, w_dec3, w_dec2, w_dec1):
    w_enc2, w_enc3 = jnp.swapaxes(w_enc2, 1, 2), jnp.swapaxes(w_enc3, 1, 2)
    args = (features, w_enc1, w_enc2, w_enc3, w_enc4, w_dec3, w_dec2, w_dec1)
    ny = lax.axis_size("gy")
    far = 5 * ny - 1
    dma = pltpu.SemaphoreType.DMA
    scratch = [pltpu.VMEM(a.shape, BF) for a in args]
    scratch.append(pltpu.VMEM((32, 8, 8, 128), BF))
    for shape in (
        (10, 320, 128), (8, 256, 128), (4, 128, 128),
        (6, 64, 128), (2, 64, 128), (2, 3, 64, 128),
        (4, 32, 128), (2, 32, 128), (2, 3, 32, 128),
        (5, ny + 4, 16, 128), (6, 6, 32, 128), (4, 4, 32, 128),
        (192, 384), (768, 768), (768, 768), (1024, 512), (384, 256),
        (512, 2304), (4, 4, 32, 128),
    ):
        scratch.append(pltpu.VMEM(shape, BF))
    scratch.append(pltpu.VMEM((6, 6, 32, 128), F32))
    scratch.append(pltpu.VMEM((6, 5, 128, 128), BF))
    scratch.append(pltpu.VMEM((8, 256, 128), BF))
    scratch += [dma((8,)), dma]
    for n in (8, 8, 8, far, 8, 8):
        scratch += [dma((n,)), dma((n,))]
    return pl.pallas_call(
        kernel,
        out_shape=jax.ShapeDtypeStruct(features.shape, BF),
        in_specs=[pl.BlockSpec(memory_space=pl.ANY)] * 8,
        out_specs=pl.BlockSpec(memory_space=pl.ANY),
        scratch_shapes=scratch,
        compiler_params=pltpu.CompilerParams(
            collective_id=0, has_side_effects=True, vmem_limit_bytes=56 * 1024 * 1024
        ),
        cost_estimate=pl.CostEstimate(flops=2 * 1115000000, bytes_accessed=7000000, transcendentals=1000000),
    )(*args)


def solution(mesh):
    return jax.shard_map(
        local,
        mesh=mesh,
        in_specs=(P(None, "gx", "gy", None), P(), P(), P(), P(), P(), P(), P()),
        out_specs=P(None, "gx", "gy", None),
        check_vma=False,
    )
```

```python
import functools

import jax
import jax.numpy as jnp
from jax import lax
from jax.experimental import pallas as pl
from jax.experimental.pallas import tpu as pltpu
from jax.sharding import PartitionSpec as P

BF = jnp.bfloat16
F32 = jnp.float32
MESH = pl.DeviceIdType.MESH
DIRS = [(-1, -1), (-1, 1), (1, -1), (1, 1), (-1, 0), (1, 0), (0, -1), (0, 1)]
TAPS = (((0,), (1, 2)), ((0, 1), (2,)))


def nn(a, b):
    return lax.dot_general(a, b, (((1,), (0,)), ((), ())), preferred_element_type=F32)


def nt(a, b):
    return lax.dot_general(a, b, (((1,), (1,)), ((), ())), preferred_element_type=F32)


def iota(shape, dim):
    return lax.broadcasted_iota(jnp.int32, shape, dim)


def ones_where(mask):
    return jnp.where(mask, 1.0, 0.0).astype(BF)


def gelu(x):
    return 0.5 * x * (1.0 + jnp.tanh(0.7978845608028654 * (x + 0.044715 * (x * x * x))))


def shifted(v, step, axis, period):
    n = v.shape[axis]
    place = iota(v.shape, axis) % period
    edge = 0 if step == 1 else period - 1
    return jnp.where(place == edge, 0.0, pltpu.roll(v, step % n, axis))


def cat(parts, axis):
    return parts[0] if len(parts) == 1 else jnp.concatenate(parts, axis=axis)


def side(d, n, width=1, pad=1):
    if d == 1:
        return (pad + (n - 1)) * width, 0, width
    if d == -1:
        return pad * width, (n + pad) * width, width
    return pad * width, pad * width, n * width


def kernel(
    feat, w1h, w2h, w3h, w4h, v3h, v2h, v1h, out,
    fv, w1, w2, w3, v2, v1,
    fext, e1, p1, y1s, y1r, p2, y2s, y2r, p3, e2e, e3e,
    k1, k2, k3, k4, kd3, g2, g1, pd3, d3e, d2e, q, dd,
    lsem, osem, s1, r1, s2, r2, s3, r3, s4, r4, se2, re2, se3, re3,
):
    gx, gy = lax.axis_index("gx"), lax.axis_index("gy")
    nx, ny = lax.axis_size("gx"), lax.axis_size("gy")

    loads = []

    def load(src, dst):
        c = pltpu.make_async_copy(src, dst, lsem.at[len(loads)])
        c.start()
        loads.append(c)
        return c

    def target(dx, dy):
        return (lax.rem(gx + dx + nx, nx), lax.rem(gy + dy + ny, ny))

    barrier = pltpu.get_barrier_semaphore()
    got_feat = load(feat, fv)
    for dx, dy in DIRS:
        pl.semaphore_signal(barrier, inc=1, device_id=target(dx, dy), device_id_type=MESH)
    got_w1, got_w2, got_w3 = load(w1h, w1), load(w2h, w2), load(w3h, w3)
    got_v2, got_v1 = load(v2h, v2), load(v1h, v1)
    got_w4 = [load(w4h.at[n], k4.at[:, pl.ds(128 * n, 128)]) for n in range(9)]
    got_v3 = [load(v3h.at[n], kd3.at[:, pl.ds(256 * n, 256)]) for n in range(9)]

    def far(d):
        return abs(d[0]) + min(d[1], ny - d[1])

    window = [(dx, dy) for dx in range(-2, 3) for dy in range(ny) if (dx, dy) != (0, 0)]
    window.sort(key=far, reverse=True)

    def send(n, dx, dy, src, dst, ss, rs):
        return pltpu.make_async_remote_copy(
            src_ref=src, dst_ref=dst, send_sem=ss.at[n], recv_sem=rs.at[n],
            device_id=target(dx, dy), device_id_type=MESH,
        )

    def start(copies):
        for c in copies:
            c.start()

    def arrive(copies):
        for c in copies:
            c.wait_recv()

    got_feat.wait()
    r, c = iota((256, 256), 0), iota((256, 256), 1)
    perm = ones_where((r // 32 == c % 8) & (r % 32 == c // 8))

    def place(x, carry):
        a = fv[:, pl.ds(2 * x, 1)].astype(F32).reshape(256, 128).astype(BF)
        b = fv[:, pl.ds(2 * x + 1, 1)].astype(F32).reshape(256, 128).astype(BF)
        t = nn(perm, cat([a, b], 1)).astype(BF)
        fext[2 * x + 1, pl.ds(32, 256), :] = t[:, :128]
        fext[2 * x + 2, pl.ds(32, 256), :] = t[:, 128:]
        return carry

    lax.fori_loop(0, 4, place, 0)
    for n in range(4):
        p3[:, n if n < 2 else n + 4] = jnp.zeros((5, 16, 128), BF)
    pl.semaphore_wait(barrier, len(DIRS))

    x1 = []
    for n, (dx, dy) in enumerate(DIRS):
        sx, tx, cx = side(dx, 8)
        sy, ty, cy = side(dy, 8, 32)
        x1.append(
            send(n, dx, dy, fext.at[pl.ds(sx, cx), pl.ds(sy, cy)], fext.at[pl.ds(tx, cx), pl.ds(ty, cy)], s1, r1)
        )
    start(x1)

    got_w1.wait()
    t = None
    r, c = iota((32, 256), 0), iota((32, 256), 1)
    for j in range(3):
        taps = cat([w1[pl.ds(9 * i + 3 * j, 3)].reshape(96, 32) for i in range(3)], 0)
        u = nn(taps, ones_where((r == c % 32) & (c // 32 % 4 == c // 128 + j)))
        t = u if t is None else t + u
    t = t.astype(BF)
    for i in range(3):
        for l in range(3):
            for yo in range(2):
                k1[pl.ds(64 * l + 32 * yo, 32), pl.ds(128 * i, 128)] = t[
                    96 * i + 32 * l : 96 * i + 32 * l + 32, 128 * yo : 128 * yo + 128
                ]

    def enc1(xa, xb, b):
        rhs = cat(
            [cat([fext[xa + i, pl.ds(64 * b, 128), :], fext[xb + i, pl.ds(64 * b, 128), :]], 1) for i in range(3)],
            0,
        )
        t = nn(k1[...], rhs)
        for h, x in enumerate((xa, xb)):
            u = t[:, 128 * h : 128 * (h + 1)]
            v = u[64:128] + shifted(u[:64], 1, 1, 128) + shifted(u[128:], -1, 1, 128)
            e1[x, pl.ds(64 * b, 64), :] = gelu(v).astype(BF)

    def enc1_inner(n, carry, blocks):
        for b in blocks:
            enc1(2 * n + 1, 2 * n + 2, b)
        return carry

    lax.fori_loop(0, 3, functools.partial(enc1_inner, blocks=(1, 2)), 0)

    got_w2.wait()
    r, c = iota((64, 256), 0), iota((64, 256), 1)
    spots = [ones_where(c == r + 64 * yo) for yo in range(4)]
    taps = [cat([w2[pl.ds(9 * i + 3 * j, 3)].reshape(96, 64) for i in range(3)], 0) for j in range(3)]
    for n, yi in enumerate((0, 1, 2, 3, -1, 4)):
        t = None
        for j in range(3):
            if 0 <= yi + 1 - j < 4:
                u = nn(taps[j], spots[yi + 1 - j])
                t = u if t is None else t + u
        t = t.astype(BF)
        for i in range(3):
            for l in range(3):
                k2[pl.ds(256 * i + 32 * n, 32), pl.ds(256 * l, 256)] = t[96 * i + 32 * l : 96 * i + 32 * l + 32]
    for i in range(3):
        k2[pl.ds(256 * i + 192, 64), :] = jnp.zeros((64, 768), BF)
    got_w3.wait()
    z128 = jnp.zeros((64, 128), BF)
    for i in range(3):
        for n, yi in enumerate((0, 1, -1, 2)):
            for l in range(3):
                for yo in range(2):
                    j = yi - yo + 1
                    k3[pl.ds(256 * i + 64 * n, 64), pl.ds(256 * l + 128 * yo, 128)] = (
                        w3[9 * i + 3 * j + l] if 0 <= j < 3 else z128
                    )

    arrive(x1[6:])

    @pl.when(gy == 0)
    def _():
        fext[pl.ds(1, 8), pl.ds(0, 32)] = jnp.zeros((8, 32, 128), BF)

    @pl.when(gy == ny - 1)
    def _():
        fext[pl.ds(1, 8), pl.ds(288, 32)] = jnp.zeros((8, 32, 128), BF)

    lax.fori_loop(0, 3, functools.partial(enc1_inner, blocks=(0, 3)), 0)

    def pool1(x):
        a = e1[2 * x].astype(F32) + e1[2 * x + 1].astype(F32)
        a = cat([a[64 * b : 64 * b + 32] + a[64 * b + 32 : 64 * b + 64] for b in range(4)], 0)
        a = (a + pltpu.roll(a, 127, 1)) * 0.125
        return a.astype(BF)

    pick64 = ones_where(iota((64, 128), 1) == 2 * iota((64, 128), 0))
    pooled = [None, pool1(1), pool1(2), None]
    arrive(x1[:6])

    @pl.when(gx == 0)
    def _():
        fext[0] = jnp.zeros((320, 128), BF)

    @pl.when(gx == nx - 1)
    def _():
        fext[9] = jnp.zeros((320, 128), BF)

    @pl.when(gy == 0)
    def _():
        for x in (0, 9):
            fext[x, pl.ds(0, 32)] = jnp.zeros((32, 128), BF)

    @pl.when(gy == ny - 1)
    def _():
        for x in (0, 9):
            fext[x, pl.ds(288, 32)] = jnp.zeros((32, 128), BF)

    for b in range(4):
        enc1(0, 7, b)
    pooled[0], pooled[3] = pool1(0), pool1(3)

    for s, y in ((0, 0), (1, 96)):
        y1s[s] = nt(pick64, cat([p[y : y + 32] for p in pooled], 0)).astype(BF)
    for x in range(4):
        p1[x + 1] = nt(pick64, pooled[x]).astype(BF)

    def halo(main, ys, yr, n_local, ss, rs):
        copies = []
        for n, (dx, dy) in enumerate(DIRS):
            if dy == 0:
                sx, tx, _ = side(dx, n_local)
                copies.append(send(n, dx, dy, main.at[sx], main.at[tx], ss, rs))
            else:
                s = 1 if dy == 1 else 0
                copies.append(send(n, dx, dy, ys.at[s], yr.at[1 - s, 1 - dx], ss, rs))
        return copies

    x2 = halo(p1, y1s, y1r, 4, s2, r2)
    start(x2)

    got_v2.wait()
    for px in range(2):
        for py in range(2):
            for tx in range(2):
                for ty in range(2):
                    s = []
                    for l in range(3):
                        terms = [
                            v2[9 * i + 3 * j + l].astype(F32) for i in TAPS[px][tx] for j in TAPS[py][ty]
                        ]
                        s.append(functools.reduce(jnp.add, terms))
                    block = cat([s[0], s[2], s[1] + s[2], s[0] + s[1]], 0).astype(BF)
                    g2[pl.ds(256 * (2 * px + py), 256), pl.ds(128 * (2 * tx + ty), 128)] = block
    got_v1.wait()
    for px in range(2):
        for py in range(2):
            for l in range(3):
                row = []
                for tx in range(2):
                    for ty in range(2):
                        terms = [
                            v1[9 * i + 3 * j + l].astype(F32) for i in TAPS[px][tx] for j in TAPS[py][ty]
                        ]
                        row.append(functools.reduce(jnp.add, terms).astype(BF))
                g1[pl.ds(96 * (2 * px + py) + 32 * l, 32), :] = cat(row, 1)

    arrive(x2)

    def sides(yr, n_local, c):
        found = []
        for x in range(n_local + 2):
            slot, at = (0, n_local - 1) if x == 0 else (2, 0) if x == n_local + 1 else (1, x - 1)
            inside = (gx > 0) if x == 0 else (gx < nx - 1) if x == n_local + 1 else True
            lo = yr[0, slot][:, at * c : (at + 1) * c]
            hi = yr[1, slot][:, at * c : (at + 1) * c]
            zero = jnp.zeros_like(lo)
            lo = jnp.where(inside & (gy > 0), lo, zero)
            hi = jnp.where(inside & (gy < ny - 1), hi, zero)
            parts = [lo, hi]
            if c < 64:
                parts.append(jnp.zeros((lo.shape[0], 128 - 2 * c), BF))
            found.append(cat(parts, 1))
        return found

    def mains(main, n_local):
        found = []
        for x in range(n_local + 2):
            v = main[x]
            if x == 0:
                v = jnp.where(gx > 0, v, jnp.zeros_like(v))
            if x == n_local + 1:
                v = jnp.where(gx < nx - 1, v, jnp.zeros_like(v))
            found.append(v)
        return found

    m1, h1 = mains(p1, 4), sides(y1r, 4, 32)
    lhs = cat([cat([cat([m1[x + i], h1[x + i]], 1) for i in range(3)], 1) for x in range(4)], 0)
    t = nn(lhs, k2[...])
    e2 = gelu(t[:, 256:512] + shifted(t[:, :256], 1, 0, 64) + shifted(t[:, 512:], -1, 0, 64)).astype(BF)
    f = e2.astype(F32)
    low = iota((64, 128), 1) < 64
    pick32 = ones_where(iota((32, 64), 1) == 2 * iota((32, 64), 0))
    p2v = []
    for x in range(2):
        a = f[128 * x : 128 * x + 64] + f[128 * x + 64 : 128 * x + 128]
        a0, a1 = a[:, :128], a[:, 128:]
        a = jnp.where(low, a0 + pltpu.roll(a0, 64, 1), a1 + pltpu.roll(a1, 64, 1))
        a = (a + pltpu.roll(a, 63, 0)) * 0.125
        a = nn(pick32, a.astype(BF))
        p2v.append(a)
        p2[x + 1] = a.astype(BF)
    low32 = iota((32, 128), 1) < 64
    y2s[0] = jnp.where(low32, p2v[0], pltpu.roll(p2v[1], 64, 1)).astype(BF)
    y2s[1] = jnp.where(low32, pltpu.roll(p2v[0], 64, 1), p2v[1]).astype(BF)
    x3 = halo(p2, y2s, y2r, 2, s3, r3)
    start(x3)

    rr, cc = iota((64, 64), 0), iota((64, 64), 1)
    split = ones_where(cc == 2 * (rr % 32) + rr // 32)
    for x in range(4):
        a = nn(split, e2[64 * x : 64 * x + 64])
        for y in range(4):
            ev = a[:32, 128 * (y // 2) : 128 * (y // 2) + 128]
            od = a[32:, 128 * (y // 2) : 128 * (y // 2) + 128]
            if y % 2 == 0:
                cell = jnp.where(low32, ev, pltpu.roll(od, 64, 1))
            else:
                cell = jnp.where(low32, pltpu.roll(ev, 64, 1), od)
            e2e[x + 1, y + 1] = cell.astype(BF)

    def cells(ref, n_local, ss, rs):
        copies = []
        for n, (dx, dy) in enumerate(DIRS):
            sx, tx, cx = side(dx, n_local)
            sy, ty, cy = side(dy, n_local)
            copies.append(
                send(n, dx, dy, ref.at[pl.ds(sx, cx), pl.ds(sy, cy)], ref.at[pl.ds(tx, cx), pl.ds(ty, cy)], ss, rs)
            )
        return copies

    xe2 = cells(e2e, 4, se2, re2)
    start(xe2)
    arrive(x3)

    m2, h2 = mains(p2, 2), sides(y2r, 2, 64)
    lhs = cat([cat([cat([m2[x + i], h2[x + i]], 1) for i in range(3)], 1) for x in range(2)], 0)
    t = nn(lhs, k3[...])
    e3 = gelu(t[:, 256:512] + shifted(t[:, :256], 1, 0, 32) + shifted(t[:, 512:], -1, 0, 32)).astype(BF)
    f = e3.astype(F32)
    a = f[:32] + f[32:]
    a = a[:, :128] + a[:, 128:]
    a = (a + pltpu.roll(a, 31, 0)) * 0.125
    pick16 = ones_where(iota((16, 32), 1) == 2 * iota((16, 32), 0))
    p3[2, gy + 2] = nn(pick16, a.astype(BF)).astype(BF)
    x4 = []
    for n, (dx, dy) in enumerate(window):
        x4.append(send(n, dx, dy, p3.at[2, gy + 2], p3.at[2 - dx, gy + 2], s4, r4))
    start(x4)
    for x in range(2):
        for y in range(2):
            e3e[x + 1, y + 1] = e3[32 * x : 32 * x + 32, 128 * y : 128 * y + 128]
    xe3 = cells(e3e, 2, se3, re3)
    start(xe3)

    for c in got_w4:
        c.wait()
    for n, (dx, dy) in enumerate(window):
        pltpu.make_async_remote_copy(
            src_ref=p3.at[2, gy + 2], dst_ref=p3.at[2 - dx, lax.rem(gy - dy + ny, ny) + 2],
            send_sem=s4.at[n], recv_sem=r4.at[n], device_id=target(dx, dy), device_id_type=MESH,
        ).wait_recv()

    cell = []
    for x in range(5):
        inside = (gx + (x - 2) >= 0) & (gx + (x - 2) < nx)
        line = []
        for y in range(5):
            v = p3[x, gy + y]
            line.append(jnp.where(inside, v, jnp.zeros_like(v)))
        cell.append(line)
    lhs = cat(
        [
            cat([cell[x + i][y + j] for i in range(3) for j in range(3)], 1)
            for x in range(3)
            for y in range(3)
        ],
        0,
    )
    t = nt(lhs, k4[...])
    e4 = gelu(t[:, 256:512] + shifted(t[:, :256], 1, 0, 16) + shifted(t[:, 512:], -1, 0, 16))

    def inside(x, y, width, n_local):
        ok = True
        if x == 0:
            ok = gx > 0
        if x == n_local + 1:
            ok = gx < nx - 1
        if y == 0:
            ok = ok & (gy > 0)
        if y == n_local + 1:
            ok = ok & (gy < ny - 1)
        return ok

    def kept(v, ok):
        return v if ok is True else jnp.where(ok, v, jnp.zeros_like(v))

    e4 = [kept(e4[16 * n : 16 * n + 16], inside(n // 3, n % 3, 16, 1)).astype(BF) for n in range(9)]

    for c in got_v3:
        c.wait()
    twice = ones_where(iota((32, 16), 1) == iota((32, 16), 0) // 2)
    up = nn(twice, cat(e4, 1)).astype(BF)
    at = ((0, 0, 1), (0, 1, 1), (1, 1, 2), (1, 2, 2))
    for x in range(4):
        for y in range(4):
            for i in range(3):
                for j in range(3):
                    n = 3 * at[x][i] + at[y][j]
                    pd3[pl.ds(128 * x + 32 * y, 32), pl.ds(256 * (3 * i + j), 256)] = up[:, 256 * n : 256 * n + 256]
    t = nt(pd3[...], kd3[...])
    v = gelu(t[:, 128:256] + shifted(t[:, :128], 1, 0, 32) + shifted(t[:, 256:], -1, 0, 32))
    arrive(xe3)
    for x in range(4):
        for y in range(4):
            n = 128 * x + 32 * y
            w = v[n : n + 32] + e3e[x, y].astype(F32)
            d3e[x, y] = kept(w, inside(x, y, 32, 2)).astype(BF)

    arrive(xe2)
    lane = iota((288, 128), 1) < 64
    lhs = cat(
        [
            cat([d3e[k, m], d3e[k, m + 1], d3e[k + 1, m], d3e[k + 1, m + 1]], 1)
            for k in range(3)
            for m in range(3)
        ],
        0,
    )
    t = nt(lhs, g2[...])
    for px in range(2):
        for py in range(2):
            n = 256 * (2 * px + py)
            a, b = t[:, n : n + 128], t[:, n + 128 : n + 256]
            v = gelu(b + jnp.where(lane, shifted(a, 1, 0, 32), shifted(a, -1, 0, 32)))
            for k in range(3):
                for m in range(3):
                    x, y = 2 * k + 1 - px, 2 * m + 1 - py
                    w = v[96 * k + 32 * m : 96 * k + 32 * m + 32] + e2e[x, y].astype(F32)
                    d2e[x, y] = kept(w, inside(x, y, 32, 4))

    rr, cc = iota((128, 64), 0), iota((128, 64), 1)
    spread = ones_where((rr // 4 == cc % 32) & (rr // 2 % 2 == cc // 32))
    for x in range(6):
        line = []
        for m in range(5):
            a, b = d2e[x, m], d2e[x, m + 1]
            top = jnp.where(low32, a, pltpu.roll(b, 64, 1))
            bottom = jnp.where(low32, pltpu.roll(a, 64, 1), b)
            line.append(cat([top, bottom], 0).astype(BF))
        a = nn(spread, cat(line, 1)).astype(BF)
        for m in range(5):
            q[x, m] = a[:, 128 * m : 128 * m + 128]

    done = []
    for k in range(5):
        for ms in ((0, 1), (2, 3), (4,)):
            t = nt(g1[...], cat([cat([q[k, m], q[k + 1, m]], 1) for m in ms], 0))
            for px in range(2):
                for py in range(2):
                    for h, m in enumerate(ms):
                        a, b = k - px, m - py
                        if not (0 <= a < 4 and 0 <= b < 4):
                            continue
                        x, y = 2 * a + px, 2 * b + py
                        n = 96 * (2 * px + py)
                        u = t[n : n + 96, 128 * h : 128 * h + 128]
                        v = gelu(u[32:64] + shifted(u[:32], 1, 1, 128) + shifted(u[64:], -1, 1, 128))
                        v = v + e1[x, pl.ds(32 * y, 32), :].astype(F32)
                        dd[x, y] = v.astype(BF)
        for x in (2 * k - 1, 2 * k):
            if 0 <= x < 8:
                c = pltpu.make_async_copy(dd.at[x], out.at[x], osem.at[x])
                c.start()
                done.append(c)

    for copies in (x1, x2, x3, x4, xe2, xe3):
        for c in copies:
            c.wait_send()
    for c in done:
        c.wait()


def local(features, w_enc1, w_enc2, w_enc3, w_enc4, w_dec3, w_dec2, w_dec1):
    w_enc2, w_enc3 = jnp.swapaxes(w_enc2, 1, 2), jnp.swapaxes(w_enc3, 1, 2)
    w_enc4, w_dec3 = w_enc4.reshape(9, 768, 128), w_dec3.reshape(9, 384, 256)
    args = (features, w_enc1, w_enc2, w_enc3, w_enc4, w_dec3, w_dec2, w_dec1)
    ny = lax.axis_size("gy")
    far = 5 * ny - 1
    dma = pltpu.SemaphoreType.DMA
    scratch = [pltpu.VMEM(a.shape, BF) for a in (features, w_enc1, w_enc2, w_enc3, w_dec2, w_dec1)]
    for shape in (
        (10, 320, 128), (8, 256, 128),
        (6, 64, 128), (2, 64, 128), (2, 3, 64, 128),
        (4, 32, 128), (2, 32, 128), (2, 3, 32, 128),
        (5, ny + 4, 16, 128), (6, 6, 32, 128), (4, 4, 32, 128),
        (192, 384), (768, 768), (768, 768), (768, 1152), (384, 2304), (1024, 512), (384, 256),
        (512, 2304), (4, 4, 32, 128),
    ):
        scratch.append(pltpu.VMEM(shape, BF))
    scratch.append(pltpu.VMEM((6, 6, 32, 128), F32))
    scratch.append(pltpu.VMEM((6, 5, 128, 128), BF))
    scratch.append(pltpu.VMEM((8, 8, 32, 128), BF))
    scratch += [dma((24,)), dma((8,))]
    for n in (8, 8, 8, far, 8, 8):
        scratch += [dma((n,)), dma((n,))]
    decoded = pl.pallas_call(
        kernel,
        out_shape=jax.ShapeDtypeStruct((8, 8, 32, 128), BF),
        in_specs=[pl.BlockSpec(memory_space=pl.ANY)] * 8,
        out_specs=pl.BlockSpec(memory_space=pl.ANY),
        scratch_shapes=scratch,
        compiler_params=pltpu.CompilerParams(
            collective_id=0, has_side_effects=True, vmem_limit_bytes=56 * 1024 * 1024
        ),
        cost_estimate=pl.CostEstimate(flops=2 * 1115000000, bytes_accessed=7000000, transcendentals=1000000),
    )(*args)
    return jnp.transpose(decoded, (2, 0, 1, 3))


def solution(mesh):
    return jax.shard_map(
        local,
        mesh=mesh,
        in_specs=(P(None, "gx", "gy", None), P(), P(), P(), P(), P(), P(), P()),
        out_specs=P(None, "gx", "gy", None),
        check_vma=False,
    )
```

```python
import functools

import jax
import jax.numpy as jnp
from jax import lax
from jax.experimental import pallas as pl
from jax.experimental.pallas import tpu as pltpu
from jax.sharding import PartitionSpec as P

BF = jnp.bfloat16
F32 = jnp.float32
MESH = pl.DeviceIdType.MESH
DIRS = [(-1, -1), (-1, 1), (1, -1), (1, 1), (-1, 0), (1, 0), (0, -1), (0, 1)]
TAPS = (((0,), (1, 2)), ((0, 1), (2,)))


def nn(a, b):
    return lax.dot_general(a, b, (((1,), (0,)), ((), ())), preferred_element_type=F32)


def nt(a, b):
    return lax.dot_general(a, b, (((1,), (1,)), ((), ())), preferred_element_type=F32)


def iota(shape, dim):
    return lax.broadcasted_iota(jnp.int32, shape, dim)


def ones_where(mask):
    return jnp.where(mask, 1.0, 0.0).astype(BF)


def gelu(x):
    return 0.5 * x * (1.0 + jnp.tanh(0.7978845608028654 * (x + 0.044715 * (x * x * x))))


def shifted(v, step, axis, period):
    n = v.shape[axis]
    place = iota(v.shape, axis) % period
    edge = 0 if step == 1 else period - 1
    return jnp.where(place == edge, 0.0, pltpu.roll(v, step % n, axis))


def cat(parts, axis):
    return parts[0] if len(parts) == 1 else jnp.concatenate(parts, axis=axis)


def side(d, n, width=1, pad=1):
    if d == 1:
        return (pad + (n - 1)) * width, 0, width
    if d == -1:
        return pad * width, (n + pad) * width, width
    return pad * width, pad * width, n * width


def kernel(
    feat, w1h, w2h, w3h, w4h, v3h, v2h, v1h, out,
    fv, w1, w2, w3, v2, v1,
    fext, e1, p1, p3, e2e, e3e,
    k1, k2, k3, k4, kd3, g2, g1, pd3, d3e, d2e, q, dd,
    lsem, osem, s1, r1, s2, r2, s4, r4, se3, re3,
):
    gx, gy = lax.axis_index("gx"), lax.axis_index("gy")
    nx, ny = lax.axis_size("gx"), lax.axis_size("gy")

    loads = []

    def load(src, dst):
        c = pltpu.make_async_copy(src, dst, lsem.at[len(loads)])
        c.start()
        loads.append(c)
        return c

    def target(dx, dy):
        return (lax.rem(gx + dx + nx, nx), lax.rem(gy + dy + ny, ny))

    barrier = pltpu.get_barrier_semaphore()
    got_feat = load(feat, fv)
    for dx, dy in DIRS:
        pl.semaphore_signal(barrier, inc=1, device_id=target(dx, dy), device_id_type=MESH)
    got_w1, got_w2, got_w3 = load(w1h, w1), load(w2h, w2), load(w3h, w3)
    got_v2, got_v1 = load(v2h, v2), load(v1h, v1)
    got_w4 = [load(w4h.at[n], k4.at[:, pl.ds(128 * n, 128)]) for n in range(9)]
    got_v3 = [load(v3h.at[n], kd3.at[:, pl.ds(256 * n, 256)]) for n in range(9)]

    def far(d):
        return abs(d[0]) + min(d[1], ny - d[1])

    window = [(dx, dy) for dx in range(-2, 3) for dy in range(ny) if (dx, dy) != (0, 0)]
    window.sort(key=far, reverse=True)

    def send(n, dx, dy, src, dst, ss, rs):
        return pltpu.make_async_remote_copy(
            src_ref=src, dst_ref=dst, send_sem=ss.at[n], recv_sem=rs.at[n],
            device_id=target(dx, dy), device_id_type=MESH,
        )

    def start(copies):
        for c in copies:
            c.start()

    def arrive(copies):
        for c in copies:
            c.wait_recv()

    got_feat.wait()
    r, c = iota((256, 256), 0), iota((256, 256), 1)
    perm = ones_where((r // 32 == c % 8) & (r % 32 == c // 8))

    def place(x, carry):
        a = fv[:, pl.ds(2 * x, 1)].astype(F32).reshape(256, 128).astype(BF)
        b = fv[:, pl.ds(2 * x + 1, 1)].astype(F32).reshape(256, 128).astype(BF)
        t = nn(perm, cat([a, b], 1)).astype(BF)
        fext[2 * x + 1, pl.ds(32, 256), :] = t[:, :128]
        fext[2 * x + 2, pl.ds(32, 256), :] = t[:, 128:]
        return carry

    lax.fori_loop(0, 4, place, 0)
    for n in range(4):
        p3[:, n if n < 2 else n + 4] = jnp.zeros((5, 16, 128), BF)
    pl.semaphore_wait(barrier, len(DIRS))

    x1 = []
    for n, (dx, dy) in enumerate(DIRS):
        sx, tx, cx = side(dx, 8)
        sy, ty, cy = side(dy, 8, 32)
        x1.append(
            send(n, dx, dy, fext.at[pl.ds(sx, cx), pl.ds(sy, cy)], fext.at[pl.ds(tx, cx), pl.ds(ty, cy)], s1, r1)
        )
    start(x1)

    got_w1.wait()
    t = None
    r, c = iota((32, 256), 0), iota((32, 256), 1)
    for j in range(3):
        taps = cat([w1[pl.ds(9 * i + 3 * j, 3)].reshape(96, 32) for i in range(3)], 0)
        u = nn(taps, ones_where((r == c % 32) & (c // 32 % 4 == c // 128 + j)))
        t = u if t is None else t + u
    t = t.astype(BF)
    for i in range(3):
        for l in range(3):
            for yo in range(2):
                k1[pl.ds(64 * l + 32 * yo, 32), pl.ds(128 * i, 128)] = t[
                    96 * i + 32 * l : 96 * i + 32 * l + 32, 128 * yo : 128 * yo + 128
                ]

    def enc1(xa, xb, b):
        rhs = cat(
            [cat([fext[xa + i, pl.ds(64 * b, 128), :], fext[xb + i, pl.ds(64 * b, 128), :]], 1) for i in range(3)],
            0,
        )
        t = nn(k1[...], rhs)
        for h, x in enumerate((xa, xb)):
            u = t[:, 128 * h : 128 * (h + 1)]
            v = u[64:128] + shifted(u[:64], 1, 1, 128) + shifted(u[128:], -1, 1, 128)
            e1[x, pl.ds(64 * b, 64), :] = gelu(v).astype(BF)

    def enc1_inner(n, carry, blocks):
        for b in blocks:
            enc1(2 * n + 1, 2 * n + 2, b)
        return carry

    lax.fori_loop(0, 3, functools.partial(enc1_inner, blocks=(1, 2)), 0)

    got_w2.wait()
    r, c = iota((64, 256), 0), iota((64, 256), 1)
    spots = [ones_where(c == r + 64 * yo) for yo in range(4)]
    taps = [cat([w2[pl.ds(9 * i + 3 * j, 3)].reshape(96, 64) for i in range(3)], 0) for j in range(3)]
    for yi in range(1, 7):
        t = None
        for j in range(3):
            if 0 <= yi - 1 - j < 4:
                u = nn(taps[j], spots[yi - 1 - j])
                t = u if t is None else t + u
        t = t.astype(BF)
        for i in range(3):
            for l in range(3):
                k2[pl.ds(256 * i + 32 * yi, 32), pl.ds(256 * l, 256)] = t[96 * i + 32 * l : 96 * i + 32 * l + 32]
    for i in range(3):
        for yi in (0, 7):
            k2[pl.ds(256 * i + 32 * yi, 32), :] = jnp.zeros((32, 768), BF)
    got_w3.wait()
    z128 = jnp.zeros((64, 128), BF)
    for i in range(3):
        for yi in range(4):
            for l in range(3):
                for yo in range(2):
                    j = yi - yo
                    k3[pl.ds(256 * i + 64 * yi, 64), pl.ds(256 * l + 128 * yo, 128)] = (
                        w3[9 * i + 3 * j + l] if 0 <= j < 3 else z128
                    )

    arrive(x1[6:])

    @pl.when(gy == 0)
    def _():
        fext[pl.ds(1, 8), pl.ds(0, 32)] = jnp.zeros((8, 32, 128), BF)

    @pl.when(gy == ny - 1)
    def _():
        fext[pl.ds(1, 8), pl.ds(288, 32)] = jnp.zeros((8, 32, 128), BF)

    lax.fori_loop(0, 3, functools.partial(enc1_inner, blocks=(0, 3)), 0)

    def pool1(x):
        a = e1[2 * x].astype(F32) + e1[2 * x + 1].astype(F32)
        a = cat([a[64 * b : 64 * b + 32] + a[64 * b + 32 : 64 * b + 64] for b in range(4)], 0)
        a = (a + pltpu.roll(a, 127, 1)) * 0.125
        return a.astype(BF)

    pick64 = ones_where(iota((64, 128), 1) == 2 * iota((64, 128), 0))
    pooled = [None, pool1(1), pool1(2), None]
    arrive(x1[:6])

    @pl.when(gx == 0)
    def _():
        fext[0] = jnp.zeros((320, 128), BF)

    @pl.when(gx == nx - 1)
    def _():
        fext[9] = jnp.zeros((320, 128), BF)

    @pl.when(gy == 0)
    def _():
        for x in (0, 9):
            fext[x, pl.ds(0, 32)] = jnp.zeros((32, 128), BF)

    @pl.when(gy == ny - 1)
    def _():
        for x in (0, 9):
            fext[x, pl.ds(288, 32)] = jnp.zeros((32, 128), BF)

    for b in range(4):
        enc1(0, 7, b)
    pooled[0], pooled[3] = pool1(0), pool1(3)

    t = nt(pick64, cat(pooled, 0)).astype(BF)
    for x in range(4):
        p1[1, x + 3] = t[:, 128 * x : 128 * x + 128]
    x2 = []
    for n, (dx, dy) in enumerate(DIRS):
        sx, tx, cx = ((3, 7, 3), (3, 3, 4), (4, 0, 3))[dx + 1]
        x2.append(send(n, dx, dy, p1.at[1, pl.ds(sx, cx)], p1.at[1 - dy, pl.ds(tx, cx)], s2, r2))
    start(x2)

    got_v2.wait()
    for px in range(2):
        for py in range(2):
            for tx in range(2):
                for ty in range(2):
                    s = []
                    for l in range(3):
                        terms = [
                            v2[9 * i + 3 * j + l].astype(F32) for i in TAPS[px][tx] for j in TAPS[py][ty]
                        ]
                        s.append(functools.reduce(jnp.add, terms))
                    block = cat([s[0], s[2], s[1] + s[2], s[0] + s[1]], 0).astype(BF)
                    g2[pl.ds(256 * (2 * px + py), 256), pl.ds(128 * (2 * tx + ty), 128)] = block
    got_v1.wait()
    for px in range(2):
        for py in range(2):
            for l in range(3):
                row = []
                for tx in range(2):
                    for ty in range(2):
                        terms = [
                            v1[9 * i + 3 * j + l].astype(F32) for i in TAPS[px][tx] for j in TAPS[py][ty]
                        ]
                        row.append(functools.reduce(jnp.add, terms).astype(BF))
                g1[pl.ds(96 * (2 * px + py) + 32 * l, 32), :] = cat(row, 1)

    arrive(x2)

    @pl.when(gx == 0)
    def _():
        p1[:, pl.ds(0, 3)] = jnp.zeros((3, 3, 64, 128), BF)

    @pl.when(gx == nx - 1)
    def _():
        p1[:, pl.ds(7, 3)] = jnp.zeros((3, 3, 64, 128), BF)

    @pl.when(gy == 0)
    def _():
        p1[0] = jnp.zeros((10, 64, 128), BF)

    @pl.when(gy == ny - 1)
    def _():
        p1[2] = jnp.zeros((10, 64, 128), BF)

    low = iota((64, 128), 1) < 64
    e2 = []
    pairs = []
    for g in range(2):
        lhs = cat(
            [cat([cat([p1[g, x + i], p1[g + 1, x + i]], 1) for i in range(3)], 1) for x in range(8)], 0
        )
        t = nn(lhs, k2[...])
        t = gelu(t[:, 256:512] + shifted(t[:, :256], 1, 0, 64) + shifted(t[:, 512:], -1, 0, 64))
        rows = []
        for x in range(8):
            v = t[64 * x : 64 * x + 64]
            halves = [v[:, :128], v[:, 128:]]
            for h in range(2):
                ok = True if h != g else (gy > 0) if g == 0 else (gy < ny - 1)
                if x < 2:
                    ok = ok & (gx > 0)
                if x > 5:
                    ok = ok & (gx < nx - 1)
                if ok is not True:
                    halves[h] = jnp.where(ok, halves[h], jnp.zeros_like(halves[h]))
            rows.append([v.astype(BF) for v in halves])
        e2.append(rows)
        for x in range(4):
            a0, a1 = [rows[2 * x][h].astype(F32) + rows[2 * x + 1][h].astype(F32) for h in range(2)]
            a = jnp.where(low, a0 + pltpu.roll(a0, 64, 1), a1 + pltpu.roll(a1, 64, 1))
            pairs.append(((a + pltpu.roll(a, 63, 0)) * 0.125).astype(BF))
    pick32 = ones_where(iota((32, 64), 1) == 2 * iota((32, 64), 0))
    t = nn(pick32, cat(pairs, 1)).astype(BF)
    p2 = [cat([t[:, 128 * x : 128 * x + 128], t[:, 512 + 128 * x : 512 + 128 * x + 128]], 1) for x in range(4)]

    lhs = cat([cat([p2[x + i] for i in range(3)], 1) for x in range(2)], 0)
    t = nn(lhs, k3[...])
    e3 = gelu(t[:, 256:512] + shifted(t[:, :256], 1, 0, 32) + shifted(t[:, 512:], -1, 0, 32)).astype(BF)
    f = e3.astype(F32)
    a = f[:32] + f[32:]
    a = a[:, :128] + a[:, 128:]
    a = (a + pltpu.roll(a, 31, 0)) * 0.125
    pick16 = ones_where(iota((16, 32), 1) == 2 * iota((16, 32), 0))
    p3[2, gy + 2] = nn(pick16, a.astype(BF)).astype(BF)
    x4 = []
    for n, (dx, dy) in enumerate(window):
        x4.append(send(n, dx, dy, p3.at[2, gy + 2], p3.at[2 - dx, gy + 2], s4, r4))
    start(x4)
    for x in range(2):
        for y in range(2):
            e3e[x + 1, y + 1] = e3[32 * x : 32 * x + 32, 128 * y : 128 * y + 128]
    def cells(ref, n_local, ss, rs):
        copies = []
        for n, (dx, dy) in enumerate(DIRS):
            sx, tx, cx = side(dx, n_local)
            sy, ty, cy = side(dy, n_local)
            copies.append(
                send(n, dx, dy, ref.at[pl.ds(sx, cx), pl.ds(sy, cy)], ref.at[pl.ds(tx, cx), pl.ds(ty, cy)], ss, rs)
            )
        return copies

    xe3 = cells(e3e, 2, se3, re3)
    start(xe3)

    low32 = iota((32, 128), 1) < 64
    rr, cc = iota((64, 64), 0), iota((64, 64), 1)
    split = ones_where(cc == 2 * (rr % 32) + rr // 32)
    for x in range(6):
        t = nn(split, cat([e2[g][x + 1][h] for g in range(2) for h in range(2)], 1))
        for y in range(6):
            n = 128 * ((y + 1) // 2)
            ev, od = t[:32, n : n + 128], t[32:, n : n + 128]
            if y % 2 == 1:
                cell = jnp.where(low32, ev, pltpu.roll(od, 64, 1))
            else:
                cell = jnp.where(low32, pltpu.roll(ev, 64, 1), od)
            e2e[x, y] = cell.astype(BF)

    for c in got_w4:
        c.wait()
    for n, (dx, dy) in enumerate(window):
        pltpu.make_async_remote_copy(
            src_ref=p3.at[2, gy + 2], dst_ref=p3.at[2 - dx, lax.rem(gy - dy + ny, ny) + 2],
            send_sem=s4.at[n], recv_sem=r4.at[n], device_id=target(dx, dy), device_id_type=MESH,
        ).wait_recv()

    cell = []
    for x in range(5):
        inside = (gx + (x - 2) >= 0) & (gx + (x - 2) < nx)
        line = []
        for y in range(5):
            v = p3[x, gy + y]
            line.append(jnp.where(inside, v, jnp.zeros_like(v)))
        cell.append(line)
    lhs = cat(
        [
            cat([cell[x + i][y + j] for i in range(3) for j in range(3)], 1)
            for x in range(3)
            for y in range(3)
        ],
        0,
    )
    t = nt(k4[...], lhs)
    e4 = gelu(t[256:512] + shifted(t[:256], 1, 1, 16) + shifted(t[512:], -1, 1, 16))
    n = iota((256, 144), 1) // 16
    x, y = gx - 1 + n // 3, gy - 1 + n % 3
    e4 = jnp.where((x >= 0) & (x < nx) & (y >= 0) & (y < ny), e4, 0.0).astype(BF)

    def inside(x, y, width, n_local):
        ok = True
        if x == 0:
            ok = gx > 0
        if x == n_local + 1:
            ok = gx < nx - 1
        if y == 0:
            ok = ok & (gy > 0)
        if y == n_local + 1:
            ok = ok & (gy < ny - 1)
        return ok

    def kept(v, ok):
        return v if ok is True else jnp.where(ok, v, jnp.zeros_like(v))


    for c in got_v3:
        c.wait()
    up = nt(ones_where(iota((288, 144), 1) == iota((288, 144), 0) // 2), e4).astype(BF)
    at = ((0, 0, 1), (0, 1, 1), (1, 1, 2), (1, 2, 2))
    for x in range(4):
        for y in range(4):
            for i in range(3):
                for j in range(3):
                    n = 3 * at[x][i] + at[y][j]
                    pd3[pl.ds(128 * x + 32 * y, 32), pl.ds(256 * (3 * i + j), 256)] = up[32 * n : 32 * n + 32]
    t = nt(pd3[...], kd3[...])
    v = gelu(t[:, 128:256] + shifted(t[:, :128], 1, 0, 32) + shifted(t[:, 256:], -1, 0, 32))
    arrive(xe3)
    for x in range(4):
        for y in range(4):
            n = 128 * x + 32 * y
            w = v[n : n + 32] + e3e[x, y].astype(F32)
            d3e[x, y] = kept(w, inside(x, y, 32, 2)).astype(BF)

    lane = iota((288, 128), 1) < 64
    lhs = cat(
        [
            cat([d3e[k, m], d3e[k, m + 1], d3e[k + 1, m], d3e[k + 1, m + 1]], 1)
            for k in range(3)
            for m in range(3)
        ],
        0,
    )
    t = nt(lhs, g2[...])
    for px in range(2):
        for py in range(2):
            n = 256 * (2 * px + py)
            a, b = t[:, n : n + 128], t[:, n + 128 : n + 256]
            v = gelu(b + jnp.where(lane, shifted(a, 1, 0, 32), shifted(a, -1, 0, 32)))
            for k in range(3):
                for m in range(3):
                    x, y = 2 * k + 1 - px, 2 * m + 1 - py
                    w = v[96 * k + 32 * m : 96 * k + 32 * m + 32] + e2e[x, y].astype(F32)
                    d2e[x, y] = kept(w, inside(x, y, 32, 4))

    rr, cc = iota((128, 64), 0), iota((128, 64), 1)
    spread = ones_where((rr // 4 == cc % 32) & (rr // 2 % 2 == cc // 32))
    for x in range(6):
        line = []
        for m in range(5):
            a, b = d2e[x, m], d2e[x, m + 1]
            top = jnp.where(low32, a, pltpu.roll(b, 64, 1))
            bottom = jnp.where(low32, pltpu.roll(a, 64, 1), b)
            line.append(cat([top, bottom], 0).astype(BF))
        a = nn(spread, cat(line, 1)).astype(BF)
        for m in range(5):
            q[x, m] = a[:, 128 * m : 128 * m + 128]

    done = []
    for k in range(5):
        for ms in ((0, 1), (2, 3), (4,)):
            t = nt(g1[...], cat([cat([q[k, m], q[k + 1, m]], 1) for m in ms], 0))
            for px in range(2):
                for py in range(2):
                    for h, m in enumerate(ms):
                        a, b = k - px, m - py
                        if not (0 <= a < 4 and 0 <= b < 4):
                            continue
                        x, y = 2 * a + px, 2 * b + py
                        n = 96 * (2 * px + py)
                        u = t[n : n + 96, 128 * h : 128 * h + 128]
                        v = gelu(u[32:64] + shifted(u[:32], 1, 1, 128) + shifted(u[64:], -1, 1, 128))
                        v = v + e1[x, pl.ds(32 * y, 32), :].astype(F32)
                        dd[x, y] = v.astype(BF)
        for x in (2 * k - 1, 2 * k):
            if 0 <= x < 8:
                c = pltpu.make_async_copy(dd.at[x], out.at[x], osem.at[x])
                c.start()
                done.append(c)

    for copies in (x1, x2, x4, xe3):
        for c in copies:
            c.wait_send()
    for c in done:
        c.wait()


def local(features, w_enc1, w_enc2, w_enc3, w_enc4, w_dec3, w_dec2, w_dec1):
    w_enc2, w_enc3 = jnp.swapaxes(w_enc2, 1, 2), jnp.swapaxes(w_enc3, 1, 2)
    w_enc4, w_dec3 = w_enc4.reshape(9, 768, 128), w_dec3.reshape(9, 384, 256)
    args = (features, w_enc1, w_enc2, w_enc3, w_enc4, w_dec3, w_dec2, w_dec1)
    ny = lax.axis_size("gy")
    far = 5 * ny - 1
    dma = pltpu.SemaphoreType.DMA
    scratch = [pltpu.VMEM(a.shape, BF) for a in (features, w_enc1, w_enc2, w_enc3, w_dec2, w_dec1)]
    for shape in (
        (10, 320, 128), (8, 256, 128),
        (3, 10, 64, 128),
        (5, ny + 4, 16, 128), (6, 6, 32, 128), (4, 4, 32, 128),
        (192, 384), (768, 768), (768, 768), (768, 1152), (384, 2304), (1024, 512), (384, 256),
        (512, 2304), (4, 4, 32, 128),
    ):
        scratch.append(pltpu.VMEM(shape, BF))
    scratch.append(pltpu.VMEM((6, 6, 32, 128), F32))
    scratch.append(pltpu.VMEM((6, 5, 128, 128), BF))
    scratch.append(pltpu.VMEM((8, 8, 32, 128), BF))
    scratch += [dma((24,)), dma((8,))]
    for n in (8, 8, far, 8):
        scratch += [dma((n,)), dma((n,))]
    decoded = pl.pallas_call(
        kernel,
        out_shape=jax.ShapeDtypeStruct((8, 8, 32, 128), BF),
        in_specs=[pl.BlockSpec(memory_space=pl.ANY)] * 8,
        out_specs=pl.BlockSpec(memory_space=pl.ANY),
        scratch_shapes=scratch,
        compiler_params=pltpu.CompilerParams(
            collective_id=0, has_side_effects=True, vmem_limit_bytes=56 * 1024 * 1024
        ),
        cost_estimate=pl.CostEstimate(flops=2 * 1115000000, bytes_accessed=7000000, transcendentals=1000000),
    )(*args)
    return jnp.transpose(decoded, (2, 0, 1, 3))


def solution(mesh):
    return jax.shard_map(
        local,
        mesh=mesh,
        in_specs=(P(None, "gx", "gy", None), P(), P(), P(), P(), P(), P(), P()),
        out_specs=P(None, "gx", "gy", None),
        check_vma=False,
    )
```

```python
import functools

import jax
import jax.numpy as jnp
from jax import lax
from jax.experimental import pallas as pl
from jax.experimental.pallas import tpu as pltpu
from jax.sharding import PartitionSpec as P

BF = jnp.bfloat16
F32 = jnp.float32
MESH = pl.DeviceIdType.MESH
DIRS = [(-1, -1), (-1, 1), (1, -1), (1, 1), (-1, 0), (1, 0), (0, -1), (0, 1)]
TAPS = (((0,), (1, 2)), ((0, 1), (2,)))


def nn(a, b):
    return lax.dot_general(a, b, (((1,), (0,)), ((), ())), preferred_element_type=F32)


def nt(a, b):
    return lax.dot_general(a, b, (((1,), (1,)), ((), ())), preferred_element_type=F32)


def iota(shape, dim):
    return lax.broadcasted_iota(jnp.int32, shape, dim)


def ones_where(mask):
    return jnp.where(mask, 1.0, 0.0).astype(BF)


def gelu(x):
    return 0.5 * x * (1.0 + jnp.tanh(0.7978845608028654 * (x + 0.044715 * (x * x * x))))


def shifted(v, step, axis, period):
    n = v.shape[axis]
    place = iota(v.shape, axis) % period
    edge = 0 if step == 1 else period - 1
    return jnp.where(place == edge, 0.0, pltpu.roll(v, step % n, axis))


def cat(parts, axis):
    return parts[0] if len(parts) == 1 else jnp.concatenate(parts, axis=axis)


def side(d, n, width=1, pad=1):
    if d == 1:
        return (pad + (n - 1)) * width, 0, width
    if d == -1:
        return pad * width, (n + pad) * width, width
    return pad * width, pad * width, n * width


def kernel(
    feat, w1h, w2h, w3h, w4h, v3h, v2h, v1h, out,
    fv, w1, w2, w3, v2, v1,
    fext, e1, p1, p3, e2e, e3e,
    k1, k2, k3, k4, kd3, g2, g1, pd3, d3e, d2e, q,
    lsem, s1, r1, s2, r2, s4, r4, se3, re3,
):
    gx, gy = lax.axis_index("gx"), lax.axis_index("gy")
    nx, ny = lax.axis_size("gx"), lax.axis_size("gy")

    loads = []

    def load(src, dst):
        c = pltpu.make_async_copy(src, dst, lsem.at[len(loads)])
        c.start()
        loads.append(c)
        return c

    def target(dx, dy):
        return (lax.rem(gx + dx + nx, nx), lax.rem(gy + dy + ny, ny))

    barrier = pltpu.get_barrier_semaphore()
    got_feat = load(feat, fv)
    for dx, dy in DIRS:
        pl.semaphore_signal(barrier, inc=1, device_id=target(dx, dy), device_id_type=MESH)
    got_w1, got_w2, got_w3 = load(w1h, w1), load(w2h, w2), load(w3h, w3)
    got_v2, got_v1 = load(v2h, v2), load(v1h, v1)
    got_w4 = [load(w4h.at[n], k4.at[:, pl.ds(128 * n, 128)]) for n in range(9)]
    got_v3 = [load(v3h.at[n], kd3.at[:, pl.ds(256 * n, 256)]) for n in range(9)]

    def far(d):
        return abs(d[0]) + min(d[1], ny - d[1])

    window = [(dx, dy) for dx in range(-2, 3) for dy in range(ny) if (dx, dy) != (0, 0)]
    window.sort(key=far, reverse=True)

    def send(n, dx, dy, src, dst, ss, rs):
        return pltpu.make_async_remote_copy(
            src_ref=src, dst_ref=dst, send_sem=ss.at[n], recv_sem=rs.at[n],
            device_id=target(dx, dy), device_id_type=MESH,
        )

    def start(copies):
        for c in copies:
            c.start()

    def arrive(copies):
        for c in copies:
            c.wait_recv()

    got_feat.wait()
    r, c = iota((256, 256), 0), iota((256, 256), 1)
    perm = ones_where((r // 32 == c % 8) & (r % 32 == c // 8))

    def place(x, carry):
        a = fv[:, pl.ds(2 * x, 1)].astype(F32).reshape(256, 128).astype(BF)
        b = fv[:, pl.ds(2 * x + 1, 1)].astype(F32).reshape(256, 128).astype(BF)
        t = nn(perm, cat([a, b], 1)).astype(BF)
        fext[2 * x + 1, pl.ds(32, 256), :] = t[:, :128]
        fext[2 * x + 2, pl.ds(32, 256), :] = t[:, 128:]
        return carry

    lax.fori_loop(0, 4, place, 0)
    for n in range(4):
        p3[:, n if n < 2 else n + 4] = jnp.zeros((5, 16, 128), BF)
    pl.semaphore_wait(barrier, len(DIRS))

    x1 = []
    for n, (dx, dy) in enumerate(DIRS):
        sx, tx, cx = side(dx, 8)
        sy, ty, cy = side(dy, 8, 32)
        x1.append(
            send(n, dx, dy, fext.at[pl.ds(sx, cx), pl.ds(sy, cy)], fext.at[pl.ds(tx, cx), pl.ds(ty, cy)], s1, r1)
        )
    start(x1)

    got_w1.wait()
    t = None
    r, c = iota((32, 256), 0), iota((32, 256), 1)
    for j in range(3):
        taps = cat([w1[pl.ds(9 * i + 3 * j, 3)].reshape(96, 32) for i in range(3)], 0)
        u = nn(taps, ones_where((r == c % 32) & (c // 32 % 4 == c // 128 + j)))
        t = u if t is None else t + u
    t = t.astype(BF)
    for i in range(3):
        for l in range(3):
            for yo in range(2):
                k1[pl.ds(64 * l + 32 * yo, 32), pl.ds(128 * i, 128)] = t[
                    96 * i + 32 * l : 96 * i + 32 * l + 32, 128 * yo : 128 * yo + 128
                ]

    def enc1(xa, xb, b):
        rhs = cat(
            [cat([fext[xa + i, pl.ds(64 * b, 128), :], fext[xb + i, pl.ds(64 * b, 128), :]], 1) for i in range(3)],
            0,
        )
        t = nn(k1[...], rhs)
        for h, x in enumerate((xa, xb)):
            u = t[:, 128 * h : 128 * (h + 1)]
            v = u[64:128] + shifted(u[:64], 1, 1, 128) + shifted(u[128:], -1, 1, 128)
            e1[x, pl.ds(64 * b, 64), :] = gelu(v).astype(BF)

    def enc1_inner(n, carry, blocks):
        for b in blocks:
            enc1(2 * n + 1, 2 * n + 2, b)
        return carry

    lax.fori_loop(0, 3, functools.partial(enc1_inner, blocks=(1, 2)), 0)

    got_w2.wait()
    r, c = iota((64, 256), 0), iota((64, 256), 1)
    spots = [ones_where(c == r + 64 * yo) for yo in range(4)]
    taps = [cat([w2[pl.ds(9 * i + 3 * j, 3)].reshape(96, 64) for i in range(3)], 0) for j in range(3)]
    for yi in range(1, 7):
        t = None
        for j in range(3):
            if 0 <= yi - 1 - j < 4:
                u = nn(taps[j], spots[yi - 1 - j])
                t = u if t is None else t + u
        t = t.astype(BF)
        for i in range(3):
            for l in range(3):
                k2[pl.ds(256 * i + 32 * yi, 32), pl.ds(256 * l, 256)] = t[96 * i + 32 * l : 96 * i + 32 * l + 32]
    for i in range(3):
        for yi in (0, 7):
            k2[pl.ds(256 * i + 32 * yi, 32), :] = jnp.zeros((32, 768), BF)
    got_w3.wait()
    z128 = jnp.zeros((64, 128), BF)
    for i in range(3):
        for yi in range(4):
            for l in range(3):
                for yo in range(2):
                    j = yi - yo
                    k3[pl.ds(256 * i + 64 * yi, 64), pl.ds(256 * l + 128 * yo, 128)] = (
                        w3[9 * i + 3 * j + l] if 0 <= j < 3 else z128
                    )

    arrive(x1[6:])

    @pl.when(gy == 0)
    def _():
        fext[pl.ds(1, 8), pl.ds(0, 32)] = jnp.zeros((8, 32, 128), BF)

    @pl.when(gy == ny - 1)
    def _():
        fext[pl.ds(1, 8), pl.ds(288, 32)] = jnp.zeros((8, 32, 128), BF)

    lax.fori_loop(0, 3, functools.partial(enc1_inner, blocks=(0, 3)), 0)

    def pool1(x):
        a = e1[2 * x].astype(F32) + e1[2 * x + 1].astype(F32)
        a = cat([a[64 * b : 64 * b + 32] + a[64 * b + 32 : 64 * b + 64] for b in range(4)], 0)
        a = (a + pltpu.roll(a, 127, 1)) * 0.125
        return a.astype(BF)

    pick64 = ones_where(iota((64, 128), 1) == 2 * iota((64, 128), 0))
    pooled = [None, pool1(1), pool1(2), None]
    arrive(x1[:6])

    @pl.when(gx == 0)
    def _():
        fext[0] = jnp.zeros((320, 128), BF)

    @pl.when(gx == nx - 1)
    def _():
        fext[9] = jnp.zeros((320, 128), BF)

    @pl.when(gy == 0)
    def _():
        for x in (0, 9):
            fext[x, pl.ds(0, 32)] = jnp.zeros((32, 128), BF)

    @pl.when(gy == ny - 1)
    def _():
        for x in (0, 9):
            fext[x, pl.ds(288, 32)] = jnp.zeros((32, 128), BF)

    for b in range(4):
        enc1(0, 7, b)
    pooled[0], pooled[3] = pool1(0), pool1(3)

    t = nt(pick64, cat(pooled, 0)).astype(BF)
    for x in range(4):
        p1[1, x + 3] = t[:, 128 * x : 128 * x + 128]
    x2 = []
    for n, (dx, dy) in enumerate(DIRS):
        sx, tx, cx = ((3, 7, 3), (3, 3, 4), (4, 0, 3))[dx + 1]
        x2.append(send(n, dx, dy, p1.at[1, pl.ds(sx, cx)], p1.at[1 - dy, pl.ds(tx, cx)], s2, r2))
    start(x2)

    got_v2.wait()
    for px in range(2):
        for py in range(2):
            for tx in range(2):
                for ty in range(2):
                    s = []
                    for l in range(3):
                        terms = [
                            v2[9 * i + 3 * j + l].astype(F32) for i in TAPS[px][tx] for j in TAPS[py][ty]
                        ]
                        s.append(functools.reduce(jnp.add, terms))
                    block = cat([s[0], s[2], s[1] + s[2], s[0] + s[1]], 0).astype(BF)
                    g2[pl.ds(256 * (2 * px + py), 256), pl.ds(128 * (2 * tx + ty), 128)] = block
    got_v1.wait()
    for px in range(2):
        for py in range(2):
            for l in range(3):
                row = []
                for tx in range(2):
                    for ty in range(2):
                        terms = [
                            v1[9 * i + 3 * j + l].astype(F32) for i in TAPS[px][tx] for j in TAPS[py][ty]
                        ]
                        row.append(functools.reduce(jnp.add, terms).astype(BF))
                g1[pl.ds(96 * (2 * px + py) + 32 * l, 32), :] = cat(row, 1)

    arrive(x2)

    @pl.when(gx == 0)
    def _():
        p1[:, pl.ds(0, 3)] = jnp.zeros((3, 3, 64, 128), BF)

    @pl.when(gx == nx - 1)
    def _():
        p1[:, pl.ds(7, 3)] = jnp.zeros((3, 3, 64, 128), BF)

    @pl.when(gy == 0)
    def _():
        p1[0] = jnp.zeros((10, 64, 128), BF)

    @pl.when(gy == ny - 1)
    def _():
        p1[2] = jnp.zeros((10, 64, 128), BF)

    low = iota((64, 128), 1) < 64
    e2 = []
    pairs = []
    for g in range(2):
        lhs = cat(
            [cat([cat([p1[g, x + i], p1[g + 1, x + i]], 1) for i in range(3)], 1) for x in range(8)], 0
        )
        t = nn(lhs, k2[...])
        t = gelu(t[:, 256:512] + shifted(t[:, :256], 1, 0, 64) + shifted(t[:, 512:], -1, 0, 64))
        rows = []
        for x in range(8):
            v = t[64 * x : 64 * x + 64]
            halves = [v[:, :128], v[:, 128:]]
            for h in range(2):
                ok = True if h != g else (gy > 0) if g == 0 else (gy < ny - 1)
                if x < 2:
                    ok = ok & (gx > 0)
                if x > 5:
                    ok = ok & (gx < nx - 1)
                if ok is not True:
                    halves[h] = jnp.where(ok, halves[h], jnp.zeros_like(halves[h]))
            rows.append([v.astype(BF) for v in halves])
        e2.append(rows)
        for x in range(4):
            a0, a1 = [rows[2 * x][h].astype(F32) + rows[2 * x + 1][h].astype(F32) for h in range(2)]
            a = jnp.where(low, a0 + pltpu.roll(a0, 64, 1), a1 + pltpu.roll(a1, 64, 1))
            pairs.append(((a + pltpu.roll(a, 63, 0)) * 0.125).astype(BF))
    pick32 = ones_where(iota((32, 64), 1) == 2 * iota((32, 64), 0))
    t = nn(pick32, cat(pairs, 1)).astype(BF)
    p2 = [cat([t[:, 128 * x : 128 * x + 128], t[:, 512 + 128 * x : 512 + 128 * x + 128]], 1) for x in range(4)]

    lhs = cat([cat([p2[x + i] for i in range(3)], 1) for x in range(2)], 0)
    t = nn(lhs, k3[...])
    e3 = gelu(t[:, 256:512] + shifted(t[:, :256], 1, 0, 32) + shifted(t[:, 512:], -1, 0, 32)).astype(BF)
    f = e3.astype(F32)
    a = f[:32] + f[32:]
    a = a[:, :128] + a[:, 128:]
    a = (a + pltpu.roll(a, 31, 0)) * 0.125
    pick16 = ones_where(iota((16, 32), 1) == 2 * iota((16, 32), 0))
    p3[2, gy + 2] = nn(pick16, a.astype(BF)).astype(BF)
    x4 = []
    for n, (dx, dy) in enumerate(window):
        x4.append(send(n, dx, dy, p3.at[2, gy + 2], p3.at[2 - dx, gy + 2], s4, r4))
    start(x4)
    for x in range(2):
        for y in range(2):
            e3e[x + 1, y + 1] = e3[32 * x : 32 * x + 32, 128 * y : 128 * y + 128]
    def cells(ref, n_local, ss, rs):
        copies = []
        for n, (dx, dy) in enumerate(DIRS):
            sx, tx, cx = side(dx, n_local)
            sy, ty, cy = side(dy, n_local)
            copies.append(
                send(n, dx, dy, ref.at[pl.ds(sx, cx), pl.ds(sy, cy)], ref.at[pl.ds(tx, cx), pl.ds(ty, cy)], ss, rs)
            )
        return copies

    xe3 = cells(e3e, 2, se3, re3)
    start(xe3)

    low32 = iota((32, 128), 1) < 64
    rr, cc = iota((64, 64), 0), iota((64, 64), 1)
    split = ones_where(cc == 2 * (rr % 32) + rr // 32)
    for x in range(6):
        t = nn(split, cat([e2[g][x + 1][h] for g in range(2) for h in range(2)], 1))
        for y in range(6):
            n = 128 * ((y + 1) // 2)
            ev, od = t[:32, n : n + 128], t[32:, n : n + 128]
            if y % 2 == 1:
                cell = jnp.where(low32, ev, pltpu.roll(od, 64, 1))
            else:
                cell = jnp.where(low32, pltpu.roll(ev, 64, 1), od)
            e2e[x, y] = cell.astype(BF)

    for c in got_w4:
        c.wait()
    for n, (dx, dy) in enumerate(window):
        pltpu.make_async_remote_copy(
            src_ref=p3.at[2, gy + 2], dst_ref=p3.at[2 - dx, lax.rem(gy - dy + ny, ny) + 2],
            send_sem=s4.at[n], recv_sem=r4.at[n], device_id=target(dx, dy), device_id_type=MESH,
        ).wait_recv()

    cell = []
    for x in range(5):
        inside = (gx + (x - 2) >= 0) & (gx + (x - 2) < nx)
        line = []
        for y in range(5):
            v = p3[x, gy + y]
            line.append(jnp.where(inside, v, jnp.zeros_like(v)))
        cell.append(line)
    lhs = cat(
        [
            cat([cell[x + i][y + j] for i in range(3) for j in range(3)], 1)
            for x in range(3)
            for y in range(3)
        ],
        0,
    )
    t = nt(k4[...], lhs)
    e4 = gelu(t[256:512] + shifted(t[:256], 1, 1, 16) + shifted(t[512:], -1, 1, 16))
    n = iota((256, 144), 1) // 16
    x, y = gx - 1 + n // 3, gy - 1 + n % 3
    e4 = jnp.where((x >= 0) & (x < nx) & (y >= 0) & (y < ny), e4, 0.0).astype(BF)

    def inside(x, y, width, n_local):
        ok = True
        if x == 0:
            ok = gx > 0
        if x == n_local + 1:
            ok = gx < nx - 1
        if y == 0:
            ok = ok & (gy > 0)
        if y == n_local + 1:
            ok = ok & (gy < ny - 1)
        return ok

    def kept(v, ok):
        return v if ok is True else jnp.where(ok, v, jnp.zeros_like(v))


    for c in got_v3:
        c.wait()
    up = nt(ones_where(iota((288, 144), 1) == iota((288, 144), 0) // 2), e4).astype(BF)
    at = ((0, 0, 1), (0, 1, 1), (1, 1, 2), (1, 2, 2))
    for x in range(4):
        for y in range(4):
            for i in range(3):
                for j in range(3):
                    n = 3 * at[x][i] + at[y][j]
                    pd3[pl.ds(128 * x + 32 * y, 32), pl.ds(256 * (3 * i + j), 256)] = up[32 * n : 32 * n + 32]
    t = nt(pd3[...], kd3[...])
    v = gelu(t[:, 128:256] + shifted(t[:, :128], 1, 0, 32) + shifted(t[:, 256:], -1, 0, 32))
    arrive(xe3)
    for x in range(4):
        for y in range(4):
            n = 128 * x + 32 * y
            w = v[n : n + 32] + e3e[x, y].astype(F32)
            d3e[x, y] = kept(w, inside(x, y, 32, 2)).astype(BF)

    lane = iota((288, 128), 1) < 64
    lhs = cat(
        [
            cat([d3e[k, m], d3e[k, m + 1], d3e[k + 1, m], d3e[k + 1, m + 1]], 1)
            for k in range(3)
            for m in range(3)
        ],
        0,
    )
    t = nt(lhs, g2[...])
    for px in range(2):
        for py in range(2):
            n = 256 * (2 * px + py)
            a, b = t[:, n : n + 128], t[:, n + 128 : n + 256]
            v = gelu(b + jnp.where(lane, shifted(a, 1, 0, 32), shifted(a, -1, 0, 32)))
            for k in range(3):
                for m in range(3):
                    x, y = 2 * k + 1 - px, 2 * m + 1 - py
                    w = v[96 * k + 32 * m : 96 * k + 32 * m + 32] + e2e[x, y].astype(F32)
                    d2e[x, y] = kept(w, inside(x, y, 32, 4))

    rr, cc = iota((128, 64), 0), iota((128, 64), 1)
    spread = ones_where((rr // 4 == cc % 32) & (rr // 2 % 2 == cc // 32))
    for x in range(6):
        line = []
        for m in range(5):
            a, b = d2e[x, m], d2e[x, m + 1]
            top = jnp.where(low32, a, pltpu.roll(b, 64, 1))
            bottom = jnp.where(low32, pltpu.roll(a, 64, 1), b)
            line.append(cat([top, bottom], 0).astype(BF))
        a = nn(spread, cat(line, 1)).astype(BF)
        for m in range(5):
            q[x, m] = a[:, 128 * m : 128 * m + 128]

    for k in range(5):
        for ms in ((0, 1), (2, 3), (4,)):
            t = nt(g1[...], cat([cat([q[k, m], q[k + 1, m]], 1) for m in ms], 0))
            for px in range(2):
                for py in range(2):
                    for h, m in enumerate(ms):
                        a, b = k - px, m - py
                        if not (0 <= a < 4 and 0 <= b < 4):
                            continue
                        x, y = 2 * a + px, 2 * b + py
                        n = 96 * (2 * px + py)
                        u = t[n : n + 96, 128 * h : 128 * h + 128]
                        v = gelu(u[32:64] + shifted(u[:32], 1, 1, 128) + shifted(u[64:], -1, 1, 128))
                        v = v + e1[x, pl.ds(32 * y, 32), :].astype(F32)
                        out[x, y] = v.astype(BF)
    for copies in (x1, x2, x4, xe3):
        for c in copies:
            c.wait_send()


def local(features, w_enc1, w_enc2, w_enc3, w_enc4, w_dec3, w_dec2, w_dec1):
    w_enc2, w_enc3 = jnp.swapaxes(w_enc2, 1, 2), jnp.swapaxes(w_enc3, 1, 2)
    w_enc4, w_dec3 = w_enc4.reshape(9, 768, 128), w_dec3.reshape(9, 384, 256)
    args = (features, w_enc1, w_enc2, w_enc3, w_enc4, w_dec3, w_dec2, w_dec1)
    ny = lax.axis_size("gy")
    far = 5 * ny - 1
    dma = pltpu.SemaphoreType.DMA
    scratch = [pltpu.VMEM(a.shape, BF) for a in (features, w_enc1, w_enc2, w_enc3, w_dec2, w_dec1)]
    for shape in (
        (10, 320, 128), (8, 256, 128),
        (3, 10, 64, 128),
        (5, ny + 4, 16, 128), (6, 6, 32, 128), (4, 4, 32, 128),
        (192, 384), (768, 768), (768, 768), (768, 1152), (384, 2304), (1024, 512), (384, 256),
        (512, 2304), (4, 4, 32, 128),
    ):
        scratch.append(pltpu.VMEM(shape, BF))
    scratch.append(pltpu.VMEM((6, 6, 32, 128), F32))
    scratch.append(pltpu.VMEM((6, 5, 128, 128), BF))
    scratch.append(dma((24,)))
    for n in (8, 8, far, 8):
        scratch += [dma((n,)), dma((n,))]
    decoded = pl.pallas_call(
        kernel,
        out_shape=pltpu.VMEM((8, 8, 32, 128), BF),
        in_specs=[pl.BlockSpec(memory_space=pl.ANY)] * 8,
        out_specs=pl.BlockSpec(memory_space=pltpu.VMEM),
        scratch_shapes=scratch,
        compiler_params=pltpu.CompilerParams(
            collective_id=0, has_side_effects=True, vmem_limit_bytes=48 * 1024 * 1024
        ),
        cost_estimate=pl.CostEstimate(flops=2 * 1115000000, bytes_accessed=7000000, transcendentals=1000000),
    )(*[pltpu.with_memory_space_constraint(a, pltpu.HBM) for a in args])
    return jnp.transpose(decoded, (2, 0, 1, 3))


def solution(mesh):
    return jax.shard_map(
        local,
        mesh=mesh,
        in_specs=(P(None, "gx", "gy", None), P(), P(), P(), P(), P(), P(), P()),
        out_specs=P(None, "gx", "gy", None),
        check_vma=False,
    )
```

```python
import functools

import jax
import jax.numpy as jnp
from jax import lax
from jax.experimental import pallas as pl
from jax.experimental.pallas import tpu as pltpu
from jax.sharding import PartitionSpec as P

BF = jnp.bfloat16
F32 = jnp.float32
MESH = pl.DeviceIdType.MESH
DIRS = [(-1, -1), (-1, 1), (1, -1), (1, 1), (-1, 0), (1, 0), (0, -1), (0, 1)]
TAPS = (((0,), (1, 2)), ((0, 1), (2,)))


def nn(a, b):
    return lax.dot_general(a, b, (((1,), (0,)), ((), ())), preferred_element_type=F32)


def nt(a, b):
    return lax.dot_general(a, b, (((1,), (1,)), ((), ())), preferred_element_type=F32)


def iota(shape, dim):
    return lax.broadcasted_iota(jnp.int32, shape, dim)


def ones_where(mask):
    return jnp.where(mask, 1.0, 0.0).astype(BF)


def gelu(x):
    half = 0.5 * x
    return half + half * jnp.tanh(x * (0.7978845608028654 + 0.035677408136300125 * (x * x)))


def shifted(v, step, axis, period):
    n = v.shape[axis]
    place = iota(v.shape, axis) % period
    edge = 0 if step == 1 else period - 1
    return jnp.where(place == edge, 0.0, pltpu.roll(v, step % n, axis))


def cat(parts, axis):
    return parts[0] if len(parts) == 1 else jnp.concatenate(parts, axis=axis)


def side(d, n, width=1, pad=1):
    if d == 1:
        return (pad + (n - 1)) * width, 0, width
    if d == -1:
        return pad * width, (n + pad) * width, width
    return pad * width, pad * width, n * width


def kernel(
    feat, w1h, w2h, w3h, w4h, v3h, v2h, v1h, out,
    fv, w1, w2, w3, v2, v1,
    fext, e1, p1, p3, e2e, e3e,
    k1, k2, k3, k4, kd3, g2, g1, pd3, g3, d3e, d2e, q,
    lsem, s1, r1, s2, r2, sp, rp, s4, r4, se3, re3,
):
    gx, gy = lax.axis_index("gx"), lax.axis_index("gy")
    nx, ny = lax.axis_size("gx"), lax.axis_size("gy")

    loads = []

    def load(src, dst):
        c = pltpu.make_async_copy(src, dst, lsem.at[len(loads)])
        c.start()
        loads.append(c)
        return c

    def target(dx, dy):
        return (lax.rem(gx + dx + nx, nx), lax.rem(gy + dy + ny, ny))

    barrier = pltpu.get_barrier_semaphore()
    got_feat = load(feat, fv)
    for dx, dy in DIRS:
        pl.semaphore_signal(barrier, inc=1, device_id=target(dx, dy), device_id_type=MESH)
    got_w1, got_w2, got_w3 = load(w1h, w1), load(w2h, w2), load(w3h, w3)
    got_v2, got_v1 = load(v2h, v2), load(v1h, v1)
    got_w4 = [load(w4h.at[n], k4.at[:, pl.ds(128 * n, 128)]) for n in range(9)]
    got_v3 = [load(v3h.at[n], kd3.at[:, pl.ds(256 * n, 256)]) for n in range(9)]

    def far(d):
        return abs(d[0]) + min(d[1], ny - d[1])

    window = [(dx, dy) for dx in range(-2, 3) for dy in range(ny) if (dx, dy) != (0, 0)]
    window.sort(key=far, reverse=True)

    def send(n, dx, dy, src, dst, ss, rs):
        return pltpu.make_async_remote_copy(
            src_ref=src, dst_ref=dst, send_sem=ss.at[n], recv_sem=rs.at[n],
            device_id=target(dx, dy), device_id_type=MESH,
        )

    def start(copies):
        for c in copies:
            c.start()

    def arrive(copies):
        for c in copies:
            c.wait_recv()

    got_feat.wait()
    r, c = iota((256, 256), 0), iota((256, 256), 1)
    perm = ones_where((r // 32 == c % 8) & (r % 32 == c // 8))

    def place(x, carry):
        a = fv[:, pl.ds(2 * x, 1)].astype(F32).reshape(256, 128).astype(BF)
        b = fv[:, pl.ds(2 * x + 1, 1)].astype(F32).reshape(256, 128).astype(BF)
        t = nn(perm, cat([a, b], 1)).astype(BF)
        fext[2 * x + 1, pl.ds(32, 256), :] = t[:, :128]
        fext[2 * x + 2, pl.ds(32, 256), :] = t[:, 128:]
        return carry

    lax.fori_loop(0, 4, place, 0)
    for n in range(4):
        p3[:, n if n < 2 else n + 4] = jnp.zeros((5, 16, 128), BF)
    pl.semaphore_wait(barrier, len(DIRS))

    x1 = []
    for n, (dx, dy) in enumerate(DIRS):
        sx, tx, cx = side(dx, 8)
        sy, ty, cy = side(dy, 8, 32)
        x1.append(
            send(n, dx, dy, fext.at[pl.ds(sx, cx), pl.ds(sy, cy)], fext.at[pl.ds(tx, cx), pl.ds(ty, cy)], s1, r1)
        )
    start(x1)

    got_w1.wait()
    t = None
    r, c = iota((32, 256), 0), iota((32, 256), 1)
    for j in range(3):
        taps = cat([w1[pl.ds(9 * i + 3 * j, 3)].reshape(96, 32) for i in range(3)], 0)
        u = nn(taps, ones_where((r == c % 32) & (c // 32 % 4 == c // 128 + j)))
        t = u if t is None else t + u
    t = t.astype(BF)
    for i in range(3):
        for l in range(3):
            for yo in range(2):
                k1[pl.ds(64 * l + 32 * yo, 32), pl.ds(128 * i, 128)] = t[
                    96 * i + 32 * l : 96 * i + 32 * l + 32, 128 * yo : 128 * yo + 128
                ]

    def enc1(xa, xb, b):
        rhs = cat(
            [cat([fext[xa + i, pl.ds(64 * b, 128), :], fext[xb + i, pl.ds(64 * b, 128), :]], 1) for i in range(3)],
            0,
        )
        t = nn(k1[...], rhs)
        for h, x in enumerate((xa, xb)):
            u = t[:, 128 * h : 128 * (h + 1)]
            v = u[64:128] + shifted(u[:64], 1, 1, 128) + shifted(u[128:], -1, 1, 128)
            e1[x, pl.ds(64 * b, 64), :] = gelu(v).astype(BF)

    def enc1_inner(n, carry, blocks):
        for b in blocks:
            enc1(2 * n + 1, 2 * n + 2, b)
        return carry

    lax.fori_loop(0, 3, functools.partial(enc1_inner, blocks=(1, 2)), 0)

    got_w2.wait()
    r, c = iota((64, 256), 0), iota((64, 256), 1)
    spots = [ones_where(c == r + 64 * yo) for yo in range(4)]
    taps = [cat([w2[pl.ds(9 * i + 3 * j, 3)].reshape(96, 64) for i in range(3)], 0) for j in range(3)]
    for yi in range(1, 7):
        t = None
        for j in range(3):
            if 0 <= yi - 1 - j < 4:
                u = nn(taps[j], spots[yi - 1 - j])
                t = u if t is None else t + u
        t = t.astype(BF)
        for i in range(3):
            for l in range(3):
                k2[pl.ds(256 * i + 32 * yi, 32), pl.ds(256 * l, 256)] = t[96 * i + 32 * l : 96 * i + 32 * l + 32]
    for i in range(3):
        for yi in (0, 7):
            k2[pl.ds(256 * i + 32 * yi, 32), :] = jnp.zeros((32, 768), BF)
    got_w3.wait()
    z128 = jnp.zeros((64, 128), BF)
    for i in range(3):
        for yi in range(4):
            for l in range(3):
                for yo in range(2):
                    j = yi - yo
                    k3[pl.ds(256 * i + 64 * yi, 64), pl.ds(256 * l + 128 * yo, 128)] = (
                        w3[9 * i + 3 * j + l] if 0 <= j < 3 else z128
                    )

    arrive(x1[6:])

    @pl.when(gy == 0)
    def _():
        fext[pl.ds(1, 8), pl.ds(0, 32)] = jnp.zeros((8, 32, 128), BF)

    @pl.when(gy == ny - 1)
    def _():
        fext[pl.ds(1, 8), pl.ds(288, 32)] = jnp.zeros((8, 32, 128), BF)

    lax.fori_loop(0, 3, functools.partial(enc1_inner, blocks=(0, 3)), 0)

    def pool1(x):
        a = e1[2 * x].astype(F32) + e1[2 * x + 1].astype(F32)
        a = cat([a[64 * b : 64 * b + 32] + a[64 * b + 32 : 64 * b + 64] for b in range(4)], 0)
        a = (a + pltpu.roll(a, 127, 1)) * 0.125
        return a.astype(BF)

    pick64 = ones_where(iota((64, 128), 1) == 2 * iota((64, 128), 0))
    pooled = [None, pool1(1), pool1(2), None]
    arrive(x1[4:6])

    @pl.when(gx == 0)
    def _():
        fext[0, pl.ds(32, 256)] = jnp.zeros((256, 128), BF)

    @pl.when(gx == nx - 1)
    def _():
        fext[9, pl.ds(32, 256)] = jnp.zeros((256, 128), BF)

    enc1(0, 7, 1)
    enc1(0, 7, 2)
    arrive(x1[:4])

    @pl.when((gx == 0) | (gy == 0))
    def _():
        fext[0, pl.ds(0, 32)] = jnp.zeros((32, 128), BF)

    @pl.when((gx == 0) | (gy == ny - 1))
    def _():
        fext[0, pl.ds(288, 32)] = jnp.zeros((32, 128), BF)

    @pl.when((gx == nx - 1) | (gy == 0))
    def _():
        fext[9, pl.ds(0, 32)] = jnp.zeros((32, 128), BF)

    @pl.when((gx == nx - 1) | (gy == ny - 1))
    def _():
        fext[9, pl.ds(288, 32)] = jnp.zeros((32, 128), BF)

    enc1(0, 7, 0)
    enc1(0, 7, 3)
    pooled[0], pooled[3] = pool1(0), pool1(3)

    t = nt(pick64, cat(pooled, 0)).astype(BF)
    for x in range(4):
        p1[1, x + 3] = t[:, 128 * x : 128 * x + 128]
    odd = lax.rem(gx, 2)
    mate = 1 - 2 * odd
    x2 = []
    for n, dy in enumerate((-1, 1)):
        x2.append(send(n, -mate, dy, p1.at[1, pl.ds(3 + odd, 3)], p1.at[1 - dy, pl.ds(7 - 7 * odd, 3)], s2, r2))
    for n, dy in enumerate((-1, 1)):
        x2.append(send(2 + n, 0, dy, p1.at[1, pl.ds(3, 4)], p1.at[1 - dy, pl.ds(3, 4)], s2, r2))
    x2.append(send(4, -1, 0, p1.at[1, pl.ds(3, 3)], p1.at[1, pl.ds(7, 3)], s2, r2))
    x2.append(send(5, 1, 0, p1.at[1, pl.ds(4, 3)], p1.at[1, pl.ds(0, 3)], s2, r2))
    start(x2)

    got_v2.wait()
    for px in range(2):
        for py in range(2):
            for tx in range(2):
                for ty in range(2):
                    s = []
                    for l in range(3):
                        terms = [
                            v2[9 * i + 3 * j + l].astype(F32) for i in TAPS[px][tx] for j in TAPS[py][ty]
                        ]
                        s.append(functools.reduce(jnp.add, terms))
                    block = cat([s[0], s[2], s[1] + s[2], s[0] + s[1]], 0).astype(BF)
                    g2[pl.ds(256 * (2 * px + py), 256), pl.ds(128 * (2 * tx + ty), 128)] = block
    got_v1.wait()
    for px in range(2):
        for py in range(2):
            for l in range(3):
                row = []
                for tx in range(2):
                    for ty in range(2):
                        terms = [
                            v1[9 * i + 3 * j + l].astype(F32) for i in TAPS[px][tx] for j in TAPS[py][ty]
                        ]
                        row.append(functools.reduce(jnp.add, terms).astype(BF))
                g1[pl.ds(96 * (2 * px + py) + 32 * l, 32), :] = cat(row, 1)

    for c in got_v3:
        c.wait()

    def sum_taps(n, carry):
        rows = pl.ds(pl.multiple_of(32 * n, 32), 32)
        lower = pl.ds(pl.multiple_of(384 + 32 * n, 32), 32)
        taps = [kd3[rows, 768 * i : 768 * i + 768] for i in range(3)]
        g3[rows, :768] = taps[0]
        g3[rows, 768:] = (taps[1].astype(F32) + taps[2].astype(F32)).astype(BF)
        g3[lower, :768] = (taps[0].astype(F32) + taps[1].astype(F32)).astype(BF)
        g3[lower, 768:] = taps[2]
        return carry

    lax.fori_loop(0, 12, sum_taps, 0)

    arrive(x2[2:4])

    @pl.when(gy == 0)
    def _():
        p1[0, pl.ds(3, 4)] = jnp.zeros((4, 64, 128), BF)

    @pl.when(gy == ny - 1)
    def _():
        p1[2, pl.ds(3, 4)] = jnp.zeros((4, 64, 128), BF)

    passed = []
    for n, dy in enumerate((-1, 1)):
        passed.append(
            send(n, mate, 0, p1.at[1 - dy, pl.ds(4 - odd, 3)], p1.at[1 - dy, pl.ds(7 * odd, 3)], sp, rp)
        )
    start(passed)

    low = iota((64, 128), 1) < 64
    e2 = [[None] * 8, [None] * 8]

    def enc2(xs):
        for g in range(2):
            lhs = cat(
                [cat([cat([p1[g, x + i], p1[g + 1, x + i]], 1) for i in range(3)], 1) for x in xs], 0
            )
            t = nn(lhs, k2[...])
            t = gelu(t[:, 256:512] + shifted(t[:, :256], 1, 0, 64) + shifted(t[:, 512:], -1, 0, 64))
            for n, x in enumerate(xs):
                v = t[64 * n : 64 * n + 64]
                halves = [v[:, :128], v[:, 128:]]
                for h in range(2):
                    ok = True if h != g else (gy > 0) if g == 0 else (gy < ny - 1)
                    if x < 2:
                        ok = ok & (gx > 0)
                    if x > 5:
                        ok = ok & (gx < nx - 1)
                    if ok is not True:
                        halves[h] = jnp.where(ok, halves[h], jnp.zeros_like(halves[h]))
                e2[g][x] = [v.astype(BF) for v in halves]

    enc2((3, 4))
    arrive(x2[:2])
    arrive(x2[4:])
    for n, dy in enumerate((-1, 1)):
        send(n, mate, 0, p1.at[1 - dy, pl.ds(3 + odd, 3)], p1.at[1 - dy, pl.ds(7 - 7 * odd, 3)], sp, rp).wait_recv()

    @pl.when(gx == 0)
    def _():
        p1[:, pl.ds(0, 3)] = jnp.zeros((3, 3, 64, 128), BF)

    @pl.when(gx == nx - 1)
    def _():
        p1[:, pl.ds(7, 3)] = jnp.zeros((3, 3, 64, 128), BF)

    @pl.when(gy == 0)
    def _():
        for x in (0, 7):
            p1[0, pl.ds(x, 3)] = jnp.zeros((3, 64, 128), BF)

    @pl.when(gy == ny - 1)
    def _():
        for x in (0, 7):
            p1[2, pl.ds(x, 3)] = jnp.zeros((3, 64, 128), BF)

    enc2((0, 1, 2, 5, 6, 7))
    pairs = []
    for g in range(2):
        for x in range(4):
            a0, a1 = [e2[g][2 * x][h].astype(F32) + e2[g][2 * x + 1][h].astype(F32) for h in range(2)]
            a = jnp.where(low, a0 + pltpu.roll(a0, 64, 1), a1 + pltpu.roll(a1, 64, 1))
            pairs.append(((a + pltpu.roll(a, 63, 0)) * 0.125).astype(BF))
    pick32 = ones_where(iota((32, 64), 1) == 2 * iota((32, 64), 0))
    t = nn(pick32, cat(pairs, 1)).astype(BF)
    p2 = [cat([t[:, 128 * x : 128 * x + 128], t[:, 512 + 128 * x : 512 + 128 * x + 128]], 1) for x in range(4)]

    lhs = cat([cat([p2[x + i] for i in range(3)], 1) for x in range(2)], 0)
    t = nn(lhs, k3[...])
    e3 = gelu(t[:, 256:512] + shifted(t[:, :256], 1, 0, 32) + shifted(t[:, 512:], -1, 0, 32)).astype(BF)
    f = e3.astype(F32)
    a = f[:32] + f[32:]
    a = a[:, :128] + a[:, 128:]
    a = (a + pltpu.roll(a, 31, 0)) * 0.125
    pick16 = ones_where(iota((16, 32), 1) == 2 * iota((16, 32), 0))
    p3[2, gy + 2] = nn(pick16, a.astype(BF)).astype(BF)
    x4 = []
    for n, (dx, dy) in enumerate(window):
        x4.append(send(n, dx, dy, p3.at[2, gy + 2], p3.at[2 - dx, gy + 2], s4, r4))
    start(x4)
    for x in range(2):
        for y in range(2):
            e3e[x + 1, y + 1] = e3[32 * x : 32 * x + 32, 128 * y : 128 * y + 128]
    def cells(ref, n_local, ss, rs):
        copies = []
        for n, (dx, dy) in enumerate(DIRS):
            sx, tx, cx = side(dx, n_local)
            sy, ty, cy = side(dy, n_local)
            copies.append(
                send(n, dx, dy, ref.at[pl.ds(sx, cx), pl.ds(sy, cy)], ref.at[pl.ds(tx, cx), pl.ds(ty, cy)], ss, rs)
            )
        return copies

    xe3 = cells(e3e, 2, se3, re3)
    start(xe3)

    low32 = iota((32, 128), 1) < 64
    rr, cc = iota((64, 64), 0), iota((64, 64), 1)
    split = ones_where(cc == 2 * (rr % 32) + rr // 32)
    for x in range(6):
        t = nn(split, cat([e2[g][x + 1][h] for g in range(2) for h in range(2)], 1))
        for y in range(6):
            n = 128 * ((y + 1) // 2)
            ev, od = t[:32, n : n + 128], t[32:, n : n + 128]
            if y % 2 == 1:
                cell = jnp.where(low32, ev, pltpu.roll(od, 64, 1))
            else:
                cell = jnp.where(low32, pltpu.roll(ev, 64, 1), od)
            e2e[x, y] = cell.astype(BF)

    for c in got_w4:
        c.wait()
    for n, (dx, dy) in enumerate(window):
        pltpu.make_async_remote_copy(
            src_ref=p3.at[2, gy + 2], dst_ref=p3.at[2 - dx, lax.rem(gy - dy + ny, ny) + 2],
            send_sem=s4.at[n], recv_sem=r4.at[n], device_id=target(dx, dy), device_id_type=MESH,
        ).wait_recv()

    cell = []
    for x in range(5):
        inside = (gx + (x - 2) >= 0) & (gx + (x - 2) < nx)
        line = []
        for y in range(5):
            v = p3[x, gy + y]
            line.append(jnp.where(inside, v, jnp.zeros_like(v)))
        cell.append(line)
    lhs = cat(
        [
            cat([cell[x + i][y + j] for i in range(3) for j in range(3)], 1)
            for x in range(3)
            for y in range(3)
        ],
        0,
    )
    t = nt(lhs, k4[...])
    e4 = gelu(t[:, 256:512] + shifted(t[:, :256], 1, 0, 16) + shifted(t[:, 512:], -1, 0, 16))

    def inside(x, y, width, n_local):
        ok = True
        if x == 0:
            ok = gx > 0
        if x == n_local + 1:
            ok = gx < nx - 1
        if y == 0:
            ok = ok & (gy > 0)
        if y == n_local + 1:
            ok = ok & (gy < ny - 1)
        return ok

    def kept(v, ok):
        return v if ok is True else jnp.where(ok, v, jnp.zeros_like(v))


    e4 = [kept(e4[16 * n : 16 * n + 16], inside(n // 3, n % 3, 16, 1)).astype(BF) for n in range(9)]
    twice = ones_where(iota((32, 16), 1) == iota((32, 16), 0) // 2)
    up = nn(twice, cat(e4, 1)).astype(BF)
    at = ((0, 0, 1), (0, 1, 1), (1, 1, 2), (1, 2, 2))
    for k in range(2):
        for y in range(4):
            for tx in range(2):
                for j in range(3):
                    n = 3 * (k + tx) + at[y][j]
                    pd3[pl.ds(128 * k + 32 * y, 32), pl.ds(256 * (3 * tx + j), 256)] = up[:, 256 * n : 256 * n + 256]
    t = nt(pd3[...], g3[...])
    arrive(xe3)
    for px in range(2):
        u = t[:, 384 * px : 384 * px + 384]
        v = gelu(u[:, 128:256] + shifted(u[:, :128], 1, 0, 32) + shifted(u[:, 256:], -1, 0, 32))
        for k in range(2):
            for y in range(4):
                x, n = 2 * k + 1 - px, 128 * k + 32 * y
                w = v[n : n + 32] + e3e[x, y].astype(F32)
                d3e[x, y] = kept(w, inside(x, y, 32, 2)).astype(BF)

    lane = iota((288, 128), 1) < 64
    lhs = cat(
        [
            cat([d3e[k, m], d3e[k, m + 1], d3e[k + 1, m], d3e[k + 1, m + 1]], 1)
            for k in range(3)
            for m in range(3)
        ],
        0,
    )
    t = nt(lhs, g2[...])
    for px in range(2):
        for py in range(2):
            n = 256 * (2 * px + py)
            a, b = t[:, n : n + 128], t[:, n + 128 : n + 256]
            v = gelu(b + jnp.where(lane, shifted(a, 1, 0, 32), shifted(a, -1, 0, 32)))
            for k in range(3):
                for m in range(3):
                    x, y = 2 * k + 1 - px, 2 * m + 1 - py
                    w = v[96 * k + 32 * m : 96 * k + 32 * m + 32] + e2e[x, y].astype(F32)
                    d2e[x, y] = kept(w, inside(x, y, 32, 4))

    rr, cc = iota((128, 64), 0), iota((128, 64), 1)
    spread = ones_where((rr // 4 == cc % 32) & (rr // 2 % 2 == cc // 32))
    for x in range(6):
        line = []
        as_is = [d2e[x, m] for m in range(6)]
        turned = [pltpu.roll(v, 64, 1) for v in as_is]
        for m in range(5):
            top = jnp.where(low32, as_is[m], turned[m + 1])
            bottom = jnp.where(low32, turned[m], as_is[m + 1])
            line.append(cat([top, bottom], 0).astype(BF))
        a = nn(spread, cat(line, 1)).astype(BF)
        for m in range(5):
            q[x, m] = a[:, 128 * m : 128 * m + 128]

    both = ((0, 0), (0, 1), (1, 0), (1, 1))
    groups = []
    for parities, windows in (
        ([c for c in both if c[0] == 0], [(0, m) for m in range(5)]),
        ([c for c in both if c[1] == 0], [(k, 0) for k in range(1, 4)]),
        (both, [(k, m) for k in range(1, 4) for m in range(1, 4)]),
        ([c for c in both if c[1] == 1], [(k, 4) for k in range(1, 4)]),
        ([c for c in both if c[0] == 1], [(4, m) for m in range(5)]),
    ):
        for n in range(0, len(windows), 2):
            groups.append((parities, windows[n : n + 2]))
    for parities, windows in groups:
        lhs = cat([g1[pl.ds(96 * (2 * px + py), 96), :] for px, py in parities], 0)
        t = nt(lhs, cat([cat([q[k, m], q[k + 1, m]], 1) for k, m in windows], 0))
        for n, (px, py) in enumerate(parities):
            for h, (k, m) in enumerate(windows):
                a, b = k - px, m - py
                if not (0 <= a < 4 and 0 <= b < 4):
                    continue
                x, y = 2 * a + px, 2 * b + py
                u = t[96 * n : 96 * n + 96, 128 * h : 128 * h + 128]
                v = gelu(u[32:64] + shifted(u[:32], 1, 1, 128) + shifted(u[64:], -1, 1, 128))
                v = v + e1[x, pl.ds(32 * y, 32), :].astype(F32)
                out[x, y] = v.astype(BF)

    for copies in (x1, x2, passed, x4, xe3):
        for c in copies:
            c.wait_send()


def local(features, w_enc1, w_enc2, w_enc3, w_enc4, w_dec3, w_dec2, w_dec1):
    w_enc2, w_enc3 = jnp.swapaxes(w_enc2, 1, 2), jnp.swapaxes(w_enc3, 1, 2)
    w_enc4, w_dec3 = w_enc4.reshape(9, 768, 128), w_dec3.reshape(9, 384, 256)
    args = (features, w_enc1, w_enc2, w_enc3, w_enc4, w_dec3, w_dec2, w_dec1)
    ny = lax.axis_size("gy")
    far = 5 * ny - 1
    dma = pltpu.SemaphoreType.DMA
    scratch = [pltpu.VMEM(a.shape, BF) for a in (features, w_enc1, w_enc2, w_enc3, w_dec2, w_dec1)]
    for shape in (
        (10, 320, 128), (8, 256, 128),
        (3, 10, 64, 128),
        (5, ny + 4, 16, 128), (6, 6, 32, 128), (4, 4, 32, 128),
        (192, 384), (768, 768), (768, 768), (768, 1152), (384, 2304), (1024, 512), (384, 256),
        (256, 1536), (768, 1536), (4, 4, 32, 128),
    ):
        scratch.append(pltpu.VMEM(shape, BF))
    scratch.append(pltpu.VMEM((6, 6, 32, 128), F32))
    scratch.append(pltpu.VMEM((6, 5, 128, 128), BF))
    scratch.append(dma((24,)))
    for n in (8, 6, 2, far, 8):
        scratch += [dma((n,)), dma((n,))]
    decoded = pl.pallas_call(
        kernel,
        out_shape=pltpu.VMEM((8, 8, 32, 128), BF),
        in_specs=[pl.BlockSpec(memory_space=pl.ANY)] * 8,
        out_specs=pl.BlockSpec(memory_space=pltpu.VMEM),
        scratch_shapes=scratch,
        compiler_params=pltpu.CompilerParams(
            collective_id=0, has_side_effects=True, vmem_limit_bytes=48 * 1024 * 1024
        ),
        cost_estimate=pl.CostEstimate(flops=2 * 1115000000, bytes_accessed=7000000, transcendentals=1000000),
    )(*[pltpu.with_memory_space_constraint(a, pltpu.HBM) for a in args])
    return jnp.transpose(decoded, (2, 0, 1, 3))


def solution(mesh):
    return jax.shard_map(
        local,
        mesh=mesh,
        in_specs=(P(None, "gx", "gy", None), P(), P(), P(), P(), P(), P(), P()),
        out_specs=P(None, "gx", "gy", None),
        check_vma=False,
    )
```

```python
import functools

import jax
import jax.numpy as jnp
from jax import lax
from jax.experimental import pallas as pl
from jax.experimental.pallas import tpu as pltpu
from jax.sharding import PartitionSpec as P

BF = jnp.bfloat16
F32 = jnp.float32
MESH = pl.DeviceIdType.MESH
DIRS = [(-1, -1), (-1, 1), (1, -1), (1, 1), (-1, 0), (1, 0), (0, -1), (0, 1)]
TAPS = (((0,), (1, 2)), ((0, 1), (2,)))


def nn(a, b):
    return lax.dot_general(a, b, (((1,), (0,)), ((), ())), preferred_element_type=F32)


def nt(a, b):
    return lax.dot_general(a, b, (((1,), (1,)), ((), ())), preferred_element_type=F32)


def iota(shape, dim):
    return lax.broadcasted_iota(jnp.int32, shape, dim)


def ones_where(mask):
    return jnp.where(mask, 1.0, 0.0).astype(BF)


def gelu(x):
    half = 0.5 * x
    return half + half * jnp.tanh(x * (0.7978845608028654 + 0.035677408136300125 * (x * x)))


def shifted(v, step, axis, period):
    n = v.shape[axis]
    place = iota(v.shape, axis) % period
    edge = 0 if step == 1 else period - 1
    return jnp.where(place == edge, 0.0, pltpu.roll(v, step % n, axis))


def cat(parts, axis):
    return parts[0] if len(parts) == 1 else jnp.concatenate(parts, axis=axis)


def side(d, n, width=1, pad=1):
    if d == 1:
        return (pad + (n - 1)) * width, 0, width
    if d == -1:
        return pad * width, (n + pad) * width, width
    return pad * width, pad * width, n * width


def kernel(
    feat, w1h, w2h, w3h, w4h, v3h, v2h, v1h, out,
    fv, w1, w2, w3, v2, v1,
    fext, e1, p1, p3, e2e, e3e,
    k1, k2, k3, k4, kd3, g2, g1, pd3, g3, d3e, d2e, q,
    lsem, s1, r1, s2, r2, sp, rp, s4, r4, se3, re3,
):
    gx, gy = lax.axis_index("gx"), lax.axis_index("gy")
    nx, ny = lax.axis_size("gx"), lax.axis_size("gy")

    loads = []

    def load(src, dst):
        c = pltpu.make_async_copy(src, dst, lsem.at[len(loads)])
        c.start()
        loads.append(c)
        return c

    def target(dx, dy):
        return (lax.rem(gx + dx + nx, nx), lax.rem(gy + dy + ny, ny))

    barrier = pltpu.get_barrier_semaphore()
    got_feat = load(feat, fv)
    for dx, dy in DIRS:
        pl.semaphore_signal(barrier, inc=1, device_id=target(dx, dy), device_id_type=MESH)
    got_w1, got_w2, got_w3 = load(w1h, w1), load(w2h, w2), load(w3h, w3)
    got_v2, got_v1 = load(v2h, v2), load(v1h, v1)
    got_w4 = [load(w4h.at[n], k4.at[:, pl.ds(128 * n, 128)]) for n in range(9)]
    got_v3 = [load(v3h.at[n], kd3.at[:, pl.ds(256 * n, 256)]) for n in range(9)]

    def far(d):
        return abs(d[0]) + min(d[1], ny - d[1])

    window = [(dx, dy) for dx in range(-2, 3) for dy in range(ny) if (dx, dy) != (0, 0)]
    window.sort(key=far, reverse=True)

    def send(n, dx, dy, src, dst, ss, rs):
        return pltpu.make_async_remote_copy(
            src_ref=src, dst_ref=dst, send_sem=ss.at[n], recv_sem=rs.at[n],
            device_id=target(dx, dy), device_id_type=MESH,
        )

    def start(copies):
        for c in copies:
            c.start()

    def arrive(copies):
        for c in copies:
            c.wait_recv()

    got_feat.wait()
    r, c = iota((256, 256), 0), iota((256, 256), 1)
    perm = ones_where((r // 32 == c % 8) & (r % 32 == c // 8))

    def place(x, carry):
        a = fv[:, pl.ds(2 * x, 1)].astype(F32).reshape(256, 128).astype(BF)
        b = fv[:, pl.ds(2 * x + 1, 1)].astype(F32).reshape(256, 128).astype(BF)
        t = nn(perm, cat([a, b], 1)).astype(BF)
        fext[2 * x + 1, pl.ds(32, 256), :] = t[:, :128]
        fext[2 * x + 2, pl.ds(32, 256), :] = t[:, 128:]
        return carry

    lax.fori_loop(0, 4, place, 0)
    for n in range(4):
        p3[:, n if n < 2 else n + 4] = jnp.zeros((5, 16, 128), BF)
    pl.semaphore_wait(barrier, len(DIRS))

    x1 = []
    for n, (dx, dy) in enumerate(DIRS):
        sx, tx, cx = side(dx, 8)
        sy, ty, cy = side(dy, 8, 32)
        x1.append(
            send(n, dx, dy, fext.at[pl.ds(sx, cx), pl.ds(sy, cy)], fext.at[pl.ds(tx, cx), pl.ds(ty, cy)], s1, r1)
        )
    start(x1)

    got_w1.wait()
    t = None
    r, c = iota((32, 256), 0), iota((32, 256), 1)
    for j in range(3):
        taps = cat([w1[pl.ds(9 * i + 3 * j, 3)].reshape(96, 32) for i in range(3)], 0)
        u = nn(taps, ones_where((r == c % 32) & (c // 32 % 4 == c // 128 + j)))
        t = u if t is None else t + u
    t = t.astype(BF)
    for i in range(3):
        for l in range(3):
            for yo in range(2):
                k1[pl.ds(64 * l + 32 * yo, 32), pl.ds(128 * i, 128)] = t[
                    96 * i + 32 * l : 96 * i + 32 * l + 32, 128 * yo : 128 * yo + 128
                ]

    def enc1(xa, xb, b):
        rhs = cat(
            [cat([fext[xa + i, pl.ds(64 * b, 128), :], fext[xb + i, pl.ds(64 * b, 128), :]], 1) for i in range(3)],
            0,
        )
        t = nn(k1[...], rhs)
        for h, x in enumerate((xa, xb)):
            u = t[:, 128 * h : 128 * (h + 1)]
            v = u[64:128] + shifted(u[:64], 1, 1, 128) + shifted(u[128:], -1, 1, 128)
            e1[x, pl.ds(64 * b, 64), :] = gelu(v).astype(BF)

    def enc1_inner(n, carry, blocks):
        for b in blocks:
            enc1(2 * n + 1, 2 * n + 2, b)
        return carry

    lax.fori_loop(0, 3, functools.partial(enc1_inner, blocks=(1, 2)), 0)

    got_w2.wait()
    r, c = iota((64, 256), 0), iota((64, 256), 1)
    spots = [ones_where(c == r + 64 * yo) for yo in range(4)]
    taps = [cat([w2[pl.ds(9 * i + 3 * j, 3)].reshape(96, 64) for i in range(3)], 0) for j in range(3)]
    for yi in range(1, 7):
        t = None
        for j in range(3):
            if 0 <= yi - 1 - j < 4:
                u = nn(taps[j], spots[yi - 1 - j])
                t = u if t is None else t + u
        t = t.astype(BF)
        for i in range(3):
            for l in range(3):
                k2[pl.ds(256 * i + 32 * yi, 32), pl.ds(256 * l, 256)] = t[96 * i + 32 * l : 96 * i + 32 * l + 32]
    for i in range(3):
        for yi in (0, 7):
            k2[pl.ds(256 * i + 32 * yi, 32), :] = jnp.zeros((32, 768), BF)
    got_w3.wait()
    z128 = jnp.zeros((64, 128), BF)
    for i in range(3):
        for yi in range(4):
            for l in range(3):
                for yo in range(2):
                    j = yi - yo
                    k3[pl.ds(256 * i + 64 * yi, 64), pl.ds(256 * l + 128 * yo, 128)] = (
                        w3[9 * i + 3 * j + l] if 0 <= j < 3 else z128
                    )

    arrive(x1[6:])

    @pl.when(gy == 0)
    def _():
        fext[pl.ds(1, 8), pl.ds(0, 32)] = jnp.zeros((8, 32, 128), BF)

    @pl.when(gy == ny - 1)
    def _():
        fext[pl.ds(1, 8), pl.ds(288, 32)] = jnp.zeros((8, 32, 128), BF)

    lax.fori_loop(0, 3, functools.partial(enc1_inner, blocks=(0, 3)), 0)

    def pool1(x):
        a = e1[2 * x].astype(F32) + e1[2 * x + 1].astype(F32)
        a = cat([a[64 * b : 64 * b + 32] + a[64 * b + 32 : 64 * b + 64] for b in range(4)], 0)
        a = (a + pltpu.roll(a, 127, 1)) * 0.125
        return a.astype(BF)

    pick64 = ones_where(iota((64, 128), 1) == 2 * iota((64, 128), 0))
    t = nt(pick64, cat([pool1(1), pool1(2)], 0)).astype(BF)
    p1[1, 4], p1[1, 5] = t[:, :128], t[:, 128:]

    odd = lax.rem(gx, 2)
    mate = 1 - 2 * odd
    inner = p1.at[1, pl.ds(4, 2)]
    x2 = []
    for n, dy in enumerate((-1, 1)):
        x2.append(send(n, -mate, dy, inner, p1.at[1 - dy, pl.ds(8 - 8 * odd, 2)], s2, r2))
    for n, dy in enumerate((-1, 1)):
        x2.append(send(2 + n, 0, dy, inner, p1.at[1 - dy, pl.ds(4, 2)], s2, r2))
    x2.append(send(4, -1, 0, inner, p1.at[1, pl.ds(8, 2)], s2, r2))
    x2.append(send(5, 1, 0, inner, p1.at[1, pl.ds(0, 2)], s2, r2))
    start(x2)

    arrive(x1[4:6])

    @pl.when(gx == 0)
    def _():
        fext[0, pl.ds(32, 256)] = jnp.zeros((256, 128), BF)

    @pl.when(gx == nx - 1)
    def _():
        fext[9, pl.ds(32, 256)] = jnp.zeros((256, 128), BF)

    enc1(0, 7, 1)
    enc1(0, 7, 2)
    arrive(x1[:4])

    @pl.when((gx == 0) | (gy == 0))
    def _():
        fext[0, pl.ds(0, 32)] = jnp.zeros((32, 128), BF)

    @pl.when((gx == 0) | (gy == ny - 1))
    def _():
        fext[0, pl.ds(288, 32)] = jnp.zeros((32, 128), BF)

    @pl.when((gx == nx - 1) | (gy == 0))
    def _():
        fext[9, pl.ds(0, 32)] = jnp.zeros((32, 128), BF)

    @pl.when((gx == nx - 1) | (gy == ny - 1))
    def _():
        fext[9, pl.ds(288, 32)] = jnp.zeros((32, 128), BF)

    enc1(0, 7, 0)
    enc1(0, 7, 3)
    t = nt(pick64, cat([pool1(0), pool1(3)], 0)).astype(BF)
    p1[1, 3], p1[1, 6] = t[:, :128], t[:, 128:]
    x2b = []
    for n, dy in enumerate((-1, 1)):
        x2b.append(send(6 + n, -mate, dy, p1.at[1, 3 + 3 * odd], p1.at[1 - dy, 7 - 5 * odd], s2, r2))
    for n, (dy, x) in enumerate(((-1, 3), (1, 3), (-1, 6), (1, 6))):
        x2b.append(send(8 + n, 0, dy, p1.at[1, x], p1.at[1 - dy, x], s2, r2))
    x2b.append(send(12, -1, 0, p1.at[1, 3], p1.at[1, 7], s2, r2))
    x2b.append(send(13, 1, 0, p1.at[1, 6], p1.at[1, 2], s2, r2))
    start(x2b)

    got_v2.wait()
    for px in range(2):
        for py in range(2):
            for tx in range(2):
                for ty in range(2):
                    s = []
                    for l in range(3):
                        terms = [
                            v2[9 * i + 3 * j + l].astype(F32) for i in TAPS[px][tx] for j in TAPS[py][ty]
                        ]
                        s.append(functools.reduce(jnp.add, terms))
                    block = cat([s[0], s[2], s[1] + s[2], s[0] + s[1]], 0).astype(BF)
                    g2[pl.ds(256 * (2 * px + py), 256), pl.ds(128 * (2 * tx + ty), 128)] = block
    got_v1.wait()
    for px in range(2):
        for py in range(2):
            for l in range(3):
                row = []
                for tx in range(2):
                    for ty in range(2):
                        terms = [
                            v1[9 * i + 3 * j + l].astype(F32) for i in TAPS[px][tx] for j in TAPS[py][ty]
                        ]
                        row.append(functools.reduce(jnp.add, terms).astype(BF))
                g1[pl.ds(96 * (2 * px + py) + 32 * l, 32), :] = cat(row, 1)

    for c in got_v3:
        c.wait()

    def sum_taps(n, carry):
        rows = pl.ds(pl.multiple_of(32 * n, 32), 32)
        lower = pl.ds(pl.multiple_of(384 + 32 * n, 32), 32)
        taps = [kd3[rows, 768 * i : 768 * i + 768] for i in range(3)]
        g3[rows, :768] = taps[0]
        g3[rows, 768:] = (taps[1].astype(F32) + taps[2].astype(F32)).astype(BF)
        g3[lower, :768] = (taps[0].astype(F32) + taps[1].astype(F32)).astype(BF)
        g3[lower, 768:] = taps[2]
        return carry

    lax.fori_loop(0, 12, sum_taps, 0)

    passed = []
    for part, xs in ((x2[2:4], (4, 5)), (x2b[2:6], (3, 6))):
        arrive(part)

        @pl.when(gy == 0)
        def _():
            for x in xs:
                p1[0, x] = jnp.zeros((64, 128), BF)

        @pl.when(gy == ny - 1)
        def _():
            for x in xs:
                p1[2, x] = jnp.zeros((64, 128), BF)

        new = []
        for n, y in enumerate((2, 0)):
            if xs == (4, 5):
                new.append(send(n, mate, 0, p1.at[y, pl.ds(4, 2)], p1.at[y, pl.ds(8 * odd, 2)], sp, rp))
            else:
                new.append(send(2 + n, mate, 0, p1.at[y, 6 - 3 * odd], p1.at[y, 2 + 5 * odd], sp, rp))
        start(new)
        passed += new

    low = iota((64, 128), 1) < 64
    e2 = [[None] * 8, [None] * 8]

    def enc2(xs):
        for g in range(2):
            lhs = cat(
                [cat([cat([p1[g, x + i], p1[g + 1, x + i]], 1) for i in range(3)], 1) for x in xs], 0
            )
            t = nn(lhs, k2[...])
            t = gelu(t[:, 256:512] + shifted(t[:, :256], 1, 0, 64) + shifted(t[:, 512:], -1, 0, 64))
            for n, x in enumerate(xs):
                v = t[64 * n : 64 * n + 64]
                halves = [v[:, :128], v[:, 128:]]
                for h in range(2):
                    ok = True if h != g else (gy > 0) if g == 0 else (gy < ny - 1)
                    if x < 2:
                        ok = ok & (gx > 0)
                    if x > 5:
                        ok = ok & (gx < nx - 1)
                    if ok is not True:
                        halves[h] = jnp.where(ok, halves[h], jnp.zeros_like(halves[h]))
                e2[g][x] = [v.astype(BF) for v in halves]

    enc2((3, 4))
    arrive(x2[:2])
    arrive(x2[4:])
    arrive(x2b[:2])
    arrive(x2b[6:])
    for n, y in enumerate((2, 0)):
        send(n, mate, 0, p1.at[y, pl.ds(4, 2)], p1.at[y, pl.ds(8 - 8 * odd, 2)], sp, rp).wait_recv()
        send(2 + n, mate, 0, p1.at[y, 3 + 3 * odd], p1.at[y, 7 - 5 * odd], sp, rp).wait_recv()

    @pl.when(gx == 0)
    def _():
        p1[:, pl.ds(0, 3)] = jnp.zeros((3, 3, 64, 128), BF)

    @pl.when(gx == nx - 1)
    def _():
        p1[:, pl.ds(7, 3)] = jnp.zeros((3, 3, 64, 128), BF)

    @pl.when(gy == 0)
    def _():
        for x in (0, 7):
            p1[0, pl.ds(x, 3)] = jnp.zeros((3, 64, 128), BF)

    @pl.when(gy == ny - 1)
    def _():
        for x in (0, 7):
            p1[2, pl.ds(x, 3)] = jnp.zeros((3, 64, 128), BF)

    enc2((0, 1, 2, 5, 6, 7))
    pairs = []
    for g in range(2):
        for x in range(4):
            a0, a1 = [e2[g][2 * x][h].astype(F32) + e2[g][2 * x + 1][h].astype(F32) for h in range(2)]
            a = jnp.where(low, a0 + pltpu.roll(a0, 64, 1), a1 + pltpu.roll(a1, 64, 1))
            pairs.append(((a + pltpu.roll(a, 63, 0)) * 0.125).astype(BF))
    pick32 = ones_where(iota((32, 64), 1) == 2 * iota((32, 64), 0))
    t = nn(pick32, cat(pairs, 1)).astype(BF)
    p2 = [cat([t[:, 128 * x : 128 * x + 128], t[:, 512 + 128 * x : 512 + 128 * x + 128]], 1) for x in range(4)]

    lhs = cat([cat([p2[x + i] for i in range(3)], 1) for x in range(2)], 0)
    t = nn(lhs, k3[...])
    e3 = gelu(t[:, 256:512] + shifted(t[:, :256], 1, 0, 32) + shifted(t[:, 512:], -1, 0, 32)).astype(BF)
    f = e3.astype(F32)
    a = f[:32] + f[32:]
    a = a[:, :128] + a[:, 128:]
    a = (a + pltpu.roll(a, 31, 0)) * 0.125
    pick16 = ones_where(iota((16, 32), 1) == 2 * iota((16, 32), 0))
    p3[2, gy + 2] = nn(pick16, a.astype(BF)).astype(BF)
    x4 = []
    for n, (dx, dy) in enumerate(window):
        x4.append(send(n, dx, dy, p3.at[2, gy + 2], p3.at[2 - dx, gy + 2], s4, r4))
    start(x4)
    for x in range(2):
        for y in range(2):
            e3e[x + 1, y + 1] = e3[32 * x : 32 * x + 32, 128 * y : 128 * y + 128]
    def cells(ref, n_local, ss, rs):
        copies = []
        for n, (dx, dy) in enumerate(DIRS):
            sx, tx, cx = side(dx, n_local)
            sy, ty, cy = side(dy, n_local)
            copies.append(
                send(n, dx, dy, ref.at[pl.ds(sx, cx), pl.ds(sy, cy)], ref.at[pl.ds(tx, cx), pl.ds(ty, cy)], ss, rs)
            )
        return copies

    xe3 = cells(e3e, 2, se3, re3)
    start(xe3)

    low32 = iota((32, 128), 1) < 64
    rr, cc = iota((64, 64), 0), iota((64, 64), 1)
    split = ones_where(cc == 2 * (rr % 32) + rr // 32)
    for x in range(6):
        t = nn(split, cat([e2[g][x + 1][h] for g in range(2) for h in range(2)], 1))
        for y in range(6):
            n = 128 * ((y + 1) // 2)
            ev, od = t[:32, n : n + 128], t[32:, n : n + 128]
            if y % 2 == 1:
                cell = jnp.where(low32, ev, pltpu.roll(od, 64, 1))
            else:
                cell = jnp.where(low32, pltpu.roll(ev, 64, 1), od)
            e2e[x, y] = cell.astype(BF)

    for c in got_w4:
        c.wait()
    for n, (dx, dy) in enumerate(window):
        pltpu.make_async_remote_copy(
            src_ref=p3.at[2, gy + 2], dst_ref=p3.at[2 - dx, lax.rem(gy - dy + ny, ny) + 2],
            send_sem=s4.at[n], recv_sem=r4.at[n], device_id=target(dx, dy), device_id_type=MESH,
        ).wait_recv()

    cell = []
    for x in range(5):
        inside = (gx + (x - 2) >= 0) & (gx + (x - 2) < nx)
        line = []
        for y in range(5):
            v = p3[x, gy + y]
            line.append(jnp.where(inside, v, jnp.zeros_like(v)))
        cell.append(line)
    lhs = cat(
        [
            cat([cell[x + i][y + j] for i in range(3) for j in range(3)], 1)
            for x in range(3)
            for y in range(3)
        ],
        0,
    )
    t = nt(lhs, k4[...])
    e4 = gelu(t[:, 256:512] + shifted(t[:, :256], 1, 0, 16) + shifted(t[:, 512:], -1, 0, 16))

    def inside(x, y, width, n_local):
        ok = True
        if x == 0:
            ok = gx > 0
        if x == n_local + 1:
            ok = gx < nx - 1
        if y == 0:
            ok = ok & (gy > 0)
        if y == n_local + 1:
            ok = ok & (gy < ny - 1)
        return ok

    def kept(v, ok):
        return v if ok is True else jnp.where(ok, v, jnp.zeros_like(v))


    e4 = [kept(e4[16 * n : 16 * n + 16], inside(n // 3, n % 3, 16, 1)).astype(BF) for n in range(9)]
    twice = ones_where(iota((32, 16), 1) == iota((32, 16), 0) // 2)
    up = nn(twice, cat(e4, 1)).astype(BF)
    at = ((0, 0, 1), (0, 1, 1), (1, 1, 2), (1, 2, 2))
    for k in range(2):
        for y in range(4):
            for tx in range(2):
                for j in range(3):
                    n = 3 * (k + tx) + at[y][j]
                    pd3[pl.ds(128 * k + 32 * y, 32), pl.ds(256 * (3 * tx + j), 256)] = up[:, 256 * n : 256 * n + 256]
    t = nt(pd3[...], g3[...])
    arrive(xe3)
    for px in range(2):
        u = t[:, 384 * px : 384 * px + 384]
        v = gelu(u[:, 128:256] + shifted(u[:, :128], 1, 0, 32) + shifted(u[:, 256:], -1, 0, 32))
        for k in range(2):
            for y in range(4):
                x, n = 2 * k + 1 - px, 128 * k + 32 * y
                w = v[n : n + 32] + e3e[x, y].astype(F32)
                d3e[x, y] = kept(w, inside(x, y, 32, 2)).astype(BF)

    lane = iota((288, 128), 1) < 64
    lhs = cat(
        [
            cat([d3e[k, m], d3e[k, m + 1], d3e[k + 1, m], d3e[k + 1, m + 1]], 1)
            for k in range(3)
            for m in range(3)
        ],
        0,
    )
    t = nt(lhs, g2[...])
    for px in range(2):
        for py in range(2):
            n = 256 * (2 * px + py)
            a, b = t[:, n : n + 128], t[:, n + 128 : n + 256]
            v = gelu(b + jnp.where(lane, shifted(a, 1, 0, 32), shifted(a, -1, 0, 32)))
            for k in range(3):
                for m in range(3):
                    x, y = 2 * k + 1 - px, 2 * m + 1 - py
                    w = v[96 * k + 32 * m : 96 * k + 32 * m + 32] + e2e[x, y].astype(F32)
                    d2e[x, y] = kept(w, inside(x, y, 32, 4))

    rr, cc = iota((128, 64), 0), iota((128, 64), 1)
    spread = ones_where((rr // 4 == cc % 32) & (rr // 2 % 2 == cc // 32))
    for x in range(6):
        line = []
        as_is = [d2e[x, m] for m in range(6)]
        turned = [pltpu.roll(v, 64, 1) for v in as_is]
        for m in range(5):
            top = jnp.where(low32, as_is[m], turned[m + 1])
            bottom = jnp.where(low32, turned[m], as_is[m + 1])
            line.append(cat([top, bottom], 0).astype(BF))
        a = nn(spread, cat(line, 1)).astype(BF)
        for m in range(5):
            q[x, m] = a[:, 128 * m : 128 * m + 128]

    both = ((0, 0), (0, 1), (1, 0), (1, 1))
    groups = []
    for parities, windows in (
        ([c for c in both if c[0] == 0], [(0, m) for m in range(5)]),
        ([c for c in both if c[1] == 0], [(k, 0) for k in range(1, 4)]),
        (both, [(k, m) for k in range(1, 4) for m in range(1, 4)]),
        ([c for c in both if c[1] == 1], [(k, 4) for k in range(1, 4)]),
        ([c for c in both if c[0] == 1], [(4, m) for m in range(5)]),
    ):
        for n in range(0, len(windows), 2):
            groups.append((parities, windows[n : n + 2]))
    for parities, windows in groups:
        lhs = cat([g1[pl.ds(96 * (2 * px + py), 96), :] for px, py in parities], 0)
        t = nt(lhs, cat([cat([q[k, m], q[k + 1, m]], 1) for k, m in windows], 0))
        for n, (px, py) in enumerate(parities):
            for h, (k, m) in enumerate(windows):
                a, b = k - px, m - py
                if not (0 <= a < 4 and 0 <= b < 4):
                    continue
                x, y = 2 * a + px, 2 * b + py
                u = t[96 * n : 96 * n + 96, 128 * h : 128 * h + 128]
                v = gelu(u[32:64] + shifted(u[:32], 1, 1, 128) + shifted(u[64:], -1, 1, 128))
                v = v + e1[x, pl.ds(32 * y, 32), :].astype(F32)
                out[x, y] = v.astype(BF)

    for copies in (x1, x2, x2b, passed, x4, xe3):
        for c in copies:
            c.wait_send()


def local(features, w_enc1, w_enc2, w_enc3, w_enc4, w_dec3, w_dec2, w_dec1):
    w_enc2, w_enc3 = jnp.swapaxes(w_enc2, 1, 2), jnp.swapaxes(w_enc3, 1, 2)
    w_enc4, w_dec3 = w_enc4.reshape(9, 768, 128), w_dec3.reshape(9, 384, 256)
    args = (features, w_enc1, w_enc2, w_enc3, w_enc4, w_dec3, w_dec2, w_dec1)
    ny = lax.axis_size("gy")
    far = 5 * ny - 1
    dma = pltpu.SemaphoreType.DMA
    scratch = [pltpu.VMEM(a.shape, BF) for a in (features, w_enc1, w_enc2, w_enc3, w_dec2, w_dec1)]
    for shape in (
        (10, 320, 128), (8, 256, 128),
        (3, 10, 64, 128),
        (5, ny + 4, 16, 128), (6, 6, 32, 128), (4, 4, 32, 128),
        (192, 384), (768, 768), (768, 768), (768, 1152), (384, 2304), (1024, 512), (384, 256),
        (256, 1536), (768, 1536), (4, 4, 32, 128),
    ):
        scratch.append(pltpu.VMEM(shape, BF))
    scratch.append(pltpu.VMEM((6, 6, 32, 128), F32))
    scratch.append(pltpu.VMEM((6, 5, 128, 128), BF))
    scratch.append(dma((24,)))
    for n in (8, 14, 4, far, 8):
        scratch += [dma((n,)), dma((n,))]
    decoded = pl.pallas_call(
        kernel,
        out_shape=pltpu.VMEM((8, 8, 32, 128), BF),
        in_specs=[pl.BlockSpec(memory_space=pl.ANY)] * 8,
        out_specs=pl.BlockSpec(memory_space=pltpu.VMEM),
        scratch_shapes=scratch,
        compiler_params=pltpu.CompilerParams(
            collective_id=0, has_side_effects=True, vmem_limit_bytes=48 * 1024 * 1024
        ),
        cost_estimate=pl.CostEstimate(flops=2 * 1115000000, bytes_accessed=7000000, transcendentals=1000000),
    )(*[pltpu.with_memory_space_constraint(a, pltpu.HBM) for a in args])
    return jnp.transpose(decoded, (2, 0, 1, 3))


def solution(mesh):
    return jax.shard_map(
        local,
        mesh=mesh,
        in_specs=(P(None, "gx", "gy", None), P(), P(), P(), P(), P(), P(), P()),
        out_specs=P(None, "gx", "gy", None),
        check_vma=False,
    )
```

```python
import functools

import jax
import jax.numpy as jnp
from jax import lax
from jax.experimental import pallas as pl
from jax.experimental.pallas import tpu as pltpu
from jax.sharding import PartitionSpec as P

BF = jnp.bfloat16
F32 = jnp.float32
MESH = pl.DeviceIdType.MESH
DIRS = [(-1, -1), (-1, 1), (1, -1), (1, 1), (-1, 0), (1, 0), (0, -1), (0, 1)]
TAPS = (((0,), (1, 2)), ((0, 1), (2,)))


def nn(a, b):
    return lax.dot_general(a, b, (((1,), (0,)), ((), ())), preferred_element_type=F32)


def nt(a, b):
    return lax.dot_general(a, b, (((1,), (1,)), ((), ())), preferred_element_type=F32)


def iota(shape, dim):
    return lax.broadcasted_iota(jnp.int32, shape, dim)


def ones_where(mask):
    return jnp.where(mask, 1.0, 0.0).astype(BF)


def gelu(x):
    half = 0.5 * x
    return half + half * jnp.tanh(x * (0.7978845608028654 + 0.035677408136300125 * (x * x)))


def shifted(v, step, axis, period):
    n = v.shape[axis]
    place = iota(v.shape, axis) % period
    edge = 0 if step == 1 else period - 1
    return jnp.where(place == edge, 0.0, pltpu.roll(v, step % n, axis))


def cat(parts, axis):
    return parts[0] if len(parts) == 1 else jnp.concatenate(parts, axis=axis)


def side(d, n, width=1, pad=1):
    if d == 1:
        return (pad + (n - 1)) * width, 0, width
    if d == -1:
        return pad * width, (n + pad) * width, width
    return pad * width, pad * width, n * width


def kernel(
    feat, w1h, w2h, w3h, w4h, v3h, v2h, v1h, out,
    fv, w1, w2, w3, v2, v1,
    fext, e1, p1, p3, e2e, e3e,
    k1, k2, k3, k4, kd3, g2, g1, pd3, g3, d3e, d2e, q,
    lsem, s1, r1, s2, r2, sp, rp, s4, r4, se3, re3,
):
    gx, gy = lax.axis_index("gx"), lax.axis_index("gy")
    nx, ny = lax.axis_size("gx"), lax.axis_size("gy")

    loads = []

    def load(src, dst):
        c = pltpu.make_async_copy(src, dst, lsem.at[len(loads)])
        c.start()
        loads.append(c)
        return c

    def target(dx, dy):
        return (lax.rem(gx + dx + nx, nx), lax.rem(gy + dy + ny, ny))

    barrier = pltpu.get_barrier_semaphore()
    for dx, dy in DIRS:
        pl.semaphore_signal(barrier, inc=1, device_id=target(dx, dy), device_id_type=MESH)
    got_feat = load(feat, fv)
    got_w1, got_w2, got_w3 = load(w1h, w1), load(w2h, w2), load(w3h, w3)
    got_v2, got_v1 = load(v2h, v2), load(v1h, v1)
    got_w4 = [load(w4h.at[n], k4.at[:, pl.ds(128 * n, 128)]) for n in range(9)]
    got_v3 = [load(v3h.at[n], kd3.at[:, pl.ds(256 * n, 256)]) for n in range(9)]

    def far(d):
        return abs(d[0]) + min(d[1], ny - d[1])

    window = [(dx, dy) for dx in range(-2, 3) for dy in range(ny) if (dx, dy) != (0, 0)]
    window.sort(key=far, reverse=True)

    def send(n, dx, dy, src, dst, ss, rs):
        return pltpu.make_async_remote_copy(
            src_ref=src, dst_ref=dst, send_sem=ss.at[n], recv_sem=rs.at[n],
            device_id=target(dx, dy), device_id_type=MESH,
        )

    def start(copies):
        for c in copies:
            c.start()

    def arrive(copies):
        for c in copies:
            c.wait_recv()

    got_feat.wait()
    r, c = iota((256, 256), 0), iota((256, 256), 1)
    perm = ones_where((r // 32 == c % 8) & (r % 32 == c // 8))

    def place(x, carry):
        a = fv[:, pl.ds(2 * x, 1)].astype(F32).reshape(256, 128).astype(BF)
        b = fv[:, pl.ds(2 * x + 1, 1)].astype(F32).reshape(256, 128).astype(BF)
        t = nn(perm, cat([a, b], 1)).astype(BF)
        fext[2 * x + 1, pl.ds(32, 256), :] = t[:, :128]
        fext[2 * x + 2, pl.ds(32, 256), :] = t[:, 128:]
        return carry

    lax.fori_loop(0, 4, place, 0)
    for n in range(4):
        p3[:, n if n < 2 else n + 4] = jnp.zeros((5, 16, 128), BF)
    pl.semaphore_wait(barrier, len(DIRS))

    x1 = []
    for n, (dx, dy) in enumerate(DIRS):
        sx, tx, cx = side(dx, 8)
        sy, ty, cy = side(dy, 8, 32)
        x1.append(
            send(n, dx, dy, fext.at[pl.ds(sx, cx), pl.ds(sy, cy)], fext.at[pl.ds(tx, cx), pl.ds(ty, cy)], s1, r1)
        )
    start(x1[:4])
    start(x1[6:])
    start(x1[4:6])

    got_w1.wait()
    t = None
    r, c = iota((32, 256), 0), iota((32, 256), 1)
    for j in range(3):
        taps = cat([w1[pl.ds(9 * i + 3 * j, 3)].reshape(96, 32) for i in range(3)], 0)
        u = nn(taps, ones_where((r == c % 32) & (c // 32 % 4 == c // 128 + j)))
        t = u if t is None else t + u
    t = t.astype(BF)
    for i in range(3):
        for l in range(3):
            for yo in range(2):
                k1[pl.ds(64 * l + 32 * yo, 32), pl.ds(128 * i, 128)] = t[
                    96 * i + 32 * l : 96 * i + 32 * l + 32, 128 * yo : 128 * yo + 128
                ]

    def enc1(xa, xb, b):
        rhs = cat(
            [cat([fext[xa + i, pl.ds(64 * b, 128), :], fext[xb + i, pl.ds(64 * b, 128), :]], 1) for i in range(3)],
            0,
        )
        t = nn(k1[...], rhs)
        for h, x in enumerate((xa, xb)):
            u = t[:, 128 * h : 128 * (h + 1)]
            v = u[64:128] + shifted(u[:64], 1, 1, 128) + shifted(u[128:], -1, 1, 128)
            e1[x, pl.ds(64 * b, 64), :] = gelu(v).astype(BF)

    def enc1_inner(n, carry, blocks):
        for b in blocks:
            enc1(2 * n + 1, 2 * n + 2, b)
        return carry

    lax.fori_loop(0, 3, functools.partial(enc1_inner, blocks=(1, 2)), 0)

    got_w2.wait()
    r, c = iota((64, 256), 0), iota((64, 256), 1)
    spots = [ones_where(c == r + 64 * yo) for yo in range(4)]
    taps = [cat([w2[pl.ds(9 * i + 3 * j, 3)].reshape(96, 64) for i in range(3)], 0) for j in range(3)]
    for yi in range(1, 7):
        t = None
        for j in range(3):
            if 0 <= yi - 1 - j < 4:
                u = nn(taps[j], spots[yi - 1 - j])
                t = u if t is None else t + u
        t = t.astype(BF)
        for i in range(3):
            for l in range(3):
                k2[pl.ds(256 * i + 32 * yi, 32), pl.ds(256 * l, 256)] = t[96 * i + 32 * l : 96 * i + 32 * l + 32]
    for i in range(3):
        for yi in (0, 7):
            k2[pl.ds(256 * i + 32 * yi, 32), :] = jnp.zeros((32, 768), BF)
    got_w3.wait()
    z128 = jnp.zeros((64, 128), BF)
    for i in range(3):
        for yi in range(4):
            for l in range(3):
                for yo in range(2):
                    j = yi - yo
                    k3[pl.ds(256 * i + 64 * yi, 64), pl.ds(256 * l + 128 * yo, 128)] = (
                        w3[9 * i + 3 * j + l] if 0 <= j < 3 else z128
                    )

    arrive(x1[6:])

    @pl.when(gy == 0)
    def _():
        fext[pl.ds(1, 8), pl.ds(0, 32)] = jnp.zeros((8, 32, 128), BF)

    @pl.when(gy == ny - 1)
    def _():
        fext[pl.ds(1, 8), pl.ds(288, 32)] = jnp.zeros((8, 32, 128), BF)

    for n in range(3):
        enc1_inner(n, 0, (0, 3))

    def pool1(x):
        a = e1[2 * x].astype(F32) + e1[2 * x + 1].astype(F32)
        a = cat([a[64 * b : 64 * b + 32] + a[64 * b + 32 : 64 * b + 64] for b in range(4)], 0)
        a = (a + pltpu.roll(a, 127, 1)) * 0.125
        return a.astype(BF)

    pick64 = ones_where(iota((64, 128), 1) == 2 * iota((64, 128), 0))
    t = nt(pick64, cat([pool1(1), pool1(2)], 0)).astype(BF)
    p1[1, 4], p1[1, 5] = t[:, :128], t[:, 128:]

    odd = lax.rem(gx, 2)
    mate = 1 - 2 * odd
    inner = p1.at[1, pl.ds(4, 2)]
    x2 = []
    for n, dy in enumerate((-1, 1)):
        x2.append(send(n, -mate, dy, inner, p1.at[1 - dy, pl.ds(8 - 8 * odd, 2)], s2, r2))
    for n, dy in enumerate((-1, 1)):
        x2.append(send(2 + n, 0, dy, inner, p1.at[1 - dy, pl.ds(4, 2)], s2, r2))
    x2.append(send(4, -1, 0, inner, p1.at[1, pl.ds(8, 2)], s2, r2))
    x2.append(send(5, 1, 0, inner, p1.at[1, pl.ds(0, 2)], s2, r2))
    start(x2)

    arrive(x1[4:6])

    @pl.when(gx == 0)
    def _():
        fext[0, pl.ds(32, 256)] = jnp.zeros((256, 128), BF)

    @pl.when(gx == nx - 1)
    def _():
        fext[9, pl.ds(32, 256)] = jnp.zeros((256, 128), BF)

    enc1(0, 7, 1)
    enc1(0, 7, 2)
    arrive(x1[:4])

    @pl.when((gx == 0) | (gy == 0))
    def _():
        fext[0, pl.ds(0, 32)] = jnp.zeros((32, 128), BF)

    @pl.when((gx == 0) | (gy == ny - 1))
    def _():
        fext[0, pl.ds(288, 32)] = jnp.zeros((32, 128), BF)

    @pl.when((gx == nx - 1) | (gy == 0))
    def _():
        fext[9, pl.ds(0, 32)] = jnp.zeros((32, 128), BF)

    @pl.when((gx == nx - 1) | (gy == ny - 1))
    def _():
        fext[9, pl.ds(288, 32)] = jnp.zeros((32, 128), BF)

    enc1(0, 7, 0)
    enc1(0, 7, 3)
    t = nt(pick64, cat([pool1(0), pool1(3)], 0)).astype(BF)
    p1[1, 3], p1[1, 6] = t[:, :128], t[:, 128:]
    x2b = []
    for n, dy in enumerate((-1, 1)):
        x2b.append(send(6 + n, -mate, dy, p1.at[1, 3 + 3 * odd], p1.at[1 - dy, 7 - 5 * odd], s2, r2))
    for n, (dy, x) in enumerate(((-1, 3), (1, 3), (-1, 6), (1, 6))):
        x2b.append(send(8 + n, 0, dy, p1.at[1, x], p1.at[1 - dy, x], s2, r2))
    x2b.append(send(12, -1, 0, p1.at[1, 3], p1.at[1, 7], s2, r2))
    x2b.append(send(13, 1, 0, p1.at[1, 6], p1.at[1, 2], s2, r2))
    start(x2b)

    got_v2.wait()
    for px in range(2):
        for py in range(2):
            for tx in range(2):
                for ty in range(2):
                    s = []
                    for l in range(3):
                        terms = [
                            v2[9 * i + 3 * j + l].astype(F32) for i in TAPS[px][tx] for j in TAPS[py][ty]
                        ]
                        s.append(functools.reduce(jnp.add, terms))
                    block = cat([s[0], s[2], s[1] + s[2], s[0] + s[1]], 0).astype(BF)
                    g2[pl.ds(256 * (2 * px + py), 256), pl.ds(128 * (2 * tx + ty), 128)] = block
    got_v1.wait()
    for px in range(2):
        for py in range(2):
            for l in range(3):
                row = []
                for tx in range(2):
                    for ty in range(2):
                        terms = [
                            v1[9 * i + 3 * j + l].astype(F32) for i in TAPS[px][tx] for j in TAPS[py][ty]
                        ]
                        row.append(functools.reduce(jnp.add, terms).astype(BF))
                g1[pl.ds(96 * (2 * px + py) + 32 * l, 32), :] = cat(row, 1)

    for c in got_v3:
        c.wait()

    def sum_taps(n, carry):
        rows = pl.ds(pl.multiple_of(32 * n, 32), 32)
        lower = pl.ds(pl.multiple_of(384 + 32 * n, 32), 32)
        taps = [kd3[rows, 768 * i : 768 * i + 768] for i in range(3)]
        g3[rows, :768] = taps[0]
        g3[rows, 768:] = (taps[1].astype(F32) + taps[2].astype(F32)).astype(BF)
        g3[lower, :768] = (taps[0].astype(F32) + taps[1].astype(F32)).astype(BF)
        g3[lower, 768:] = taps[2]
        return carry

    lax.fori_loop(0, 12, sum_taps, 0)

    passed = []
    for part, xs in ((x2[2:4], (4, 5)), (x2b[2:6], (3, 6))):
        arrive(part)

        @pl.when(gy == 0)
        def _():
            for x in xs:
                p1[0, x] = jnp.zeros((64, 128), BF)

        @pl.when(gy == ny - 1)
        def _():
            for x in xs:
                p1[2, x] = jnp.zeros((64, 128), BF)

        new = []
        for n, y in enumerate((2, 0)):
            if xs == (4, 5):
                new.append(send(n, mate, 0, p1.at[y, pl.ds(4, 2)], p1.at[y, pl.ds(8 * odd, 2)], sp, rp))
            else:
                new.append(send(2 + n, mate, 0, p1.at[y, 6 - 3 * odd], p1.at[y, 2 + 5 * odd], sp, rp))
        start(new)
        passed += new

    low = iota((64, 128), 1) < 64
    e2 = [[None] * 8, [None] * 8]

    def enc2(xs):
        for g in range(2):
            lhs = cat(
                [cat([cat([p1[g, x + i], p1[g + 1, x + i]], 1) for i in range(3)], 1) for x in xs], 0
            )
            t = nn(lhs, k2[...])
            t = gelu(t[:, 256:512] + shifted(t[:, :256], 1, 0, 64) + shifted(t[:, 512:], -1, 0, 64))
            for n, x in enumerate(xs):
                v = t[64 * n : 64 * n + 64]
                halves = [v[:, :128], v[:, 128:]]
                for h in range(2):
                    ok = True if h != g else (gy > 0) if g == 0 else (gy < ny - 1)
                    if x < 2:
                        ok = ok & (gx > 0)
                    if x > 5:
                        ok = ok & (gx < nx - 1)
                    if ok is not True:
                        halves[h] = jnp.where(ok, halves[h], jnp.zeros_like(halves[h]))
                e2[g][x] = [v.astype(BF) for v in halves]

    enc2((3, 4))
    arrive(x2[:2])
    arrive(x2[4:])
    arrive(x2b[:2])
    arrive(x2b[6:])
    for n, y in enumerate((2, 0)):
        send(n, mate, 0, p1.at[y, pl.ds(4, 2)], p1.at[y, pl.ds(8 - 8 * odd, 2)], sp, rp).wait_recv()
        send(2 + n, mate, 0, p1.at[y, 3 + 3 * odd], p1.at[y, 7 - 5 * odd], sp, rp).wait_recv()

    @pl.when(gx == 0)
    def _():
        p1[:, pl.ds(0, 3)] = jnp.zeros((3, 3, 64, 128), BF)

    @pl.when(gx == nx - 1)
    def _():
        p1[:, pl.ds(7, 3)] = jnp.zeros((3, 3, 64, 128), BF)

    @pl.when(gy == 0)
    def _():
        for x in (0, 7):
            p1[0, pl.ds(x, 3)] = jnp.zeros((3, 64, 128), BF)

    @pl.when(gy == ny - 1)
    def _():
        for x in (0, 7):
            p1[2, pl.ds(x, 3)] = jnp.zeros((3, 64, 128), BF)

    enc2((0, 1, 2, 5, 6, 7))
    pairs = []
    for g in range(2):
        for x in range(4):
            a0, a1 = [e2[g][2 * x][h].astype(F32) + e2[g][2 * x + 1][h].astype(F32) for h in range(2)]
            a = jnp.where(low, a0 + pltpu.roll(a0, 64, 1), a1 + pltpu.roll(a1, 64, 1))
            pairs.append(((a + pltpu.roll(a, 63, 0)) * 0.125).astype(BF))
    pick32 = ones_where(iota((32, 64), 1) == 2 * iota((32, 64), 0))
    t = nn(pick32, cat(pairs, 1)).astype(BF)
    p2 = [cat([t[:, 128 * x : 128 * x + 128], t[:, 512 + 128 * x : 512 + 128 * x + 128]], 1) for x in range(4)]

    lhs = cat([cat([p2[x + i] for i in range(3)], 1) for x in range(2)], 0)
    t = nn(lhs, k3[...])
    e3 = gelu(t[:, 256:512] + shifted(t[:, :256], 1, 0, 32) + shifted(t[:, 512:], -1, 0, 32)).astype(BF)
    f = e3.astype(F32)
    a = f[:32] + f[32:]
    a = a[:, :128] + a[:, 128:]
    a = (a + pltpu.roll(a, 31, 0)) * 0.125
    pick16 = ones_where(iota((16, 32), 1) == 2 * iota((16, 32), 0))
    p3[2, gy + 2] = nn(pick16, a.astype(BF)).astype(BF)
    x4 = []
    for n, (dx, dy) in enumerate(window):
        x4.append(send(n, dx, dy, p3.at[2, gy + 2], p3.at[2 - dx, gy + 2], s4, r4))
    start(x4)
    for x in range(2):
        for y in range(2):
            e3e[x + 1, y + 1] = e3[32 * x : 32 * x + 32, 128 * y : 128 * y + 128]
    def cells(ref, n_local, ss, rs):
        copies = []
        for n, (dx, dy) in enumerate(DIRS):
            sx, tx, cx = side(dx, n_local)
            sy, ty, cy = side(dy, n_local)
            copies.append(
                send(n, dx, dy, ref.at[pl.ds(sx, cx), pl.ds(sy, cy)], ref.at[pl.ds(tx, cx), pl.ds(ty, cy)], ss, rs)
            )
        return copies

    xe3 = cells(e3e, 2, se3, re3)
    start(xe3)

    low32 = iota((32, 128), 1) < 64
    rr, cc = iota((64, 64), 0), iota((64, 64), 1)
    split = ones_where(cc == 2 * (rr % 32) + rr // 32)
    for x in range(6):
        t = nn(split, cat([e2[g][x + 1][h] for g in range(2) for h in range(2)], 1))
        for y in range(6):
            n = 128 * ((y + 1) // 2)
            ev, od = t[:32, n : n + 128], t[32:, n : n + 128]
            if y % 2 == 1:
                cell = jnp.where(low32, ev, pltpu.roll(od, 64, 1))
            else:
                cell = jnp.where(low32, pltpu.roll(ev, 64, 1), od)
            e2e[x, y] = cell.astype(BF)

    for c in got_w4:
        c.wait()
    for n, (dx, dy) in enumerate(window):
        pltpu.make_async_remote_copy(
            src_ref=p3.at[2, gy + 2], dst_ref=p3.at[2 - dx, lax.rem(gy - dy + ny, ny) + 2],
            send_sem=s4.at[n], recv_sem=r4.at[n], device_id=target(dx, dy), device_id_type=MESH,
        ).wait_recv()

    cell = []
    for x in range(5):
        inside = (gx + (x - 2) >= 0) & (gx + (x - 2) < nx)
        line = []
        for y in range(5):
            v = p3[x, gy + y]
            line.append(jnp.where(inside, v, jnp.zeros_like(v)))
        cell.append(line)
    lhs = cat(
        [
            cat([cell[x + i][y + j] for i in range(3) for j in range(3)], 1)
            for x in range(3)
            for y in range(3)
        ],
        0,
    )
    t = nt(lhs, k4[...])
    e4 = gelu(t[:, 256:512] + shifted(t[:, :256], 1, 0, 16) + shifted(t[:, 512:], -1, 0, 16))

    def inside(x, y, width, n_local):
        ok = True
        if x == 0:
            ok = gx > 0
        if x == n_local + 1:
            ok = gx < nx - 1
        if y == 0:
            ok = ok & (gy > 0)
        if y == n_local + 1:
            ok = ok & (gy < ny - 1)
        return ok

    def kept(v, ok):
        return v if ok is True else jnp.where(ok, v, jnp.zeros_like(v))


    e4 = [kept(e4[16 * n : 16 * n + 16], inside(n // 3, n % 3, 16, 1)).astype(BF) for n in range(9)]
    twice = ones_where(iota((32, 16), 1) == iota((32, 16), 0) // 2)
    up = nn(twice, cat(e4, 1)).astype(BF)
    at = ((0, 0, 1), (0, 1, 1), (1, 1, 2), (1, 2, 2))
    for k in range(2):
        for y in range(4):
            for tx in range(2):
                for j in range(3):
                    n = 3 * (k + tx) + at[y][j]
                    pd3[pl.ds(128 * k + 32 * y, 32), pl.ds(256 * (3 * tx + j), 256)] = up[:, 256 * n : 256 * n + 256]
    t = nt(pd3[...], g3[...])
    arrive(xe3)
    for px in range(2):
        u = t[:, 384 * px : 384 * px + 384]
        v = gelu(u[:, 128:256] + shifted(u[:, :128], 1, 0, 32) + shifted(u[:, 256:], -1, 0, 32))
        for k in range(2):
            for y in range(4):
                x, n = 2 * k + 1 - px, 128 * k + 32 * y
                w = v[n : n + 32] + e3e[x, y].astype(F32)
                d3e[x, y] = kept(w, inside(x, y, 32, 2)).astype(BF)

    lane = iota((288, 128), 1) < 64
    lhs = cat(
        [
            cat([d3e[k, m], d3e[k, m + 1], d3e[k + 1, m], d3e[k + 1, m + 1]], 1)
            for k in range(3)
            for m in range(3)
        ],
        0,
    )
    t = nt(lhs, g2[...])
    for px in range(2):
        for py in range(2):
            n = 256 * (2 * px + py)
            a, b = t[:, n : n + 128], t[:, n + 128 : n + 256]
            v = gelu(b + jnp.where(lane, shifted(a, 1, 0, 32), shifted(a, -1, 0, 32)))
            for k in range(3):
                for m in range(3):
                    x, y = 2 * k + 1 - px, 2 * m + 1 - py
                    w = v[96 * k + 32 * m : 96 * k + 32 * m + 32] + e2e[x, y].astype(F32)
                    d2e[x, y] = kept(w, inside(x, y, 32, 4))

    rr, cc = iota((128, 64), 0), iota((128, 64), 1)
    spread = ones_where((rr // 4 == cc % 32) & (rr // 2 % 2 == cc // 32))
    for x in range(6):
        line = []
        as_is = [d2e[x, m] for m in range(6)]
        turned = [pltpu.roll(v, 64, 1) for v in as_is]
        for m in range(5):
            top = jnp.where(low32, as_is[m], turned[m + 1])
            bottom = jnp.where(low32, turned[m], as_is[m + 1])
            line.append(cat([top, bottom], 0).astype(BF))
        a = nn(spread, cat(line, 1)).astype(BF)
        for m in range(5):
            q[x, m] = a[:, 128 * m : 128 * m + 128]

    both = ((0, 0), (0, 1), (1, 0), (1, 1))
    groups = []
    for parities, windows in (
        ([c for c in both if c[0] == 0], [(0, m) for m in range(5)]),
        ([c for c in both if c[1] == 0], [(k, 0) for k in range(1, 4)]),
        (both, [(k, m) for k in range(1, 4) for m in range(1, 4)]),
        ([c for c in both if c[1] == 1], [(k, 4) for k in range(1, 4)]),
        ([c for c in both if c[0] == 1], [(4, m) for m in range(5)]),
    ):
        for n in range(0, len(windows), 2):
            groups.append((parities, windows[n : n + 2]))
    for parities, windows in groups:
        lhs = cat([g1[pl.ds(96 * (2 * px + py), 96), :] for px, py in parities], 0)
        t = nt(lhs, cat([cat([q[k, m], q[k + 1, m]], 1) for k, m in windows], 0))
        for n, (px, py) in enumerate(parities):
            for h, (k, m) in enumerate(windows):
                a, b = k - px, m - py
                if not (0 <= a < 4 and 0 <= b < 4):
                    continue
                x, y = 2 * a + px, 2 * b + py
                u = t[96 * n : 96 * n + 96, 128 * h : 128 * h + 128]
                v = gelu(u[32:64] + shifted(u[:32], 1, 1, 128) + shifted(u[64:], -1, 1, 128))
                v = v + e1[x, pl.ds(32 * y, 32), :].astype(F32)
                out[x, y] = v.astype(BF)

    for copies in (x1, x2, x2b, passed, x4, xe3):
        for c in copies:
            c.wait_send()


def local(features, w_enc1, w_enc2, w_enc3, w_enc4, w_dec3, w_dec2, w_dec1):
    w_enc2, w_enc3 = jnp.swapaxes(w_enc2, 1, 2), jnp.swapaxes(w_enc3, 1, 2)
    w_enc4, w_dec3 = w_enc4.reshape(9, 768, 128), w_dec3.reshape(9, 384, 256)
    args = (features, w_enc1, w_enc2, w_enc3, w_enc4, w_dec3, w_dec2, w_dec1)
    ny = lax.axis_size("gy")
    far = 5 * ny - 1
    dma = pltpu.SemaphoreType.DMA
    scratch = [pltpu.VMEM(a.shape, BF) for a in (features, w_enc1, w_enc2, w_enc3, w_dec2, w_dec1)]
    for shape in (
        (10, 320, 128), (8, 256, 128),
        (3, 10, 64, 128),
        (5, ny + 4, 16, 128), (6, 6, 32, 128), (4, 4, 32, 128),
        (192, 384), (768, 768), (768, 768), (768, 1152), (384, 2304), (1024, 512), (384, 256),
        (256, 1536), (768, 1536), (4, 4, 32, 128),
    ):
        scratch.append(pltpu.VMEM(shape, BF))
    scratch.append(pltpu.VMEM((6, 6, 32, 128), F32))
    scratch.append(pltpu.VMEM((6, 5, 128, 128), BF))
    scratch.append(dma((24,)))
    for n in (8, 14, 4, far, 8):
        scratch += [dma((n,)), dma((n,))]
    decoded = pl.pallas_call(
        kernel,
        out_shape=pltpu.VMEM((8, 8, 32, 128), BF),
        in_specs=[pl.BlockSpec(memory_space=pl.ANY)] * 8,
        out_specs=pl.BlockSpec(memory_space=pltpu.VMEM),
        scratch_shapes=scratch,
        compiler_params=pltpu.CompilerParams(
            collective_id=0, has_side_effects=True, vmem_limit_bytes=48 * 1024 * 1024
        ),
        cost_estimate=pl.CostEstimate(flops=2 * 1115000000, bytes_accessed=7000000, transcendentals=1000000),
    )(*[pltpu.with_memory_space_constraint(a, pltpu.HBM) for a in args])
    return jnp.transpose(decoded, (2, 0, 1, 3))


def solution(mesh):
    return jax.shard_map(
        local,
        mesh=mesh,
        in_specs=(P(None, "gx", "gy", None), P(), P(), P(), P(), P(), P(), P()),
        out_specs=P(None, "gx", "gy", None),
        check_vma=False,
    )
```

```python
import functools

import jax
import jax.numpy as jnp
from jax import lax
from jax.experimental import pallas as pl
from jax.experimental.pallas import tpu as pltpu
from jax.sharding import PartitionSpec as P

BF = jnp.bfloat16
F32 = jnp.float32
MESH = pl.DeviceIdType.MESH
DIRS = [(-1, -1), (-1, 1), (1, -1), (1, 1), (-1, 0), (1, 0), (0, -1), (0, 1)]
TAPS = (((0,), (1, 2)), ((0, 1), (2,)))


def nn(a, b):
    return lax.dot_general(a, b, (((1,), (0,)), ((), ())), preferred_element_type=F32)


def nt(a, b):
    return lax.dot_general(a, b, (((1,), (1,)), ((), ())), preferred_element_type=F32)


def iota(shape, dim):
    return lax.broadcasted_iota(jnp.int32, shape, dim)


def ones_where(mask):
    return jnp.where(mask, 1.0, 0.0).astype(BF)


def gelu(x):
    half = 0.5 * x
    return half + half * jnp.tanh(x * (0.7978845608028654 + 0.035677408136300125 * (x * x)))


def shifted(v, step, axis, period):
    n = v.shape[axis]
    place = iota(v.shape, axis) % period
    edge = 0 if step == 1 else period - 1
    return jnp.where(place == edge, 0.0, pltpu.roll(v, step % n, axis))


def cat(parts, axis):
    return parts[0] if len(parts) == 1 else jnp.concatenate(parts, axis=axis)


def side(d, n, width=1, pad=1):
    if d == 1:
        return (pad + (n - 1)) * width, 0, width
    if d == -1:
        return pad * width, (n + pad) * width, width
    return pad * width, pad * width, n * width


def kernel(
    feat, w1h, w2h, w3h, w4h, v3h, v2h, v1h, out,
    fv, w1, w2, w3, v2, v1,
    fext, e1, p1, p3, e2e, e3e,
    k1, k2, k3, k4, kd3, g2, g1, pd3, g3, d3e, d2e, q,
    lsem, s1, r1, s2, r2, sp, rp, s4, r4, se3, re3,
):
    gx, gy = lax.axis_index("gx"), lax.axis_index("gy")
    nx, ny = lax.axis_size("gx"), lax.axis_size("gy")

    loads = []

    def load(src, dst):
        c = pltpu.make_async_copy(src, dst, lsem.at[len(loads)])
        c.start()
        loads.append(c)
        return c

    def target(dx, dy):
        return (lax.rem(gx + dx + nx, nx), lax.rem(gy + dy + ny, ny))

    barrier = pltpu.get_barrier_semaphore()
    for dx, dy in DIRS:
        pl.semaphore_signal(barrier, inc=1, device_id=target(dx, dy), device_id_type=MESH)
    got_feat = load(feat, fv)
    got_w1, got_w2, got_w3 = load(w1h, w1), load(w2h, w2), load(w3h, w3)
    got_v2, got_v1 = load(v2h, v2), load(v1h, v1)
    got_w4 = [load(w4h.at[n], k4.at[:, pl.ds(128 * n, 128)]) for n in range(9)]
    got_v3 = [load(v3h.at[n], kd3.at[:, pl.ds(256 * n, 256)]) for n in range(9)]

    def far(d):
        return abs(d[0]) + min(d[1], ny - d[1])

    window = [(dx, dy) for dx in range(-2, 3) for dy in range(ny) if (dx, dy) != (0, 0)]
    window.sort(key=far, reverse=True)

    def send(n, dx, dy, src, dst, ss, rs):
        return pltpu.make_async_remote_copy(
            src_ref=src, dst_ref=dst, send_sem=ss.at[n], recv_sem=rs.at[n],
            device_id=target(dx, dy), device_id_type=MESH,
        )

    def start(copies):
        for c in copies:
            c.start()

    def arrive(copies):
        for c in copies:
            c.wait_recv()

    got_feat.wait()
    r, c = iota((256, 256), 0), iota((256, 256), 1)
    perm = ones_where((r // 32 == c % 8) & (r % 32 == c // 8))

    def place(x, carry):
        a = fv[:, pl.ds(2 * x, 1)].astype(F32).reshape(256, 128).astype(BF)
        b = fv[:, pl.ds(2 * x + 1, 1)].astype(F32).reshape(256, 128).astype(BF)
        t = nn(perm, cat([a, b], 1)).astype(BF)
        fext[2 * x + 1, pl.ds(32, 256), :] = t[:, :128]
        fext[2 * x + 2, pl.ds(32, 256), :] = t[:, 128:]
        return carry

    lax.fori_loop(0, 4, place, 0)
    for n in range(4):
        p3[:, n if n < 2 else n + 4] = jnp.zeros((5, 16, 128), BF)
    pl.semaphore_wait(barrier, len(DIRS))

    x1 = []
    for n, (dx, dy) in enumerate(DIRS):
        sx, tx, cx = side(dx, 8)
        sy, ty, cy = side(dy, 8, 32)
        x1.append(
            send(n, dx, dy, fext.at[pl.ds(sx, cx), pl.ds(sy, cy)], fext.at[pl.ds(tx, cx), pl.ds(ty, cy)], s1, r1)
        )
    start(x1[:4])
    start(x1[6:])
    start(x1[4:6])

    got_w1.wait()
    t = None
    r, c = iota((32, 256), 0), iota((32, 256), 1)
    for j in range(3):
        taps = cat([w1[pl.ds(9 * i + 3 * j, 3)].reshape(96, 32) for i in range(3)], 0)
        u = nn(taps, ones_where((r == c % 32) & (c // 32 % 4 == c // 128 + j)))
        t = u if t is None else t + u
    t = t.astype(BF)
    for i in range(3):
        for l in range(3):
            for yo in range(2):
                k1[pl.ds(64 * l + 32 * yo, 32), pl.ds(128 * i, 128)] = t[
                    96 * i + 32 * l : 96 * i + 32 * l + 32, 128 * yo : 128 * yo + 128
                ]

    def enc1(xa, xb, b):
        rhs = cat(
            [cat([fext[xa + i, pl.ds(64 * b, 128), :], fext[xb + i, pl.ds(64 * b, 128), :]], 1) for i in range(3)],
            0,
        )
        t = nn(k1[...], rhs)
        for h, x in enumerate((xa, xb)):
            u = t[:, 128 * h : 128 * (h + 1)]
            v = u[64:128] + shifted(u[:64], 1, 1, 128) + shifted(u[128:], -1, 1, 128)
            e1[x, pl.ds(64 * b, 64), :] = gelu(v).astype(BF)

    def enc1_inner(n, carry, blocks):
        for b in blocks:
            enc1(2 * n + 1, 2 * n + 2, b)
        return carry

    lax.fori_loop(0, 3, functools.partial(enc1_inner, blocks=(1, 2)), 0)

    got_w2.wait()
    r, c = iota((64, 256), 0), iota((64, 256), 1)
    spots = [ones_where(c == r + 64 * yo) for yo in range(4)]
    taps = [cat([w2[pl.ds(9 * i + 3 * j, 3)].reshape(96, 64) for i in range(3)], 0) for j in range(3)]
    for yi in range(1, 7):
        t = None
        for j in range(3):
            if 0 <= yi - 1 - j < 4:
                u = nn(taps[j], spots[yi - 1 - j])
                t = u if t is None else t + u
        t = t.astype(BF)
        for i in range(3):
            for l in range(3):
                k2[pl.ds(256 * i + 32 * yi, 32), pl.ds(256 * l, 256)] = t[96 * i + 32 * l : 96 * i + 32 * l + 32]
    for i in range(3):
        for yi in (0, 7):
            k2[pl.ds(256 * i + 32 * yi, 32), :] = jnp.zeros((32, 768), BF)
    got_w3.wait()
    z128 = jnp.zeros((64, 128), BF)
    for i in range(3):
        for yi in range(4):
            for l in range(3):
                for yo in range(2):
                    j = yi - yo
                    k3[pl.ds(256 * i + 64 * yi, 64), pl.ds(256 * l + 128 * yo, 128)] = (
                        w3[9 * i + 3 * j + l] if 0 <= j < 3 else z128
                    )

    arrive(x1[6:])

    @pl.when(gy == 0)
    def _():
        fext[pl.ds(1, 8), pl.ds(0, 32)] = jnp.zeros((8, 32, 128), BF)

    @pl.when(gy == ny - 1)
    def _():
        fext[pl.ds(1, 8), pl.ds(288, 32)] = jnp.zeros((8, 32, 128), BF)

    for n in range(3):
        enc1_inner(n, 0, (0, 3))

    def pool1(x):
        a = e1[2 * x].astype(F32) + e1[2 * x + 1].astype(F32)
        a = cat([a[64 * b : 64 * b + 32] + a[64 * b + 32 : 64 * b + 64] for b in range(4)], 0)
        a = (a + pltpu.roll(a, 127, 1)) * 0.125
        return a.astype(BF)

    pick64 = ones_where(iota((64, 128), 1) == 2 * iota((64, 128), 0))
    t = nt(pick64, cat([pool1(1), pool1(2)], 0)).astype(BF)
    p1[1, 4], p1[1, 5] = t[:, :128], t[:, 128:]

    odd = lax.rem(gx, 2)
    mate = 1 - 2 * odd
    inner = p1.at[1, pl.ds(4, 2)]
    x2 = []
    for n, dy in enumerate((-1, 1)):
        x2.append(send(n, -mate, dy, inner, p1.at[1 - dy, pl.ds(8 - 8 * odd, 2)], s2, r2))
    for n, dy in enumerate((-1, 1)):
        x2.append(send(2 + n, 0, dy, inner, p1.at[1 - dy, pl.ds(4, 2)], s2, r2))
    x2.append(send(4, -1, 0, inner, p1.at[1, pl.ds(8, 2)], s2, r2))
    x2.append(send(5, 1, 0, inner, p1.at[1, pl.ds(0, 2)], s2, r2))
    start(x2)

    arrive(x1[4:6])

    @pl.when(gx == 0)
    def _():
        fext[0, pl.ds(32, 256)] = jnp.zeros((256, 128), BF)

    @pl.when(gx == nx - 1)
    def _():
        fext[9, pl.ds(32, 256)] = jnp.zeros((256, 128), BF)

    enc1(0, 7, 1)
    enc1(0, 7, 2)
    arrive(x1[:4])

    @pl.when((gx == 0) | (gy == 0))
    def _():
        fext[0, pl.ds(0, 32)] = jnp.zeros((32, 128), BF)

    @pl.when((gx == 0) | (gy == ny - 1))
    def _():
        fext[0, pl.ds(288, 32)] = jnp.zeros((32, 128), BF)

    @pl.when((gx == nx - 1) | (gy == 0))
    def _():
        fext[9, pl.ds(0, 32)] = jnp.zeros((32, 128), BF)

    @pl.when((gx == nx - 1) | (gy == ny - 1))
    def _():
        fext[9, pl.ds(288, 32)] = jnp.zeros((32, 128), BF)

    enc1(0, 7, 0)
    enc1(0, 7, 3)
    t = nt(pick64, cat([pool1(0), pool1(3)], 0)).astype(BF)
    p1[1, 3], p1[1, 6] = t[:, :128], t[:, 128:]
    x2b = []
    for n, dy in enumerate((-1, 1)):
        x2b.append(send(6 + n, -mate, dy, p1.at[1, 3 + 3 * odd], p1.at[1 - dy, 7 - 5 * odd], s2, r2))
    for n, (dy, x) in enumerate(((-1, 3), (1, 3), (-1, 6), (1, 6))):
        x2b.append(send(8 + n, 0, dy, p1.at[1, x], p1.at[1 - dy, x], s2, r2))
    x2b.append(send(12, -1, 0, p1.at[1, 3], p1.at[1, 7], s2, r2))
    x2b.append(send(13, 1, 0, p1.at[1, 6], p1.at[1, 2], s2, r2))
    start(x2b)

    got_v2.wait()
    for px in range(2):
        for py in range(2):
            for tx in range(2):
                for ty in range(2):
                    s = []
                    for l in range(3):
                        terms = [
                            v2[9 * i + 3 * j + l].astype(F32) for i in TAPS[px][tx] for j in TAPS[py][ty]
                        ]
                        s.append(functools.reduce(jnp.add, terms))
                    block = cat([s[0], s[2], s[1] + s[2], s[0] + s[1]], 0).astype(BF)
                    g2[pl.ds(256 * (2 * px + py), 256), pl.ds(128 * (2 * tx + ty), 128)] = block
    got_v1.wait()
    for px in range(2):
        for py in range(2):
            for l in range(3):
                row = []
                for tx in range(2):
                    for ty in range(2):
                        terms = [
                            v1[9 * i + 3 * j + l].astype(F32) for i in TAPS[px][tx] for j in TAPS[py][ty]
                        ]
                        row.append(functools.reduce(jnp.add, terms).astype(BF))
                g1[pl.ds(96 * (2 * px + py) + 32 * l, 32), :] = cat(row, 1)

    for c in got_v3:
        c.wait()

    def sum_taps(n, carry):
        rows = pl.ds(pl.multiple_of(32 * n, 32), 32)
        lower = pl.ds(pl.multiple_of(384 + 32 * n, 32), 32)
        taps = [kd3[rows, 768 * i : 768 * i + 768] for i in range(3)]
        g3[rows, :768] = taps[0]
        g3[rows, 768:] = (taps[1].astype(F32) + taps[2].astype(F32)).astype(BF)
        g3[lower, :768] = (taps[0].astype(F32) + taps[1].astype(F32)).astype(BF)
        g3[lower, 768:] = taps[2]
        return carry

    lax.fori_loop(0, 12, sum_taps, 0)

    passed = []
    for part, xs in ((x2[2:4], (4, 5)), (x2b[2:6], (3, 6))):
        arrive(part)

        @pl.when(gy == 0)
        def _():
            for x in xs:
                p1[0, x] = jnp.zeros((64, 128), BF)

        @pl.when(gy == ny - 1)
        def _():
            for x in xs:
                p1[2, x] = jnp.zeros((64, 128), BF)

        new = []
        for n, y in enumerate((2, 0)):
            if xs == (4, 5):
                new.append(send(n, mate, 0, p1.at[y, pl.ds(4, 2)], p1.at[y, pl.ds(8 * odd, 2)], sp, rp))
            else:
                new.append(send(2 + n, mate, 0, p1.at[y, 6 - 3 * odd], p1.at[y, 2 + 5 * odd], sp, rp))
        start(new)
        passed += new

    low = iota((64, 128), 1) < 64
    e2 = [[None] * 8, [None] * 8]

    def enc2(xs):
        for g in range(2):
            lhs = cat(
                [cat([cat([p1[g, x + i], p1[g + 1, x + i]], 1) for i in range(3)], 1) for x in xs], 0
            )
            t = nn(lhs, k2[...])
            t = gelu(t[:, 256:512] + shifted(t[:, :256], 1, 0, 64) + shifted(t[:, 512:], -1, 0, 64))
            for n, x in enumerate(xs):
                v = t[64 * n : 64 * n + 64]
                halves = [v[:, :128], v[:, 128:]]
                for h in range(2):
                    ok = True if h != g else (gy > 0) if g == 0 else (gy < ny - 1)
                    if x < 2:
                        ok = ok & (gx > 0)
                    if x > 5:
                        ok = ok & (gx < nx - 1)
                    if ok is not True:
                        halves[h] = jnp.where(ok, halves[h], jnp.zeros_like(halves[h]))
                e2[g][x] = [v.astype(BF) for v in halves]

    enc2((3, 4))
    arrive(x2[:2])
    arrive(x2[4:])
    arrive(x2b[:2])
    arrive(x2b[6:])
    for n, y in enumerate((2, 0)):
        send(n, mate, 0, p1.at[y, pl.ds(4, 2)], p1.at[y, pl.ds(8 - 8 * odd, 2)], sp, rp).wait_recv()
        send(2 + n, mate, 0, p1.at[y, 3 + 3 * odd], p1.at[y, 7 - 5 * odd], sp, rp).wait_recv()

    @pl.when(gx == 0)
    def _():
        p1[:, pl.ds(0, 3)] = jnp.zeros((3, 3, 64, 128), BF)

    @pl.when(gx == nx - 1)
    def _():
        p1[:, pl.ds(7, 3)] = jnp.zeros((3, 3, 64, 128), BF)

    @pl.when(gy == 0)
    def _():
        for x in (0, 7):
            p1[0, pl.ds(x, 3)] = jnp.zeros((3, 64, 128), BF)

    @pl.when(gy == ny - 1)
    def _():
        for x in (0, 7):
            p1[2, pl.ds(x, 3)] = jnp.zeros((3, 64, 128), BF)

    enc2((0, 1, 2))
    enc2((5, 6, 7))
    pairs = []
    for g in range(2):
        for x in range(4):
            a0, a1 = [e2[g][2 * x][h].astype(F32) + e2[g][2 * x + 1][h].astype(F32) for h in range(2)]
            a = jnp.where(low, a0 + pltpu.roll(a0, 64, 1), a1 + pltpu.roll(a1, 64, 1))
            pairs.append(((a + pltpu.roll(a, 63, 0)) * 0.125).astype(BF))
    pick32 = ones_where(iota((32, 64), 1) == 2 * iota((32, 64), 0))
    t = nn(pick32, cat(pairs, 1)).astype(BF)
    p2 = [cat([t[:, 128 * x : 128 * x + 128], t[:, 512 + 128 * x : 512 + 128 * x + 128]], 1) for x in range(4)]

    lhs = cat([cat([p2[x + i] for i in range(3)], 1) for x in range(2)], 0)
    t = nn(lhs, k3[...])
    e3 = gelu(t[:, 256:512] + shifted(t[:, :256], 1, 0, 32) + shifted(t[:, 512:], -1, 0, 32)).astype(BF)
    f = e3.astype(F32)
    a = f[:32] + f[32:]
    a = a[:, :128] + a[:, 128:]
    a = (a + pltpu.roll(a, 31, 0)) * 0.125
    pick16 = ones_where(iota((16, 32), 1) == 2 * iota((16, 32), 0))
    p3[2, gy + 2] = nn(pick16, a.astype(BF)).astype(BF)
    x4 = []
    for n, (dx, dy) in enumerate(window):
        x4.append(send(n, dx, dy, p3.at[2, gy + 2], p3.at[2 - dx, gy + 2], s4, r4))
    start(x4)
    for x in range(2):
        for y in range(2):
            e3e[x + 1, y + 1] = e3[32 * x : 32 * x + 32, 128 * y : 128 * y + 128]
    def cells(ref, n_local, ss, rs):
        copies = []
        for n, (dx, dy) in enumerate(DIRS):
            sx, tx, cx = side(dx, n_local)
            sy, ty, cy = side(dy, n_local)
            copies.append(
                send(n, dx, dy, ref.at[pl.ds(sx, cx), pl.ds(sy, cy)], ref.at[pl.ds(tx, cx), pl.ds(ty, cy)], ss, rs)
            )
        return copies

    xe3 = cells(e3e, 2, se3, re3)
    start(xe3)

    low32 = iota((32, 128), 1) < 64
    rr, cc = iota((64, 64), 0), iota((64, 64), 1)
    split = ones_where(cc == 2 * (rr % 32) + rr // 32)
    for x in range(6):
        t = nn(split, cat([e2[g][x + 1][h] for g in range(2) for h in range(2)], 1))
        for y in range(6):
            n = 128 * ((y + 1) // 2)
            ev, od = t[:32, n : n + 128], t[32:, n : n + 128]
            if y % 2 == 1:
                cell = jnp.where(low32, ev, pltpu.roll(od, 64, 1))
            else:
                cell = jnp.where(low32, pltpu.roll(ev, 64, 1), od)
            e2e[x, y] = cell.astype(BF)

    for c in got_w4:
        c.wait()
    for n, (dx, dy) in enumerate(window):
        pltpu.make_async_remote_copy(
            src_ref=p3.at[2, gy + 2], dst_ref=p3.at[2 - dx, lax.rem(gy - dy + ny, ny) + 2],
            send_sem=s4.at[n], recv_sem=r4.at[n], device_id=target(dx, dy), device_id_type=MESH,
        ).wait_recv()

    cell = []
    for x in range(5):
        inside = (gx + (x - 2) >= 0) & (gx + (x - 2) < nx)
        line = []
        for y in range(5):
            v = p3[x, gy + y]
            line.append(jnp.where(inside, v, jnp.zeros_like(v)))
        cell.append(line)
    lhs = cat(
        [
            cat([cell[x + i][y + j] for i in range(3) for j in range(3)], 1)
            for x in range(3)
            for y in range(3)
        ],
        0,
    )
    t = nt(lhs, k4[...])
    e4 = gelu(t[:, 256:512] + shifted(t[:, :256], 1, 0, 16) + shifted(t[:, 512:], -1, 0, 16))

    def inside(x, y, width, n_local):
        ok = True
        if x == 0:
            ok = gx > 0
        if x == n_local + 1:
            ok = gx < nx - 1
        if y == 0:
            ok = ok & (gy > 0)
        if y == n_local + 1:
            ok = ok & (gy < ny - 1)
        return ok

    def kept(v, ok):
        return v if ok is True else jnp.where(ok, v, jnp.zeros_like(v))


    e4 = [kept(e4[16 * n : 16 * n + 16], inside(n // 3, n % 3, 16, 1)).astype(BF) for n in range(9)]
    twice = ones_where(iota((32, 16), 1) == iota((32, 16), 0) // 2)
    up = nn(twice, cat(e4, 1)).astype(BF)
    at = ((0, 0, 1), (0, 1, 1), (1, 1, 2), (1, 2, 2))
    for k in range(2):
        for y in range(4):
            for tx in range(2):
                for j in range(3):
                    n = 3 * (k + tx) + at[y][j]
                    pd3[pl.ds(128 * k + 32 * y, 32), pl.ds(256 * (3 * tx + j), 256)] = up[:, 256 * n : 256 * n + 256]
    t = nt(pd3[...], g3[...])
    arrive(xe3)
    for px in range(2):
        u = t[:, 384 * px : 384 * px + 384]
        v = gelu(u[:, 128:256] + shifted(u[:, :128], 1, 0, 32) + shifted(u[:, 256:], -1, 0, 32))
        for k in range(2):
            for y in range(4):
                x, n = 2 * k + 1 - px, 128 * k + 32 * y
                w = v[n : n + 32] + e3e[x, y].astype(F32)
                d3e[x, y] = kept(w, inside(x, y, 32, 2)).astype(BF)

    lane = iota((288, 128), 1) < 64
    lhs = cat(
        [
            cat([d3e[k, m], d3e[k, m + 1], d3e[k + 1, m], d3e[k + 1, m + 1]], 1)
            for k in range(3)
            for m in range(3)
        ],
        0,
    )
    t = nt(lhs, g2[...])
    for px in range(2):
        for py in range(2):
            n = 256 * (2 * px + py)
            a, b = t[:, n : n + 128], t[:, n + 128 : n + 256]
            v = gelu(b + jnp.where(lane, shifted(a, 1, 0, 32), shifted(a, -1, 0, 32)))
            for k in range(3):
                for m in range(3):
                    x, y = 2 * k + 1 - px, 2 * m + 1 - py
                    w = v[96 * k + 32 * m : 96 * k + 32 * m + 32] + e2e[x, y].astype(F32)
                    d2e[x, y] = kept(w, inside(x, y, 32, 4))

    rr, cc = iota((128, 64), 0), iota((128, 64), 1)
    spread = ones_where((rr // 4 == cc % 32) & (rr // 2 % 2 == cc // 32))
    for x in range(6):
        line = []
        as_is = [d2e[x, m] for m in range(6)]
        turned = [pltpu.roll(v, 64, 1) for v in as_is]
        for m in range(5):
            top = jnp.where(low32, as_is[m], turned[m + 1])
            bottom = jnp.where(low32, turned[m], as_is[m + 1])
            line.append(cat([top, bottom], 0).astype(BF))
        a = nn(spread, cat(line, 1)).astype(BF)
        for m in range(5):
            q[x, m] = a[:, 128 * m : 128 * m + 128]

    both = ((0, 0), (0, 1), (1, 0), (1, 1))
    groups = []
    for parities, windows in (
        ([c for c in both if c[0] == 0], [(0, m) for m in range(5)]),
        ([c for c in both if c[1] == 0], [(k, 0) for k in range(1, 4)]),
        (both, [(k, m) for k in range(1, 4) for m in range(1, 4)]),
        ([c for c in both if c[1] == 1], [(k, 4) for k in range(1, 4)]),
        ([c for c in both if c[0] == 1], [(4, m) for m in range(5)]),
    ):
        for n in range(0, len(windows), 2):
            groups.append((parities, windows[n : n + 2]))
    for parities, windows in groups:
        lhs = cat([g1[pl.ds(96 * (2 * px + py), 96), :] for px, py in parities], 0)
        t = nt(lhs, cat([cat([q[k, m], q[k + 1, m]], 1) for k, m in windows], 0))
        for n, (px, py) in enumerate(parities):
            for h, (k, m) in enumerate(windows):
                a, b = k - px, m - py
                if not (0 <= a < 4 and 0 <= b < 4):
                    continue
                x, y = 2 * a + px, 2 * b + py
                u = t[96 * n : 96 * n + 96, 128 * h : 128 * h + 128]
                v = gelu(u[32:64] + shifted(u[:32], 1, 1, 128) + shifted(u[64:], -1, 1, 128))
                v = v + e1[x, pl.ds(32 * y, 32), :].astype(F32)
                out[x, y] = v.astype(BF)

    for copies in (x1, x2, x2b, passed, x4, xe3):
        for c in copies:
            c.wait_send()


def local(features, w_enc1, w_enc2, w_enc3, w_enc4, w_dec3, w_dec2, w_dec1):
    w_enc2, w_enc3 = jnp.swapaxes(w_enc2, 1, 2), jnp.swapaxes(w_enc3, 1, 2)
    w_enc4, w_dec3 = w_enc4.reshape(9, 768, 128), w_dec3.reshape(9, 384, 256)
    args = (features, w_enc1, w_enc2, w_enc3, w_enc4, w_dec3, w_dec2, w_dec1)
    ny = lax.axis_size("gy")
    far = 5 * ny - 1
    dma = pltpu.SemaphoreType.DMA
    scratch = [pltpu.VMEM(a.shape, BF) for a in (features, w_enc1, w_enc2, w_enc3, w_dec2, w_dec1)]
    for shape in (
        (10, 320, 128), (8, 256, 128),
        (3, 10, 64, 128),
        (5, ny + 4, 16, 128), (6, 6, 32, 128), (4, 4, 32, 128),
        (192, 384), (768, 768), (768, 768), (768, 1152), (384, 2304), (1024, 512), (384, 256),
        (256, 1536), (768, 1536), (4, 4, 32, 128),
    ):
        scratch.append(pltpu.VMEM(shape, BF))
    scratch.append(pltpu.VMEM((6, 6, 32, 128), F32))
    scratch.append(pltpu.VMEM((6, 5, 128, 128), BF))
    scratch.append(dma((24,)))
    for n in (8, 14, 4, far, 8):
        scratch += [dma((n,)), dma((n,))]
    decoded = pl.pallas_call(
        kernel,
        out_shape=pltpu.VMEM((8, 8, 32, 128), BF),
        in_specs=[pl.BlockSpec(memory_space=pl.ANY)] * 8,
        out_specs=pl.BlockSpec(memory_space=pltpu.VMEM),
        scratch_shapes=scratch,
        compiler_params=pltpu.CompilerParams(
            collective_id=0, has_side_effects=True, vmem_limit_bytes=48 * 1024 * 1024
        ),
        cost_estimate=pl.CostEstimate(flops=2 * 1115000000, bytes_accessed=7000000, transcendentals=1000000),
    )(*[pltpu.with_memory_space_constraint(a, pltpu.HBM) for a in args])
    return jnp.transpose(decoded, (2, 0, 1, 3))


def solution(mesh):
    return jax.shard_map(
        local,
        mesh=mesh,
        in_specs=(P(None, "gx", "gy", None), P(), P(), P(), P(), P(), P(), P()),
        out_specs=P(None, "gx", "gy", None),
        check_vma=False,
    )
```
